32 devices in a mesh: fsdp: 4 (over y, x), expert: 8 (over z, core).
Axes of the slice: x: 2, y: 2, z: 4, core: 2. Of those that a mesh axis runs over, the one named last changes fastest.
Arguments:
- tokens: bfloat16 [4096, 2048], P(('fsdp', 'expert')), may hold values from -6 to 6
- cotangent: bfloat16 [4096, 2048], P(('fsdp', 'expert')), may hold values from -6 to 6
- lengths: int32 [32, 4], P(('fsdp', 'expert')), may hold values from 1 to 64, 128 in all within a row
- routes: int32 [2, 4096, 8], P(None, ('fsdp', 'expert')), may hold values from 0 to 31, all different within a row; in each aligned block of 128 rows (0 to 127, 128 to 255, ..., all dimensions but the last counted through in order) at most 48 rows name the same one
- gains: bfloat16 [2, 4352], P(None, ('fsdp', 'expert')), may hold values from 0.5 to 1.5
- w_query: bfloat16 [2, 2048, 4096], P(None, ('fsdp', 'expert')), may hold values from -0.125 to 0.125
- key_weight: bfloat16 [2, 2048, 512], P(None, ('fsdp', 'expert')), may hold values from -0.125 to 0.125
- value_weight: bfloat16 [2, 2048, 512], P(None, ('fsdp', 'expert')), may hold values from -0.125 to 0.125
- w_out: bfloat16 [2, 4096, 2048], P(None, ('fsdp', 'expert')), may hold values from -0.25 to 0.25
- w_router: bfloat16 [2, 2048, 32], P(None, ('fsdp', 'expert')), may hold values from -0.0625 to 0.0625
- w_gate: bfloat16 [2, 32, 2048, 768], P(None, 'expert', 'fsdp'), may hold values from -0.125 to 0.125
- w_up: bfloat16 [2, 32, 2048, 768], P(None, 'expert', 'fsdp'), may hold values from -0.125 to 0.125
- w_down: bfloat16 [2, 32, 768, 2048], P(None, 'expert', None, 'fsdp'), may hold values from -0.4375 to 0.4375
Outputs:
- output: bfloat16 [4096, 2048], P(('fsdp', 'expert'))
- d_tokens: bfloat16 [4096, 2048], P(('fsdp', 'expert'))
- d_gains: float32 [2, 4352], P(None, ('fsdp', 'expert'))
- d_query: float32 [2, 2048, 4096], P(None, ('fsdp', 'expert'))
- d_key: float32 [2, 2048, 512], P(None, ('fsdp', 'expert'))
- d_value: float32 [2, 2048, 512], P(None, ('fsdp', 'expert'))
- d_out: float32 [2, 4096, 2048], P(None, ('fsdp', 'expert'))
- d_router: float32 [2, 2048, 32], P(None, ('fsdp', 'expert'))
- d_gate: float32 [2, 32, 2048, 768], P(None, 'expert', 'fsdp')
- d_up: float32 [2, 32, 2048, 768], P(None, 'expert', 'fsdp')
- d_down: float32 [2, 32, 768, 2048], P(None, 'expert', None, 'fsdp')
The draws below stay inside these ranges and needn't reach their ends.
Inputs may be any that keep to these rules, and one draw needn't show every extreme that they name: `routes`: each row names 8 different experts. In each layer the 128 rows of one device name any one expert at most 48 times. The 4 lengths of one device sum to 128.
All inputs are finite; a program needn't handle non-finite values.
Results may differ from the reference program's by a relative error of at most 0.022.
Values may be sent and summed in bfloat16 or wider, within the bound.
A program may use at most 512 MiB of HBM per device.

```python
import math
import jax
import jax.numpy as jnp
import numpy as np
from jax import lax

MODEL_WIDTH = 2048
QUERY_HEADS = 32
KEY_VALUE_HEADS = 4
HEAD_SIZE = 128
FF = 768
TOP = 8
EXPERTS = 32
DECODER_LAYERS = 2
SEQS = 4
DEVICE_TOKENS = 128
CAP = 48
TOKENS = 4096
GAINS = 4352


def block_levels(key, shape, shards, low, largest):
    def one(dim, blocks):
        draws = jax.random.uniform(jax.random.fold_in(jax.random.fold_in(key, 6), dim), (blocks,), jnp.float32, low / len(shards), largest / len(shards))
        return jnp.repeat(jnp.exp(draws), shape[dim] // blocks).reshape((-1,) + (1,) * (len(shape) - dim - 1))

    factor_of = one(*shards[0])
    for cut in shards[1:]:
        factor_of = factor_of * one(*cut)
    return factor_of


def split_up(amount, total, most, lean):
    portions = [(1 << 20) // math.isqrt(rank ** lean) + 1 for rank in range(2, amount + 1)]
    surplus, counts = total - most - (amount - 1), [1] * (amount - 1)
    while surplus > 0:
        free = [i for i in range(amount - 1) if counts[i] < most]
        mass, left = sum([portions[i] for i in free]), surplus
        for i in free:
            addition = min(most - counts[i], max(1, left * portions[i] // mass), surplus)
            counts[i] = counts[i] + addition
            surplus = surplus - addition
    return np.array([most] + counts)


def ragged(own_key, amount, total, reach, slope):
    if amount == 2:
        one = jax.random.randint(own_key, (), max(1, total - reach), min(reach, total - 1) + 1)
        return jnp.stack([one, total - one])
    sizes = jnp.asarray(split_up(amount, total, reach, slope), jnp.int32)
    couples = (amount - 1) // 2
    donor, receiver = sizes[1:1 + 2 * couples:2], sizes[2:2 + 2 * couples:2]
    slack = jnp.minimum(donor - 1, reach - receiver)
    passed = jax.random.randint(jax.random.fold_in(own_key, 1), (couples,), 0, 1 << 20) % (slack + 1)
    sizes = sizes.at[1:1 + 2 * couples:2].set(donor - passed).at[2:2 + 2 * couples:2].set(receiver + passed)
    return sizes[jax.random.permutation(jax.random.fold_in(own_key, 2), amount)]


def routed_block(rng, own, number, rows, amount, top, most, lean):
    ranking = jax.random.permutation(rng, amount)
    crowded, ordinary = load_shares(amount, rows * top, most, lean, True), load_shares(amount, rows * top, most, lean, False)
    places = jnp.arange(amount)

    def named(tallies, rotation):
        used = int((tallies > 0).sum())
        fixed = max(1, used // 4)
        passed = fixed + (places - fixed + rotation * (used - fixed)) % max(1, amount - fixed)
        return jnp.zeros((amount,), jnp.int32).at[ranking[jnp.where(places < fixed, places, passed)]].set(jnp.asarray(tallies, jnp.int32))

    tallies = jnp.where(number % 4 == 0, named(crowded, number // 4), named(ordinary, number - number // 4 - 1))
    mixed = jax.random.permutation(jax.random.fold_in(own, 3), amount)
    source_of, taker = mixed[0:amount // 2 * 2:2], mixed[1:amount // 2 * 2:2]
    room = jnp.minimum(tallies[source_of] - 1, most - tallies[taker]) // 2
    room = jnp.where((source_of == ranking[0]) | (taker == ranking[0]) | (tallies[taker] == 0), 0, jnp.maximum(room, 0))
    passed = jax.random.randint(jax.random.fold_in(own, 4), (amount // 2,), 0, 1 << 20) % (room + 1)
    tallies = tallies.at[source_of].add(-passed).at[taker].add(passed)
    labels = jnp.searchsorted(jnp.cumsum(tallies), jnp.arange(rows * top), side="right").astype(jnp.int32)
    grid = labels.reshape(top, rows).T
    grid = grid[jax.random.permutation(jax.random.fold_in(own, 1), rows)]
    rotation = jax.random.randint(jax.random.fold_in(own, 2), (rows, 1), 0, top)
    return jnp.take_along_axis(grid, (jnp.arange(top)[None, :] + rotation) % top, axis=1)


def load_shares(number_of, total, bound, slope, full):
    loads = [(1 << 20) // math.isqrt(grade ** slope) + 1 for grade in range(1, number_of + 1)]
    largest = bound if full else min(bound, max(-(-total // number_of), total * loads[0] // sum(loads)))
    least = 1 if total - largest >= number_of - 1 else 0
    counts, surplus = [largest] + [least] * (number_of - 1), total - largest - least * (number_of - 1)
    while surplus > 0:
        candidates = [i for i in range(1, number_of) if counts[i] < largest] or [i for i in range(1, number_of) if counts[i] < bound]
        pool, remaining = sum([loads[i] for i in candidates]), surplus
        for i in candidates:
            extra = min(bound - counts[i], max(1, remaining * loads[i] // pool), surplus)
            counts[i] = counts[i] + extra
            surplus = surplus - extra
    return np.array(counts)


def gaussian(own_key, extent, scale, reach, shards=(), held_as=jnp.bfloat16):
    gain = block_levels(own_key, extent, shards, -0.22, 0.18) if shards else 1.0
    values = jax.random.normal(own_key, extent, jnp.float32) * scale * gain
    return jnp.minimum(jnp.maximum(values, -reach), reach).astype(held_as)


def setup_inputs(seed: int = 0) -> dict:
    key_of = jax.random.split(jax.random.key(seed), 14)
    tokens = gaussian(key_of[0], (TOKENS, MODEL_WIDTH), 1.0, 6.0, ((0, 32),))
    cotangent = gaussian(key_of[1], (TOKENS, MODEL_WIDTH), 1.0, 6.0, ((0, 32),))
    lengths = jax.vmap(lambda own: ragged(own, SEQS, DEVICE_TOKENS, DEVICE_TOKENS // 2, 2))(jax.random.split(key_of[2], (TOKENS // DEVICE_TOKENS))).reshape((TOKENS // DEVICE_TOKENS, SEQS)).astype(jnp.int32)
    routes_keys = jax.random.split(jax.random.fold_in(key_of[3], 1), DECODER_LAYERS * TOKENS // DEVICE_TOKENS)
    routes_turns = jax.random.permutation(jax.random.fold_in(key_of[3], 3), DECODER_LAYERS * TOKENS // DEVICE_TOKENS)
    routes = jax.vmap(lambda own, number: routed_block(jax.random.fold_in(key_of[3], 2), own, number, DEVICE_TOKENS, EXPERTS, TOP, CAP, 2))(routes_keys, routes_turns).reshape((DECODER_LAYERS, TOKENS, TOP))
    gains = jnp.clip(1.0 + 0.1 * jax.random.normal(key_of[4], (DECODER_LAYERS, GAINS), jnp.float32), 0.5, 1.5).astype(jnp.bfloat16)
    w_query = gaussian(key_of[5], (DECODER_LAYERS, MODEL_WIDTH, QUERY_HEADS * HEAD_SIZE), MODEL_WIDTH ** -0.5, 0.125, ((1, 32),))
    key_weight = gaussian(key_of[6], (DECODER_LAYERS, MODEL_WIDTH, KEY_VALUE_HEADS * HEAD_SIZE), MODEL_WIDTH ** -0.5, 0.125, ((1, 32),))
    value_weight = gaussian(key_of[7], (DECODER_LAYERS, MODEL_WIDTH, KEY_VALUE_HEADS * HEAD_SIZE), MODEL_WIDTH ** -0.5, 0.125, ((1, 32),))
    w_out = gaussian(key_of[8], (DECODER_LAYERS, QUERY_HEADS * HEAD_SIZE, MODEL_WIDTH), (QUERY_HEADS * HEAD_SIZE // 8) ** -0.5, 0.25, ((1, 32),))
    w_router = gaussian(key_of[9], (DECODER_LAYERS, MODEL_WIDTH, EXPERTS), (4 * MODEL_WIDTH) ** -0.5, 0.0625, ((1, 32),))
    w_gate = gaussian(key_of[10], (DECODER_LAYERS, EXPERTS, MODEL_WIDTH, FF), MODEL_WIDTH ** -0.5, 0.125, ((1, 8), (2, 4)))
    w_up = gaussian(key_of[11], (DECODER_LAYERS, EXPERTS, MODEL_WIDTH, FF), MODEL_WIDTH ** -0.5, 0.125, ((1, 8), (2, 4)))
    w_down = gaussian(key_of[12], (DECODER_LAYERS, EXPERTS, FF, MODEL_WIDTH), (FF // 4) ** -0.5, 0.4375, ((1, 8), (3, 4)))
    return {"tokens": tokens, "cotangent": cotangent, "lengths": lengths, "routes": routes, "gains": gains, "w_query": w_query, "key_weight": key_weight, "value_weight": value_weight, "w_out": w_out, "w_router": w_router, "w_gate": w_gate, "w_up": w_up, "w_down": w_down}


@jax.custom_vjp
def reduced_precision(v):
    return lax.optimization_barrier(v.astype(jnp.bfloat16)).astype(jnp.float32)

@jax.custom_vjp
def reduced_precision_backward(v):
    return v

def low_keep(v):
    return (reduced_precision(v), None)

def low_pass(kept, grad):
    return (grad,)

def back_keep(v):
    return (v, None)

def back_low(kept, grad):
    return (reduced_precision(grad),)
reduced_precision.defvjp(low_keep, low_pass)
reduced_precision_backward.defvjp(back_keep, back_low)
EPSILON = 1e-06
ROPE_BASE = 1000000.0
PRECISE = lax.Precision.HIGHEST

def matrix_product(left, right):
    return jnp.dot(left, right, precision=PRECISE, preferred_element_type=jnp.float32)

def norm_rows(operand, gain_vec):
    return operand * lax.rsqrt(lax.optimization_barrier(jnp.mean(operand * operand, axis=-1, keepdims=True)) + EPSILON) * gain_vec

def softmax_last(operand):
    shifted = operand - lax.optimization_barrier(jnp.max(operand, axis=-1, keepdims=True))
    weights = jnp.exp(shifted)
    return weights / lax.optimization_barrier(jnp.sum(weights, axis=-1, keepdims=True))

def rotate(operand, cosine, sine):
    half_size = operand.shape[-1] // 2
    front_half = operand[..., :half_size]
    back_half = operand[..., half_size:]
    return jnp.concatenate([front_half * cosine - back_half * sine, back_half * cosine + front_half * sine], axis=-1)

def geometry(lengths):
    seq_ends = jnp.cumsum(lengths, axis=1)
    seq_starts = seq_ends - lengths
    offsets = jnp.arange(DEVICE_TOKENS, dtype=jnp.int32)
    segment = lax.optimization_barrier(jnp.sum((offsets[None, :, None] >= seq_ends[:, None, :]).astype(jnp.int32), axis=2))
    begins = jnp.take_along_axis(seq_starts, segment, axis=1)
    position = (offsets[None, :] - begins).astype(jnp.float32)
    inverse = jnp.exp(-(2.0 * jnp.arange(HEAD_SIZE // 2, dtype=jnp.float32) / HEAD_SIZE) * math.log(ROPE_BASE))
    angles = position[:, :, None] * inverse[None, None, :]
    allowed = (segment[:, :, None] == segment[:, None, :]) & (offsets[None, None, :] <= offsets[None, :, None])
    return (jnp.cos(angles)[:, :, None, :], jnp.sin(angles)[:, :, None, :], allowed)

def slot_table(route_rows):
    layer_blocks = TOKENS // DEVICE_TOKENS
    flat_routes = route_rows.reshape(layer_blocks, DEVICE_TOKENS * TOP)
    matches = (flat_routes[:, :, None] == jnp.arange(EXPERTS, dtype=jnp.int32)[None, None, :]).astype(jnp.int32)
    rank_in = lax.optimization_barrier(jnp.sum((jnp.cumsum(matches, axis=1) - 1) * matches, axis=2))
    block_ids = jnp.arange(layer_blocks, dtype=jnp.int32)[:, None]
    return ((block_ids * EXPERTS + flat_routes) * CAP + rank_in).reshape(TOKENS * TOP)

def attend(query_rows, rows_of_key, rows_of_value, allowed):
    query_group_size = QUERY_HEADS // KEY_VALUE_HEADS
    grouped_rows = query_rows.reshape(DEVICE_TOKENS, KEY_VALUE_HEADS, query_group_size, HEAD_SIZE)
    raw_scores = jnp.einsum('tgjd,sgd->gjts', grouped_rows, rows_of_key, precision=PRECISE) * (1.0 / math.sqrt(HEAD_SIZE))
    scores = reduced_precision_backward(jnp.where(allowed[None, None], raw_scores, -1e+30))
    probability = reduced_precision(softmax_last(scores))
    mixed = jnp.einsum('gjts,sgd->tgjd', probability, rows_of_value, precision=PRECISE)
    return mixed.reshape(DEVICE_TOKENS, QUERY_HEADS * HEAD_SIZE)

def expert_block(pieces):
    expert_rows, gate_matrix, up_matrix, down_matrix = pieces
    gate_pre = reduced_precision_backward(matrix_product(expert_rows, gate_matrix))
    up_pre = reduced_precision_backward(matrix_product(expert_rows, up_matrix))
    hidden = reduced_precision(jax.nn.silu(gate_pre) * up_pre)
    return reduced_precision(reduced_precision_backward(matrix_product(hidden, down_matrix)))

def layer(state, weights, route_rows, slot_ids, cosine, sine, allowed):
    w_query, key_weight, value_weight, w_out, w_router, gain_vec, w_gate, w_up, w_down = weights
    layer_blocks = TOKENS // DEVICE_TOKENS
    g_attn = gain_vec[:MODEL_WIDTH]
    g_ffn = gain_vec[MODEL_WIDTH:2 * MODEL_WIDTH]
    g_query = gain_vec[2 * MODEL_WIDTH:2 * MODEL_WIDTH + HEAD_SIZE]
    g_key = gain_vec[2 * MODEL_WIDTH + HEAD_SIZE:]
    normalized_input = reduced_precision(norm_rows(state, g_attn))
    query_rows = reduced_precision_backward(matrix_product(normalized_input, w_query)).reshape(layer_blocks, DEVICE_TOKENS, QUERY_HEADS, HEAD_SIZE)
    rows_of_key = reduced_precision_backward(matrix_product(normalized_input, key_weight)).reshape(layer_blocks, DEVICE_TOKENS, KEY_VALUE_HEADS, HEAD_SIZE)
    rows_of_value = reduced_precision(reduced_precision_backward(matrix_product(normalized_input, value_weight))).reshape(layer_blocks, DEVICE_TOKENS, KEY_VALUE_HEADS, HEAD_SIZE)
    query_rows = reduced_precision(rotate(norm_rows(query_rows, g_query), cosine, sine))
    rows_of_key = reduced_precision(rotate(norm_rows(rows_of_key, g_key), cosine, sine))
    attended = jax.vmap(attend)(query_rows, rows_of_key, rows_of_value, allowed)
    attended = reduced_precision(reduced_precision_backward(attended)).reshape(TOKENS, QUERY_HEADS * HEAD_SIZE)
    middle = state + reduced_precision_backward(matrix_product(attended, w_out))
    mixer_in = reduced_precision(norm_rows(middle, g_ffn))
    logits = reduced_precision_backward(matrix_product(mixer_in, w_router))
    gates = softmax_last(jnp.take_along_axis(logits, route_rows, axis=1))
    buffer = jnp.zeros((layer_blocks * EXPERTS * CAP, MODEL_WIDTH), jnp.float32).at[slot_ids].set(jnp.repeat(mixer_in, TOP, axis=0))
    buffer = reduced_precision_backward(buffer)
    grouped_rows = buffer.reshape(layer_blocks, EXPERTS, CAP, MODEL_WIDTH).transpose(1, 0, 2, 3).reshape(EXPERTS, layer_blocks * CAP, MODEL_WIDTH)
    results = lax.map(expert_block, (grouped_rows, w_gate, w_up, w_down))
    results = results.reshape(EXPERTS, layer_blocks, CAP, MODEL_WIDTH).transpose(1, 0, 2, 3).reshape(layer_blocks * EXPERTS * CAP, MODEL_WIDTH)
    picked = results[slot_ids].reshape(TOKENS, TOP, MODEL_WIDTH)
    return middle + lax.optimization_barrier(jnp.sum(gates[:, :, None] * picked, axis=1))

def reference(tokens, cotangent, lengths, routes, gains, w_query, key_weight, value_weight, w_out, w_router, w_gate, w_up, w_down):
    cosine, sine, allowed = geometry(lengths)
    slot_list = [slot_table(routes[number]) for number in range(DECODER_LAYERS)]

    def forward(state, gain_all, query_all, key_all, value_all, out_all, router_all, gate_all, up_all, down_all):
        for number in range(DECODER_LAYERS):
            weights = (query_all[number], key_all[number], value_all[number], out_all[number], router_all[number], gain_all[number], gate_all[number], up_all[number], down_all[number])
            state = layer(state, weights, routes[number], slot_list[number], cosine, sine, allowed)
        return state
    inputs = [operand.astype(jnp.float32) for operand in (tokens, gains, w_query, key_weight, value_weight, w_out, w_router, w_gate, w_up, w_down)]
    result, pullback = jax.vjp(forward, *inputs)
    grads = pullback(cotangent.astype(jnp.float32))
    return (result.astype(jnp.bfloat16), grads[0].astype(jnp.bfloat16), grads[1], grads[2], grads[3], grads[4], grads[5], grads[6], grads[7], grads[8], grads[9])
```

```python
from functools import partial
import math

import jax
import jax.numpy as jnp
from jax import lax
from jax.experimental import pallas as pl
from jax.experimental.pallas import tpu as pltpu
from jax.sharding import Mesh
from jax.sharding import PartitionSpec as P

MODEL_WIDTH = 2048
QUERY_HEADS = 32
KEY_VALUE_HEADS = 4
HEAD_SIZE = 128
TOP = 8
EXPERTS = 32
DECODER_LAYERS = 2
CAP = 48


EPSILON = 1e-06
ROPE_BASE = 1000000.0


def norm_rows(operand, gain_vec):
    return (
        operand
        * lax.rsqrt(jnp.mean(operand * operand, axis=-1, keepdims=True) + EPSILON)
        * gain_vec
    )


def softmax_last(operand):
    shifted = operand - jnp.max(operand, axis=-1, keepdims=True)
    weights = jnp.exp(shifted)
    return weights / jnp.sum(weights, axis=-1, keepdims=True)


def rotate(operand, cosine, sine):
    half_size = operand.shape[-1] // 2
    front_half = operand[..., :half_size]
    back_half = operand[..., half_size:]
    return jnp.concatenate(
        [front_half * cosine - back_half * sine, back_half * cosine + front_half * sine], axis=-1
    )


def head_piece(query_pre, prerotation_key, g_query, g_key, cosine, sine):
    return (
        rotate(norm_rows(query_pre, g_query), cosine, sine),
        rotate(norm_rows(prerotation_key, g_key), cosine, sine),
    )


def geometry(lengths, local_rows):
    seq_ends = jnp.cumsum(lengths[0])
    seq_starts = seq_ends - lengths[0]
    offsets = jnp.arange(local_rows, dtype=jnp.int32)
    segment = jnp.sum((offsets[:, None] >= seq_ends[None, :]).astype(jnp.int32), axis=1)
    member = segment[:, None] == jnp.arange(seq_ends.shape[0], dtype=jnp.int32)[None, :]
    begins = jnp.sum(jnp.where(member, seq_starts[None, :], 0), axis=1)
    position = (offsets - begins).astype(jnp.float32)
    inverse = jnp.exp(
        -(2.0 * jnp.arange(HEAD_SIZE // 2, dtype=jnp.float32) / HEAD_SIZE) * math.log(ROPE_BASE)
    )
    angles = position[:, None] * inverse[None, :]
    allowed = (segment[:, None] == segment[None, :]) & (offsets[None, :] <= offsets[:, None])
    return (jnp.cos(angles)[:, None, :], jnp.sin(angles)[:, None, :], allowed)


def slot_table(route_rows):
    flat_routes = route_rows.reshape(-1)
    matches = (flat_routes[:, None] == jnp.arange(EXPERTS, dtype=jnp.int32)[None, :]).astype(
        jnp.int32
    )
    rank_in = jnp.sum((jnp.cumsum(matches, axis=0) - 1) * matches, axis=1)
    return flat_routes * CAP + rank_in


def split_gains(gain_vec):
    return (
        gain_vec[:MODEL_WIDTH],
        gain_vec[MODEL_WIDTH : 2 * MODEL_WIDTH],
        gain_vec[2 * MODEL_WIDTH : 2 * MODEL_WIDTH + HEAD_SIZE],
        gain_vec[2 * MODEL_WIDTH + HEAD_SIZE :],
    )


def score_block(query_copy, key_b, allowed):
    local_rows = query_copy.shape[0]
    grouped_rows = query_copy.reshape(
        local_rows, KEY_VALUE_HEADS, QUERY_HEADS // KEY_VALUE_HEADS, HEAD_SIZE
    )
    raw_scores = jnp.einsum(
        "tgjd,sgd->gjts", grouped_rows, key_b, preferred_element_type=jnp.float32
    ) * (1.0 / math.sqrt(HEAD_SIZE))
    return jnp.where(allowed[None, None], raw_scores, -1e30)


def layer_forward(state, dense, experts, route_rows, cosine, sine, allowed, peers):
    w_query, key_weight, value_weight, w_out, w_router, gain_raw = dense
    w_gate, w_up, w_down = experts
    local_rows = state.shape[0]
    experts_here = w_gate.shape[0]
    g_attn, g_ffn, g_query, g_key = split_gains(gain_raw.astype(jnp.float32))
    normalized_input = norm_rows(state, g_attn).astype(jnp.bfloat16)
    query_pre = jnp.dot(normalized_input, w_query, preferred_element_type=jnp.float32).reshape(
        local_rows, QUERY_HEADS, HEAD_SIZE
    )
    prerotation_key = jnp.dot(
        normalized_input, key_weight, preferred_element_type=jnp.float32
    ).reshape(local_rows, KEY_VALUE_HEADS, HEAD_SIZE)
    value_b = (
        jnp.dot(normalized_input, value_weight, preferred_element_type=jnp.float32)
        .astype(jnp.bfloat16)
        .reshape(local_rows, KEY_VALUE_HEADS, HEAD_SIZE)
    )
    query_f, key_f = head_piece(query_pre, prerotation_key, g_query, g_key, cosine, sine)
    query_copy = query_f.astype(jnp.bfloat16)
    key_b = key_f.astype(jnp.bfloat16)
    scores = score_block(query_copy, key_b, allowed)
    peaks = jnp.max(scores, axis=-1, keepdims=True)
    expos = jnp.exp(scores - peaks)
    totals = jnp.sum(expos, axis=-1, keepdims=True)
    log_total = peaks + jnp.log(totals)
    probs_b = (expos / totals).astype(jnp.bfloat16)
    attended = jnp.einsum("gjts,sgd->tgjd", probs_b, value_b, preferred_element_type=jnp.float32)
    attended = attended.reshape(local_rows, QUERY_HEADS * HEAD_SIZE).astype(jnp.bfloat16)
    middle = state + jnp.dot(attended, w_out, preferred_element_type=jnp.float32)
    mixer_in = norm_rows(middle, g_ffn).astype(jnp.bfloat16)
    logits = jnp.dot(mixer_in, w_router, preferred_element_type=jnp.float32)
    gates = softmax_last(jnp.take_along_axis(logits, route_rows, axis=1))
    slot_ids = slot_table(route_rows)
    outgoing = (
        jnp.zeros((EXPERTS * CAP, MODEL_WIDTH), jnp.bfloat16)
        .at[slot_ids]
        .set(jnp.repeat(mixer_in, TOP, axis=0))
    )
    incoming = lax.all_to_all(
        outgoing.reshape(peers, experts_here * CAP, MODEL_WIDTH),
        "expert",
        split_axis=0,
        concat_axis=0,
        tiled=True,
    )
    incoming = incoming.reshape(peers, experts_here, CAP, MODEL_WIDTH)
    gate_pre = jnp.einsum("secd,edf->secf", incoming, w_gate, preferred_element_type=jnp.float32)
    up_pre = jnp.einsum("secd,edf->secf", incoming, w_up, preferred_element_type=jnp.float32)
    hidden_b = (jax.nn.silu(gate_pre) * up_pre).astype(jnp.bfloat16)
    produced = jnp.einsum(
        "secf,efd->secd", hidden_b, w_down, preferred_element_type=jnp.float32
    ).astype(jnp.bfloat16)
    returned = lax.all_to_all(
        produced.reshape(peers, experts_here * CAP, MODEL_WIDTH),
        "expert",
        split_axis=0,
        concat_axis=0,
        tiled=True,
    )
    picked = returned.reshape(EXPERTS * CAP, MODEL_WIDTH)[slot_ids].reshape(
        local_rows, TOP, MODEL_WIDTH
    )
    new_state = middle + jnp.sum(gates[:, :, None] * picked.astype(jnp.float32), axis=1)
    memo = (
        state,
        normalized_input,
        query_pre,
        prerotation_key,
        query_copy,
        key_b,
        value_b,
        log_total,
        attended,
        middle,
        mixer_in,
        gates,
        slot_ids,
        picked,
        incoming,
        gate_pre,
        up_pre,
        hidden_b,
    )
    return (new_state, memo)


def layer_backward(grad_state, memo, dense, experts, route_rows, cosine, sine, allowed, peers):
    (
        state,
        normalized_input,
        query_pre,
        prerotation_key,
        query_copy,
        key_b,
        value_b,
        log_total,
        attended,
        middle,
        mixer_in,
        gates,
        slot_ids,
        picked,
        incoming,
        gate_pre,
        up_pre,
        hidden_b,
    ) = memo
    w_query, key_weight, value_weight, w_out, w_router, gain_raw = dense
    w_gate, w_up, w_down = experts
    local_rows = state.shape[0]
    experts_here = w_gate.shape[0]
    query_group_size = QUERY_HEADS // KEY_VALUE_HEADS
    scale = 1.0 / math.sqrt(HEAD_SIZE)
    g_attn, g_ffn, g_query, g_key = split_gains(gain_raw.astype(jnp.float32))
    grad_gates = jnp.sum(picked.astype(jnp.float32) * grad_state[:, None, :], axis=2)
    grad_chosen = gates * (grad_gates - jnp.sum(gates * grad_gates, axis=1, keepdims=True))
    choose = (route_rows[:, :, None] == jnp.arange(EXPERTS, dtype=jnp.int32)[None, None, :]).astype(
        jnp.float32
    )
    grad_logits = jnp.sum(choose * grad_chosen[:, :, None], axis=1).astype(jnp.bfloat16)
    grad_router = jnp.dot(mixer_in.T, grad_logits, preferred_element_type=jnp.float32)
    grad_mixer = jnp.dot(grad_logits, w_router.T, preferred_element_type=jnp.float32)
    grad_picked = (
        (gates[:, :, None] * grad_state[:, None, :])
        .astype(jnp.bfloat16)
        .reshape(local_rows * TOP, MODEL_WIDTH)
    )
    outgoing = jnp.zeros((EXPERTS * CAP, MODEL_WIDTH), jnp.bfloat16).at[slot_ids].set(grad_picked)
    grad_produced = lax.all_to_all(
        outgoing.reshape(peers, experts_here * CAP, MODEL_WIDTH),
        "expert",
        split_axis=0,
        concat_axis=0,
        tiled=True,
    )
    grad_produced = grad_produced.reshape(peers, experts_here, CAP, MODEL_WIDTH)
    grad_down = jnp.einsum(
        "secf,secd->efd", hidden_b, grad_produced, preferred_element_type=jnp.float32
    )
    grad_hidden = jnp.einsum(
        "secd,efd->secf", grad_produced, w_down, preferred_element_type=jnp.float32
    )
    sigmoid_gate = jax.nn.sigmoid(gate_pre)
    grad_gate_pre = (
        grad_hidden * up_pre * sigmoid_gate * (1.0 + gate_pre * (1.0 - sigmoid_gate))
    ).astype(jnp.bfloat16)
    grad_up_pre = (grad_hidden * gate_pre * sigmoid_gate).astype(jnp.bfloat16)
    grad_wgate = jnp.einsum(
        "secd,secf->edf", incoming, grad_gate_pre, preferred_element_type=jnp.float32
    )
    grad_wup = jnp.einsum(
        "secd,secf->edf", incoming, grad_up_pre, preferred_element_type=jnp.float32
    )
    grad_incoming = jnp.einsum(
        "secf,edf->secd", grad_gate_pre, w_gate, preferred_element_type=jnp.float32
    )
    grad_incoming = grad_incoming + jnp.einsum(
        "secf,edf->secd", grad_up_pre, w_up, preferred_element_type=jnp.float32
    )
    grad_incoming = grad_incoming.astype(jnp.bfloat16).reshape(
        peers, experts_here * CAP, MODEL_WIDTH
    )
    grad_returned = lax.all_to_all(
        grad_incoming, "expert", split_axis=0, concat_axis=0, tiled=True
    ).reshape(EXPERTS * CAP, MODEL_WIDTH)
    grad_mixer = grad_mixer + jnp.sum(
        grad_returned[slot_ids].reshape(local_rows, TOP, MODEL_WIDTH).astype(jnp.float32), axis=1
    )
    unused_mid, norm_back = jax.vjp(norm_rows, middle, g_ffn)
    grad_mid_part, grad_g_ffn = norm_back(grad_mixer)
    grad_middle = grad_state + grad_mid_part
    grad_middle_low = grad_middle.astype(jnp.bfloat16)
    grad_wout = jnp.dot(attended.T, grad_middle_low, preferred_element_type=jnp.float32)
    attended_gradient = jnp.dot(
        grad_middle_low, w_out.T, preferred_element_type=jnp.float32
    ).astype(jnp.bfloat16)
    attended_gradient = attended_gradient.reshape(
        local_rows, KEY_VALUE_HEADS, query_group_size, HEAD_SIZE
    )
    scores = score_block(query_copy, key_b, allowed)
    probs = jnp.exp(scores - log_total)
    probs_b = probs.astype(jnp.bfloat16)
    grad_probs = jnp.einsum(
        "tgjd,sgd->gjts", attended_gradient, value_b, preferred_element_type=jnp.float32
    )
    value_gradient = jnp.einsum(
        "gjts,tgjd->sgd", probs_b, attended_gradient, preferred_element_type=jnp.float32
    )
    value_gradient_copy = value_gradient.astype(jnp.bfloat16).reshape(
        local_rows, KEY_VALUE_HEADS * HEAD_SIZE
    )
    grad_scores = (
        probs * (grad_probs - jnp.sum(grad_probs * probs, axis=-1, keepdims=True))
    ).astype(jnp.bfloat16)
    grad_query = (
        jnp.einsum("gjts,sgd->tgjd", grad_scores, key_b, preferred_element_type=jnp.float32) * scale
    )
    query_grouped = query_copy.reshape(local_rows, KEY_VALUE_HEADS, query_group_size, HEAD_SIZE)
    grad_key = (
        jnp.einsum("gjts,tgjd->sgd", grad_scores, query_grouped, preferred_element_type=jnp.float32)
        * scale
    )
    unused_heads, head_back = jax.vjp(
        partial(head_piece, cosine=cosine, sine=sine), query_pre, prerotation_key, g_query, g_key
    )
    grad_qpre, prekey_gradient, grad_gq, grad_gk = head_back(
        (grad_query.reshape(local_rows, QUERY_HEADS, HEAD_SIZE), grad_key)
    )
    grad_qpre_b = grad_qpre.astype(jnp.bfloat16).reshape(local_rows, QUERY_HEADS * HEAD_SIZE)
    prekey_gradient_copy = prekey_gradient.astype(jnp.bfloat16).reshape(
        local_rows, KEY_VALUE_HEADS * HEAD_SIZE
    )
    grad_wquery = jnp.dot(normalized_input.T, grad_qpre_b, preferred_element_type=jnp.float32)
    grad_wkey = jnp.dot(
        normalized_input.T, prekey_gradient_copy, preferred_element_type=jnp.float32
    )
    grad_wvalue = jnp.dot(
        normalized_input.T, value_gradient_copy, preferred_element_type=jnp.float32
    )
    grad_normed = jnp.dot(grad_qpre_b, w_query.T, preferred_element_type=jnp.float32)
    grad_normed = grad_normed + jnp.dot(
        prekey_gradient_copy, key_weight.T, preferred_element_type=jnp.float32
    )
    grad_normed = grad_normed + jnp.dot(
        value_gradient_copy, value_weight.T, preferred_element_type=jnp.float32
    )
    unused_state, norm_front = jax.vjp(norm_rows, state, g_attn)
    grad_in_part, grad_g_attn = norm_front(grad_normed)
    grad_input = grad_middle + grad_in_part
    grad_gains = jnp.concatenate([grad_g_attn, grad_g_ffn, grad_gq, grad_gk])
    dense_grads = (grad_wquery, grad_wkey, grad_wvalue, grad_wout, grad_router, grad_gains)
    expert_grads = (grad_wgate, grad_wup, grad_down)
    return (grad_input, dense_grads, expert_grads)


def shards(
    tokens,
    cotangent,
    lengths,
    routes,
    gains,
    w_query,
    key_weight,
    value_weight,
    w_out,
    w_router,
    w_gate,
    w_up,
    w_down,
):
    local_rows = tokens.shape[0]
    peers = lax.axis_size("expert")
    cosine, sine, allowed = geometry(lengths, local_rows)
    state = tokens.astype(jnp.float32)
    memos = []
    for number in range(DECODER_LAYERS):
        dense = (
            lax.all_gather(w_query[number], ("fsdp", "expert"), axis=0, tiled=True),
            lax.all_gather(key_weight[number], ("fsdp", "expert"), axis=0, tiled=True),
            lax.all_gather(value_weight[number], ("fsdp", "expert"), axis=0, tiled=True),
            lax.all_gather(w_out[number], ("fsdp", "expert"), axis=0, tiled=True),
            lax.all_gather(w_router[number], ("fsdp", "expert"), axis=0, tiled=True),
            lax.all_gather(gains[number], ("fsdp", "expert"), axis=0, tiled=True),
        )
        experts = (
            lax.all_gather(w_gate[number], "fsdp", axis=1, tiled=True),
            lax.all_gather(w_up[number], "fsdp", axis=1, tiled=True),
            lax.all_gather(w_down[number], "fsdp", axis=2, tiled=True),
        )
        state, memo = layer_forward(
            state, dense, experts, routes[number], cosine, sine, allowed, peers
        )
        memos.append(memo)
    result = state.astype(jnp.bfloat16)
    grad_state = cotangent.astype(jnp.float32)
    dense_list = []
    expert_list = []
    for number in reversed(range(DECODER_LAYERS)):
        dense = (
            lax.all_gather(w_query[number], ("fsdp", "expert"), axis=0, tiled=True),
            lax.all_gather(key_weight[number], ("fsdp", "expert"), axis=0, tiled=True),
            lax.all_gather(value_weight[number], ("fsdp", "expert"), axis=0, tiled=True),
            lax.all_gather(w_out[number], ("fsdp", "expert"), axis=0, tiled=True),
            lax.all_gather(w_router[number], ("fsdp", "expert"), axis=0, tiled=True),
            lax.all_gather(gains[number], ("fsdp", "expert"), axis=0, tiled=True),
        )
        experts = (
            lax.all_gather(w_gate[number], "fsdp", axis=1, tiled=True),
            lax.all_gather(w_up[number], "fsdp", axis=1, tiled=True),
            lax.all_gather(w_down[number], "fsdp", axis=2, tiled=True),
        )
        grad_state, dense_grads, expert_grads = layer_backward(
            grad_state, memos[number], dense, experts, routes[number], cosine, sine, allowed, peers
        )
        dense_shards = (
            lax.psum_scatter(dense_grads[0], ("fsdp", "expert"), scatter_dimension=0, tiled=True),
            lax.psum_scatter(dense_grads[1], ("fsdp", "expert"), scatter_dimension=0, tiled=True),
            lax.psum_scatter(dense_grads[2], ("fsdp", "expert"), scatter_dimension=0, tiled=True),
            lax.psum_scatter(dense_grads[3], ("fsdp", "expert"), scatter_dimension=0, tiled=True),
            lax.psum_scatter(dense_grads[4], ("fsdp", "expert"), scatter_dimension=0, tiled=True),
            lax.psum_scatter(dense_grads[5], ("fsdp", "expert"), scatter_dimension=0, tiled=True),
        )
        expert_shards = (
            lax.psum_scatter(
                expert_grads[0].astype(jnp.bfloat16), "fsdp", scatter_dimension=1, tiled=True
            ).astype(jnp.float32),
            lax.psum_scatter(
                expert_grads[1].astype(jnp.bfloat16), "fsdp", scatter_dimension=1, tiled=True
            ).astype(jnp.float32),
            lax.psum_scatter(
                expert_grads[2].astype(jnp.bfloat16), "fsdp", scatter_dimension=2, tiled=True
            ).astype(jnp.float32),
        )
        dense_list.insert(0, dense_shards)
        expert_list.insert(0, expert_shards)
    d_gains = jnp.stack([entry[5] for entry in dense_list])
    d_query = jnp.stack([entry[0] for entry in dense_list])
    d_key = jnp.stack([entry[1] for entry in dense_list])
    d_value = jnp.stack([entry[2] for entry in dense_list])
    d_out = jnp.stack([entry[3] for entry in dense_list])
    d_router = jnp.stack([entry[4] for entry in dense_list])
    d_gate = jnp.stack([entry[0] for entry in expert_list])
    d_up = jnp.stack([entry[1] for entry in expert_list])
    d_down = jnp.stack([entry[2] for entry in expert_list])
    return (
        result,
        grad_state.astype(jnp.bfloat16),
        d_gains,
        d_query,
        d_key,
        d_value,
        d_out,
        d_router,
        d_gate,
        d_up,
        d_down,
    )


def general(mesh):
    return jax.shard_map(
        shards,
        mesh=mesh,
        in_specs=(
            P(("fsdp", "expert"), None),
            P(("fsdp", "expert"), None),
            P(("fsdp", "expert"), None),
            P(None, ("fsdp", "expert"), None),
            P(None, ("fsdp", "expert")),
            P(None, ("fsdp", "expert"), None),
            P(None, ("fsdp", "expert"), None),
            P(None, ("fsdp", "expert"), None),
            P(None, ("fsdp", "expert"), None),
            P(None, ("fsdp", "expert"), None),
            P(None, "expert", "fsdp", None),
            P(None, "expert", "fsdp", None),
            P(None, "expert", None, "fsdp"),
        ),
        out_specs=(
            P(("fsdp", "expert"), None),
            P(("fsdp", "expert"), None),
            P(None, ("fsdp", "expert")),
            P(None, ("fsdp", "expert"), None),
            P(None, ("fsdp", "expert"), None),
            P(None, ("fsdp", "expert"), None),
            P(None, ("fsdp", "expert"), None),
            P(None, ("fsdp", "expert"), None),
            P(None, "expert", "fsdp", None),
            P(None, "expert", "fsdp", None),
            P(None, "expert", None, "fsdp"),
        ),
        check_vma=False,
    )


CHIPS = ("fsdp", "line")
EVERY = ("fsdp", "line", "core")


def swap(operand):
    return lax.ppermute(operand, "core", [(0, 1), (1, 0)])


def by_core(core, mine, other, axis):
    return jnp.where(
        core == 0,
        jnp.concatenate([mine, other], axis=axis),
        jnp.concatenate([other, mine], axis=axis),
    )


def turned(operand):
    half_rows = operand.shape[0] // 2
    return jnp.concatenate([operand[half_rows:], operand[:half_rows]], axis=0)


def offload_gather(operand):
    return lax.all_gather(operand, CHIPS, axis=0, tiled=True)


def offload_scatter(operand):
    return lax.psum_scatter(operand, CHIPS, scatter_dimension=0, tiled=True)


PAIR = 4
ROW_UNITS = 8


def routes_of_shards(depth):
    offsets = [s * k for k in range(1, depth) for s in (-1, 1)]

    def source(offset):
        return "below" if offset < 0 else "above"

    def onward(offset):
        return "above" if offset < 0 else "below"

    def further(offset):
        return offset - 1 if offset < 0 else offset + 1

    def line_hops(bits, first, last, offset):
        if offset == 0:
            return [
                ("above", first, last, (bits, -1, first, last, "below")),
                ("below", first, last, (bits, 1, first, last, "above")),
            ]
        if abs(further(offset)) >= depth:
            return []
        return [(onward(offset), first, last, (bits, further(offset), first, last, source(offset)))]

    plan = []
    own = [("x", 0, 8, (1, 0, 0, 8, "x")), ("y", 0, 8, (2, 0, 0, 8, "y"))]
    plan.append((None, own + line_hops(0, 0, 8, 0)))
    plan.append(
        ((1, 0, 0, 8, "x"), [("y", 3, 7, (3, 0, 3, 7, "y"))] + line_hops(1, 6, 8, 0))
    )
    plan.append(
        (
            (2, 0, 0, 8, "y"),
            [("x", 0, 3, (3, 0, 0, 3, "x")), ("x", 7, 8, (3, 0, 7, 8, "x"))]
            + line_hops(2, 6, 8, 0),
        )
    )

    def spread(offset):
        return (
            (0, offset, 0, 8, source(offset)),
            line_hops(0, 0, 8, offset)
            + [("x", 0, 6, (1, offset, 0, 6, "x")), ("y", 0, 6, (2, offset, 0, 6, "y"))],
        )

    def crossed(offset):
        return [
            ((1, offset, 0, 6, "x"), [("y", 3, 6, (3, offset, 3, 6, "y"))]),
            ((2, offset, 0, 6, "y"), [("x", 0, 3, (3, offset, 0, 3, "x"))]),
        ]

    def lined(offset):
        return [
            ((bits, offset, 6, 8, source(offset)), line_hops(bits, 6, 8, offset))
            for bits in (1, 2, 3)
        ]

    def last(offset):
        return [((3, offset, 3, 6, "y"), []), ((3, offset, 0, 3, "x"), [])]

    steps = [(-k, k) for k in range(1, depth)]
    plan += [spread(o) for o in steps[0]]
    plan += [
        ((3, 0, 3, 7, "y"), []),
        ((3, 0, 0, 3, "x"), []),
        ((3, 0, 7, 8, "x"), line_hops(3, 6, 8, 0)),
    ]
    for number, pair in enumerate(steps):
        for offset in pair:
            plan += crossed(offset)
        if number + 1 < len(steps):
            plan += [spread(o) for o in steps[number + 1]]
        for offset in pair:
            plan += lined(offset)
        for offset in pair:
            plan += last(offset)
    return plan


class Place:
    def __init__(self, depth):
        self.depth = depth
        self.pair = lax.axis_index("fsdp")
        self.line = lax.axis_index("line")
        self.core = lax.axis_index("core")
        x = lax.rem(self.pair, 2)
        y = lax.div(self.pair, 2)
        self.pairs = [
            self.pair,
            self.pair + 1 - 2 * x,
            self.pair + 2 - 4 * y,
            PAIR - 1 - self.pair,
        ]

    def shard(self, bits, offset):
        return self.pairs[bits] * self.depth + self.line + offset

    def device(self, neighbour):
        if neighbour == "x":
            return (self.pairs[1], self.line, self.core)
        if neighbour == "y":
            return (self.pairs[2], self.line, self.core)
        step = 1 if neighbour == "above" else -1
        return (self.pair, self.line + step, self.core)

    def holds(self, offset, neighbour=None):
        low, high = min(offset, 0), max(offset, 0)
        if neighbour == "above":
            high = max(high, 1)
        if neighbour == "below":
            low = min(low, -1)
        tests = []
        if low < 0:
            tests.append(self.line >= -low)
        if high > 0:
            tests.append(self.line < self.depth - high)
        if not tests:
            return None
        return tests[0] if len(tests) == 1 else jnp.logical_and(tests[0], tests[1])

    def meet(self):
        barrier = pltpu.get_barrier_semaphore()
        for neighbour in ("x", "y", "above", "below"):

            def greet(neighbour=neighbour):
                pl.semaphore_signal(
                    barrier,
                    inc=1,
                    device_id=self.device(neighbour),
                    device_id_type=pl.DeviceIdType.MESH,
                )

            when(self.holds(0, neighbour), greet)
        ends = (self.line == 0).astype(jnp.int32) + (self.line == self.depth - 1).astype(jnp.int32)
        pl.semaphore_wait(barrier, 4 - ends)


def when(test, action):
    if test is None:
        action()
    else:
        pl.when(test)(action)


def gather_kernel(depth, x_ref, out_ref, own_sem, send_sems, recv_sems):
    plan = routes_of_shards(depth)
    number_of = {item: i for i, (item, _) in enumerate(plan)}
    unit = x_ref.shape[0] // ROW_UNITS
    here = Place(depth)
    own = pltpu.make_async_copy(x_ref, out_ref.at[here.shard(0, 0)], own_sem)
    own.start()
    here.meet()
    sent = []
    for item, hops in plan:
        bits, offset = (0, 0) if item is None else item[:2]

        def step(item=item, hops=hops, bits=bits, offset=offset, site=len(sent)):
            if item is not None:
                piece = out_ref.at[
                    here.shard(bits, offset), pl.ds(item[2] * unit, (item[3] - item[2]) * unit)
                ]
                pltpu.make_async_remote_copy(
                    src_ref=piece,
                    dst_ref=piece,
                    send_sem=send_sems.at[0],
                    recv_sem=recv_sems.at[number_of[item]],
                    device_id=here.device("x"),
                    device_id_type=pl.DeviceIdType.MESH,
                ).wait_recv()
            for hop, (neighbour, first, last, there) in enumerate(hops):
                when(
                    here.holds(0, neighbour) if neighbour in ("above", "below") else None,
                    lambda n=neighbour, f=first, l=last, t=there, s=site + hop: passing(
                        bits, offset, n, f, l, t, s, item is None
                    ).start(),
                )

        def passing(bits, offset, neighbour, first, last, there, site, own_piece):
            rows = pl.ds(first * unit, (last - first) * unit)
            target = out_ref.at[here.shard(bits, offset), rows]
            return pltpu.make_async_remote_copy(
                src_ref=x_ref.at[rows] if own_piece else target,
                dst_ref=target,
                send_sem=send_sems.at[site],
                recv_sem=recv_sems.at[number_of[there]],
                device_id=here.device(neighbour),
                device_id_type=pl.DeviceIdType.MESH,
            )

        when(None if item is None else here.holds(offset), step)
        for neighbour, first, last, there in hops:
            sent.append((bits, offset, neighbour, first, last, there, len(sent), item is None))
    for bits, offset, neighbour, first, last, there, site, own_piece in sent:

        def finish(a=(bits, offset, neighbour, first, last, there, site, own_piece)):
            passing(*a).wait_send()

        when(here.holds(offset, neighbour), finish)
    own.wait()


def count_plan(depth):
    plan = routes_of_shards(depth)
    return len(plan), sum(len(hops) for _, hops in plan)


def gather_chips(operand, collective_id):
    depth = lax.axis_size("line")
    items, hops = count_plan(depth)
    chips = PAIR * depth
    rows, columns = operand.shape
    return pl.pallas_call(
        partial(gather_kernel, depth),
        out_shape=jax.ShapeDtypeStruct((chips, rows, columns), operand.dtype),
        in_specs=[pl.BlockSpec(memory_space=pl.ANY)],
        out_specs=pl.BlockSpec(memory_space=pl.ANY),
        scratch_shapes=[
            pltpu.SemaphoreType.DMA,
            pltpu.SemaphoreType.DMA((hops,)),
            pltpu.SemaphoreType.DMA((items,)),
        ],
        compiler_params=pltpu.CompilerParams(collective_id=collective_id, has_side_effects=True),
        cost_estimate=pl.CostEstimate(
            flops=0, bytes_accessed=8 * chips * rows * columns, transcendentals=0
        ),
        name="gather_chips",
    )(operand).reshape(chips * rows, columns)


def scatter_kernel(depth, x_ref, out_ref, sums, landed, own_sem, send_sems, recv_sems):
    plan = routes_of_shards(depth)
    number_of = {item: i for i, (item, _) in enumerate(plan)}
    unit = x_ref.shape[1] // ROW_UNITS
    here = Place(depth)
    own = pltpu.make_async_copy(x_ref, sums, own_sem)
    own.start()
    here.meet()
    own.wait()
    sites = {}
    start = 0
    for item, hops in plan:
        for neighbour, first, last, there in hops:
            sites[there] = (number_of[there] - 1, start)
            start += (last - first) * unit

    def total(shard, first, last, base):
        @pl.loop(0, (last - first) * unit // 16)
        def _(i):
            rows = pl.ds(first * unit + i * 16, 16)
            value = sums[shard, rows].astype(jnp.float32)
            value = value + landed[pl.ds(base + i * 16, 16)].astype(jnp.float32)
            sums[shard, rows] = value.astype(sums.dtype)

    def sending(item):
        bits, offset, first, last, neighbour = item
        sem, base = sites[item]
        size = (last - first) * unit
        return pltpu.make_async_remote_copy(
            src_ref=sums.at[here.shard(bits, offset), pl.ds(first * unit, size)],
            dst_ref=landed.at[pl.ds(base, size)],
            send_sem=send_sems.at[number_of[item]],
            recv_sem=recv_sems.at[sem],
            device_id=here.device(neighbour),
            device_id_type=pl.DeviceIdType.MESH,
        )

    for item, hops in reversed(plan):
        bits, offset = (0, 0) if item is None else item[:2]

        def step(item=item, hops=hops, bits=bits, offset=offset):
            for neighbour, first, last, there in hops:

                def take(first=first, last=last, there=there):
                    sem, base = sites[there]
                    size = (last - first) * unit
                    pltpu.make_async_remote_copy(
                        src_ref=landed.at[pl.ds(base, size)],
                        dst_ref=landed.at[pl.ds(base, size)],
                        send_sem=send_sems.at[0],
                        recv_sem=recv_sems.at[sem],
                        device_id=here.device("x"),
                        device_id_type=pl.DeviceIdType.MESH,
                    ).wait_recv()
                    total(here.shard(bits, offset), first, last, base)

                when(
                    here.holds(0, neighbour) if neighbour in ("above", "below") else None,
                    take,
                )
            if item is not None:
                sending(item).start()

        when(None if item is None else here.holds(offset), step)
    out_ref[...] = sums[here.shard(0, 0)]
    for item, hops in plan:
        if item is not None:
            when(here.holds(item[1]), lambda item=item: sending(item).wait_send())


def scatter_chips(operand, collective_id):
    depth = lax.axis_size("line")
    chips = PAIR * depth
    items, hops = count_plan(depth)
    rows, columns = operand.shape[0] // chips, operand.shape[1]
    landed = sum(
        (last - first) * rows // ROW_UNITS
        for _, row in routes_of_shards(depth)
        for _, first, last, _ in row
    )
    return pl.pallas_call(
        partial(scatter_kernel, depth),
        out_shape=jax.ShapeDtypeStruct((rows, columns), operand.dtype),
        in_specs=[pl.BlockSpec(memory_space=pl.ANY)],
        out_specs=pl.BlockSpec(memory_space=pltpu.VMEM),
        scratch_shapes=[
            pltpu.VMEM((chips, rows, columns), operand.dtype),
            pltpu.VMEM((landed, columns), operand.dtype),
            pltpu.SemaphoreType.DMA,
            pltpu.SemaphoreType.DMA((items,)),
            pltpu.SemaphoreType.DMA((hops,)),
        ],
        compiler_params=pltpu.CompilerParams(
            collective_id=collective_id, has_side_effects=True, vmem_limit_bytes=50 * 2**20
        ),
        cost_estimate=pl.CostEstimate(
            flops=0, bytes_accessed=8 * chips * rows * columns, transcendentals=0
        ),
        name="scatter_chips",
    )(operand.reshape(chips, rows, columns))


def spread_experts(operand, place, width):
    own = lax.dynamic_index_in_dim(operand, place, 0, keepdims=False)
    pieces = jnp.zeros_like(operand)
    pieces = lax.dynamic_update_index_in_dim(pieces, own, place, 0)
    for step in range(1, width):
        sent = lax.dynamic_index_in_dim(operand, place ^ step, 0, keepdims=False)
        got = lax.ppermute(sent, "fsdp", [(i, i ^ step) for i in range(width)])
        pieces = lax.dynamic_update_index_in_dim(pieces, got, place ^ step, 0)
    return pieces


def spread_columns(operand, place, width):
    columns = operand.shape[2]
    own = lax.dynamic_index_in_dim(operand, place, 0, keepdims=False)
    whole = jnp.zeros((operand.shape[1], width * columns), operand.dtype)
    whole = lax.dynamic_update_slice_in_dim(whole, own, place * columns, 1)
    for step in range(1, width):
        sent = lax.dynamic_index_in_dim(operand, place ^ step, 0, keepdims=False)
        got = lax.ppermute(sent, "fsdp", [(i, i ^ step) for i in range(width)])
        whole = lax.dynamic_update_slice_in_dim(whole, got, (place ^ step) * columns, 1)
    return whole


def pair_scores(query_copy, key_b, allowed):
    return jnp.where(
        allowed[:, None, None],
        jnp.einsum("btgjd,bsgd->bgjts", query_copy, key_b, preferred_element_type=jnp.float32)
        * (1.0 / math.sqrt(HEAD_SIZE)),
        -1e30,
    )


def attention_forward(state, dense, angles):
    core, cosine, sine, allowed = angles
    w_qkv, w_out, g_attn, g_query, g_key = dense
    rows = state.shape[0]
    heads = QUERY_HEADS // 2
    pairs = KEY_VALUE_HEADS // 2
    group = heads // KEY_VALUE_HEADS
    normed = norm_rows(state, g_attn).astype(jnp.bfloat16)
    normed = jnp.concatenate([normed, swap(normed)], axis=0)
    qkv = jnp.dot(normed, w_qkv, preferred_element_type=jnp.float32)
    query_pre = qkv[:, : heads * HEAD_SIZE].reshape(2 * rows, heads, HEAD_SIZE)
    key_pre = qkv[:, heads * HEAD_SIZE : (heads + pairs) * HEAD_SIZE].reshape(
        2 * rows, pairs, HEAD_SIZE
    )
    value_half = qkv[:, (heads + pairs) * HEAD_SIZE :].astype(jnp.bfloat16)
    query_f, key_f = head_piece(query_pre, key_pre, g_query, g_key, cosine, sine)
    query_b = query_f.astype(jnp.bfloat16).reshape(2, rows, KEY_VALUE_HEADS, group, HEAD_SIZE)
    key_half = key_f.astype(jnp.bfloat16).reshape(2 * rows, pairs * HEAD_SIZE)
    both = jnp.concatenate([key_half, value_half], axis=1)
    other = turned(swap(both))
    width = pairs * HEAD_SIZE
    key_b = by_core(core, key_half, other[:, :width], 1)
    value_b = by_core(core, value_half, other[:, width:], 1)
    key_b = key_b.reshape(2, rows, KEY_VALUE_HEADS, HEAD_SIZE)
    value_b = value_b.reshape(2, rows, KEY_VALUE_HEADS, HEAD_SIZE)
    scores = pair_scores(query_b, key_b, allowed)
    peaks = jnp.max(scores, axis=-1, keepdims=True)
    expos = jnp.exp(scores - peaks)
    totals = jnp.sum(expos, axis=-1, keepdims=True)
    log_total = peaks + jnp.log(totals)
    probs_b = (expos / totals).astype(jnp.bfloat16)
    attended = jnp.einsum("bgjts,bsgd->btgjd", probs_b, value_b, preferred_element_type=jnp.float32)
    attended = attended.reshape(2 * rows, heads * HEAD_SIZE).astype(jnp.bfloat16)
    partial_out = jnp.dot(attended, w_out, preferred_element_type=jnp.float32)
    middle = state + (partial_out[:rows] + swap(partial_out[rows:]))
    return middle, (normed, query_pre, key_pre, query_b, key_b, value_b, log_total, attended)


def attention_backward(grad_middle, memo, dense, angles):
    core, cosine, sine, allowed = angles
    normed, query_pre, key_pre, query_b, key_b, value_b, log_total, attended = memo
    w_qkv, w_out, g_attn, g_query, g_key = dense
    rows = grad_middle.shape[0]
    heads = QUERY_HEADS // 2
    pairs = KEY_VALUE_HEADS // 2
    width = pairs * HEAD_SIZE
    scale = 1.0 / math.sqrt(HEAD_SIZE)
    low = grad_middle.astype(jnp.bfloat16)
    low = jnp.concatenate([low, swap(low)], axis=0)
    grad_attended = lax.dot_general(
        low, w_out, (((1,), (1,)), ((), ())), preferred_element_type=jnp.float32
    ).astype(jnp.bfloat16)
    grad_wout = lax.dot_general(
        attended, low, (((0,), (0,)), ((), ())), preferred_element_type=jnp.float32
    ).astype(jnp.bfloat16)
    grad_attended = grad_attended.reshape(query_b.shape)
    probs = jnp.exp(pair_scores(query_b, key_b, allowed) - log_total)
    probs_b = probs.astype(jnp.bfloat16)
    grad_probs = jnp.einsum(
        "btgjd,bsgd->bgjts", grad_attended, value_b, preferred_element_type=jnp.float32
    )
    grad_value = jnp.einsum(
        "bgjts,btgjd->bsgd", probs_b, grad_attended, preferred_element_type=jnp.float32
    ).reshape(2 * rows, 2 * width)
    grad_scores = (
        probs * (grad_probs - jnp.sum(grad_probs * probs, axis=-1, keepdims=True))
    ).astype(jnp.bfloat16)
    grad_query = (
        jnp.einsum("bgjts,bsgd->btgjd", grad_scores, key_b, preferred_element_type=jnp.float32)
        * scale
    ).reshape(2 * rows, heads, HEAD_SIZE)
    grad_key = (
        jnp.einsum("bgjts,btgjd->bsgd", grad_scores, query_b, preferred_element_type=jnp.float32)
        * scale
    ).reshape(2 * rows, 2 * width)
    mine = jnp.where(core == 0, 0, width)
    theirs = width - mine
    sent = jnp.concatenate(
        [
            lax.dynamic_slice_in_dim(grad_key, theirs, width, 1),
            lax.dynamic_slice_in_dim(grad_value, theirs, width, 1),
        ],
        axis=1,
    )
    got = turned(swap(sent))
    grad_key = lax.dynamic_slice_in_dim(grad_key, mine, width, 1) + got[:, :width]
    grad_value = lax.dynamic_slice_in_dim(grad_value, mine, width, 1) + got[:, width:]
    unused_heads, head_back = jax.vjp(
        partial(head_piece, cosine=cosine, sine=sine), query_pre, key_pre, g_query, g_key
    )
    grad_qpre, grad_kpre, grad_gq, grad_gk = head_back(
        (grad_query, grad_key.reshape(2 * rows, pairs, HEAD_SIZE))
    )
    grad_qkv = jnp.concatenate(
        [
            grad_qpre.astype(jnp.bfloat16).reshape(2 * rows, heads * HEAD_SIZE),
            grad_kpre.astype(jnp.bfloat16).reshape(2 * rows, width),
            grad_value.astype(jnp.bfloat16),
        ],
        axis=1,
    )
    grad_wqkv = lax.dot_general(
        normed, grad_qkv, (((0,), (0,)), ((), ())), preferred_element_type=jnp.float32
    ).astype(jnp.bfloat16)
    grad_normed = lax.dot_general(
        grad_qkv, w_qkv, (((1,), (1,)), ((), ())), preferred_element_type=jnp.float32
    )
    grad_normed = grad_normed[:rows] + swap(grad_normed[rows:])
    return grad_normed, grad_wqkv, grad_wout, grad_gq, grad_gk


def expert_forward(gathered, picks, row_gates, weights):
    blocks = picks[0].shape[0]
    width = gathered.shape[1]
    grouped = gathered.reshape(blocks, -1, width)
    memo = []
    total = None
    for pick, row_gate, (w_up_gate, w_down) in zip(picks, row_gates, weights):
        hidden_size = w_down.shape[0]
        rows = jnp.einsum("bst,btd->bsd", pick, grouped, preferred_element_type=jnp.float32)
        rows = rows.astype(jnp.bfloat16).reshape(-1, width)
        pre = jnp.dot(rows, w_up_gate, preferred_element_type=jnp.float32)
        gate_pre = pre[:, :hidden_size]
        up_pre = pre[:, hidden_size:]
        hidden = (jax.nn.silu(gate_pre) * up_pre).astype(jnp.bfloat16)
        produced = jnp.dot(hidden, w_down, preferred_element_type=jnp.float32)
        produced = (produced * row_gate).astype(jnp.bfloat16)
        back = jnp.einsum(
            "bst,bsd->btd",
            pick,
            produced.reshape(blocks, -1, width),
            preferred_element_type=jnp.float32,
        )
        total = back if total is None else total + back
        memo.append((rows, gate_pre, up_pre, hidden))
    return total.reshape(-1, width).astype(jnp.bfloat16), memo


def expert_backward(gathered, picks, row_gates, weights, memo):
    blocks = picks[0].shape[0]
    width = gathered.shape[1]
    grouped = gathered.reshape(blocks, -1, width)
    total = None
    grads = []
    gate_grads = []
    for pick, row_gate, (w_up_gate, w_down), kept in zip(picks, row_gates, weights, memo):
        rows, gate_pre, up_pre, hidden = kept
        grad_rows = jnp.einsum("bst,btd->bsd", pick, grouped, preferred_element_type=jnp.float32)
        grad_rows = grad_rows.astype(jnp.bfloat16).reshape(-1, width)
        through = lax.dot_general(
            grad_rows, w_down, (((1,), (1,)), ((), ())), preferred_element_type=jnp.float32
        )
        hidden_f = hidden.astype(jnp.float32)
        gate_grad = jnp.sum(hidden_f * through, axis=1)
        gate_grads.append(
            jnp.sum(
                pick.astype(jnp.float32) * gate_grad.reshape(blocks, -1)[:, :, None], axis=1
            ).reshape(-1)
        )
        grad_hidden = through * row_gate
        sigmoid_gate = jax.nn.sigmoid(gate_pre)
        grad_pre = jnp.concatenate(
            [
                (
                    grad_hidden * up_pre * sigmoid_gate * (1.0 + gate_pre * (1.0 - sigmoid_gate))
                ).astype(jnp.bfloat16),
                (grad_hidden * gate_pre * sigmoid_gate).astype(jnp.bfloat16),
            ],
            axis=1,
        )
        grad_down = lax.dot_general(
            (hidden_f * row_gate).astype(jnp.bfloat16),
            grad_rows,
            (((0,), (0,)), ((), ())),
            preferred_element_type=jnp.float32,
        ).astype(jnp.bfloat16)
        grad_up_gate = lax.dot_general(
            rows, grad_pre, (((0,), (0,)), ((), ())), preferred_element_type=jnp.float32
        ).astype(jnp.bfloat16)
        grad_in = lax.dot_general(
            grad_pre, w_up_gate, (((1,), (1,)), ((), ())), preferred_element_type=jnp.float32
        ).astype(jnp.bfloat16)
        back = jnp.einsum(
            "bst,bsd->btd",
            pick,
            grad_in.reshape(blocks, -1, width),
            preferred_element_type=jnp.float32,
        )
        total = back if total is None else total + back
        grads.append((grad_up_gate, grad_down))
    return total.reshape(-1, width).astype(jnp.bfloat16), grads, gate_grads


def chip_shards(
    tokens,
    cotangent,
    lengths,
    routes,
    gains,
    w_query,
    key_weight,
    value_weight,
    w_out,
    w_router,
    w_gate,
    w_up,
    w_down,
):
    rows = tokens.shape[0]
    width = lax.axis_size("fsdp")
    place = lax.axis_index("fsdp")
    line = lax.axis_index("line")
    core = lax.axis_index("core")
    devices = width * lax.axis_size("line") * 2
    chips = devices // 2
    chip = place * lax.axis_size("line") + line
    half_heads = QUERY_HEADS // 2
    ff = w_gate.shape[3]
    short = w_query.shape[1]
    experts_here = w_gate.shape[1]
    gain_columns = -(-gains.size // short)
    side = jnp.concatenate(
        [w_router[number] for number in range(DECODER_LAYERS)]
        + [jnp.pad(gains.reshape(-1), (0, gain_columns * short - gains.size)).reshape(short, -1)],
        axis=1,
    )
    side = by_core(core, side, swap(side), 0)
    router_columns = DECODER_LAYERS * EXPERTS
    cut = side.shape[1]
    small = jnp.concatenate(
        [side] + [routes[number].astype(jnp.bfloat16) for number in range(DECODER_LAYERS)], axis=1
    )
    small = offload_gather(jnp.pad(small, ((0, 0), (0, -small.shape[1] % 128))))
    routers = [
        small[:, number * EXPERTS : (number + 1) * EXPERTS] for number in range(DECODER_LAYERS)
    ]
    all_gains = (
        small[:, router_columns:cut]
        .reshape(devices, -1)[:, : gains.size]
        .reshape(devices, DECODER_LAYERS, -1)
        .transpose(1, 0, 2)
        .reshape(DECODER_LAYERS, -1)
        .astype(jnp.float32)
    )
    all_routes = (
        small[:, cut : cut + DECODER_LAYERS * TOP]
        .reshape(chips, rows, DECODER_LAYERS, TOP)
        .transpose(0, 2, 1, 3)
    )
    chosen = jnp.any(
        all_routes[..., None] == jnp.arange(EXPERTS, dtype=jnp.bfloat16), axis=3
    )
    chosen_f = chosen.astype(jnp.bfloat16)
    before = jnp.tril(jnp.ones((rows, rows), jnp.bfloat16), -1)
    ranks = jnp.einsum(
        "ts,clse->clte", before, chosen_f, preferred_element_type=jnp.float32
    )
    first = (line * 2 + core) * experts_here + place
    second = (line * 2 + (1 - core)) * experts_here + place
    slots = jnp.arange(CAP, dtype=jnp.float32)

    def pick_of(number, expert):
        named = lax.dynamic_index_in_dim(chosen[:, number], expert, 2, keepdims=False)
        rank = lax.dynamic_index_in_dim(ranks[:, number], expert, 2, keepdims=False)
        return (
            (rank[:, None, :] == slots[None, :, None]) & named[:, None, :]
        ).astype(jnp.bfloat16)

    picks = [(pick_of(number, first), pick_of(number, second)) for number in range(DECODER_LAYERS)]

    other_lengths = swap(lengths)
    here = geometry(lengths, rows)
    there = geometry(other_lengths, rows)
    cosine = jnp.concatenate([here[0], there[0]], axis=0)
    sine = jnp.concatenate([here[1], there[1]], axis=0)
    allowed = jnp.stack([here[2], there[2]])
    angles = (core, cosine, sine, allowed)

    heads = w_query.reshape(DECODER_LAYERS, short, half_heads, 2, HEAD_SIZE)
    pair_width = KEY_VALUE_HEADS // 2 * HEAD_SIZE

    def columns_of(which):
        return jnp.concatenate(
            [
                lax.dynamic_index_in_dim(heads, which, 3, keepdims=False).reshape(
                    DECODER_LAYERS, short, half_heads * HEAD_SIZE
                ),
                lax.dynamic_slice_in_dim(key_weight, which * pair_width, pair_width, 2),
                lax.dynamic_slice_in_dim(value_weight, which * pair_width, pair_width, 2),
            ],
            axis=2,
        )

    chip_qkv = by_core(core, columns_of(core), swap(columns_of(1 - core)), 1)
    g_attn, g_ffn, g_query, g_key = zip(*[split_gains(all_gains[i]) for i in range(DECODER_LAYERS)])

    state = tokens.astype(jnp.float32)
    kept = []
    for number in range(DECODER_LAYERS):
        first_layer = number == 0
        dense = (
            gather_chips(chip_qkv[number], 1) if first_layer else offload_gather(chip_qkv[number]),
            offload_gather(w_out[number]),
            g_attn[number],
            g_query[number],
            g_key[number],
        )
        up_gate = spread_experts(
            jnp.concatenate([w_gate[number], w_up[number]], axis=2), place, width
        ).reshape(MODEL_WIDTH, 2 * ff)
        down = spread_columns(w_down[number], place, width)
        weights = ((up_gate, down), (swap(up_gate), swap(down)))
        middle, memo = attention_forward(state, dense, angles)
        mixer_in = norm_rows(middle, g_ffn[number]).astype(jnp.bfloat16)
        gathered = gather_chips(mixer_in, 2)
        logits = jnp.dot(gathered, routers[number], preferred_element_type=jnp.float32)
        named = chosen[:, number].reshape(chips * rows, EXPERTS)
        gates = softmax_last(jnp.where(named, logits, -1e30))
        row_gates = []
        for pick, expert in zip(picks[number], (first, second)):
            gate = lax.dynamic_index_in_dim(gates, expert, 1, keepdims=False)
            row_gates.append(
                jnp.sum(
                    pick.astype(jnp.float32) * gate.reshape(chips, 1, rows), axis=2
                ).reshape(-1, 1)
            )
        produced, expert_memo = expert_forward(gathered, picks[number], row_gates, weights)
        new_state = middle + scatter_chips(produced, 3).astype(jnp.float32)
        own_gates = lax.dynamic_slice_in_dim(gates, chip * rows, rows, 0)
        kept.append(
            (state, middle, mixer_in, own_gates, row_gates, dense, weights, memo, expert_memo)
        )
        state = new_state
    result = state.astype(jnp.bfloat16)

    grad_state = cotangent.astype(jnp.float32)
    grad_low = cotangent
    grad_gathered = offload_gather(cotangent)
    outs = []
    small_grads = []
    for number in reversed(range(DECODER_LAYERS)):
        state, middle, mixer_in, own_gates, row_gates, dense, weights, memo, expert_memo = kept[
            number
        ]
        back, expert_grads, gate_grads = expert_backward(
            grad_gathered, picks[number], row_gates, weights, expert_memo
        )
        spread = jnp.zeros((chips * rows, EXPERTS), jnp.float32)
        for gate_grad, expert in zip(gate_grads, (first, second)):
            spread = lax.dynamic_update_index_in_dim(spread, gate_grad, expert, 1)
        grad_gates = offload_scatter(spread)
        grad_logits = (
            own_gates
            * (grad_gates - jnp.sum(own_gates * grad_gates, axis=1, keepdims=True))
        ).astype(jnp.bfloat16)
        grad_router = lax.dot_general(
            mixer_in, grad_logits, (((0,), (0,)), ((), ())), preferred_element_type=jnp.float32
        )
        grad_mixer = scatter_chips(back, 3).astype(jnp.float32) + lax.dot_general(
            grad_logits,
            routers[number],
            (((1,), (1,)), ((), ())),
            preferred_element_type=jnp.float32,
        )
        unused_mid, norm_back = jax.vjp(norm_rows, middle, g_ffn[number])
        grad_mid_part, grad_g_ffn = norm_back(grad_mixer)
        grad_middle = grad_state + grad_mid_part
        grad_normed, grad_wqkv, grad_wout, grad_gq, grad_gk = attention_backward(
            grad_middle, memo, dense, angles
        )
        unused_state, norm_front = jax.vjp(norm_rows, state, g_attn[number])
        grad_in_part, grad_g_attn = norm_front(grad_normed)
        grad_state = grad_middle + grad_in_part
        grad_low = grad_state.astype(jnp.bfloat16)
        if number > 0:
            grad_gathered = gather_chips(grad_low, 2)

        (own_up_gate, own_down), (other_up_gate, other_down) = expert_grads
        grad_up_gate = own_up_gate + swap(other_up_gate)
        grad_down = own_down + swap(other_down)
        d_up_gate = spread_experts(
            grad_up_gate.reshape(width, MODEL_WIDTH // width, 2 * ff), place, width
        ).astype(jnp.float32)
        d_down = spread_experts(
            grad_down.reshape(ff, width, MODEL_WIDTH // width).transpose(1, 0, 2), place, width
        ).astype(jnp.float32)
        d_out = offload_scatter(grad_wout).astype(jnp.float32)
        gain_grads = jnp.concatenate([grad_g_attn, grad_g_ffn, grad_gq, grad_gk])
        outs.insert(
            0, (d_out, d_up_gate[:, :, :ff], d_up_gate[:, :, ff:], d_down)
        )
        small_grads.insert(0, (grad_router, gain_grads.reshape(devices, -1)))
        if number > 0:
            d_qkv = offload_scatter(grad_wqkv)
    d_out, d_gate, d_up, d_down = [jnp.stack([entry[i] for entry in outs]) for i in range(4)]
    own_gains = jnp.concatenate([gain_grad for _, gain_grad in small_grads], axis=1)
    own_gains = jnp.pad(own_gains, ((0, 0), (0, gain_columns * short - gains.size)))
    side = jnp.concatenate(
        [router_grad for router_grad, _ in small_grads] + [own_gains.reshape(MODEL_WIDTH, -1)],
        axis=1,
    ).astype(jnp.bfloat16)
    side = jnp.pad(side, ((0, 0), (0, -side.shape[1] % 128)))
    qkv_columns = grad_wqkv.shape[1]
    last = scatter_chips(jnp.concatenate([grad_wqkv, side], axis=1), 4).astype(jnp.float32)
    d_qkv = d_qkv.astype(jnp.float32)
    first_qkv = last[:, :qkv_columns]
    side = last[:, qkv_columns:]
    d_qkv = jnp.stack([first_qkv, d_qkv])
    mine = lax.dynamic_slice_in_dim(d_qkv, core * short, short, 1)
    got = swap(lax.dynamic_slice_in_dim(d_qkv, (1 - core) * short, short, 1))
    small = lax.dynamic_slice_in_dim(side, core * short, short, 0) + swap(
        lax.dynamic_slice_in_dim(side, (1 - core) * short, short, 0)
    )
    d_router = jnp.stack(
        [small[:, number * EXPERTS : (number + 1) * EXPERTS] for number in range(DECODER_LAYERS)]
    )
    d_gains = small[:, router_columns : router_columns + gain_columns].reshape(-1)[: gains.size]
    d_gains = d_gains.reshape(gains.shape)
    q_width = half_heads * HEAD_SIZE
    side = (DECODER_LAYERS, short, half_heads, 1, HEAD_SIZE)
    d_query = by_core(
        core, mine[..., :q_width].reshape(side), got[..., :q_width].reshape(side), 3
    ).reshape(w_query.shape)
    cut = q_width + pair_width
    d_key = by_core(core, mine[..., q_width:cut], got[..., q_width:cut], 2)
    d_value = by_core(core, mine[..., cut:], got[..., cut:], 2)
    return (
        result,
        grad_low,
        d_gains,
        d_query,
        d_key,
        d_value,
        d_out,
        d_router,
        d_gate,
        d_up,
        d_down,
    )


def by_chip(mesh):
    grid = Mesh(
        mesh.devices.reshape(mesh.shape["fsdp"], mesh.shape["expert"] // 2, 2),
        ("fsdp", "line", "core"),
    )
    experts = ("line", "core")
    return jax.shard_map(
        chip_shards,
        mesh=grid,
        in_specs=(
            P(EVERY, None),
            P(EVERY, None),
            P(EVERY, None),
            P(None, EVERY, None),
            P(None, EVERY),
            P(None, EVERY, None),
            P(None, EVERY, None),
            P(None, EVERY, None),
            P(None, EVERY, None),
            P(None, EVERY, None),
            P(None, experts, "fsdp", None),
            P(None, experts, "fsdp", None),
            P(None, experts, None, "fsdp"),
        ),
        out_specs=(
            P(EVERY, None),
            P(EVERY, None),
            P(None, EVERY),
            P(None, EVERY, None),
            P(None, EVERY, None),
            P(None, EVERY, None),
            P(None, EVERY, None),
            P(None, EVERY, None),
            P(None, experts, "fsdp", None),
            P(None, experts, "fsdp", None),
            P(None, experts, None, "fsdp"),
        ),
        check_vma=False,
    )


def solution(mesh):
    width = mesh.shape["fsdp"]
    peers = mesh.shape["expert"]
    if width == 4 and peers % 2 == 0 and peers * width == EXPERTS:
        return by_chip(mesh)
    return general(mesh)
```

```python
from functools import partial
import math

import jax
import jax.numpy as jnp
from jax import lax
from jax.experimental import pallas as pl
from jax.experimental.pallas import tpu as pltpu
from jax.sharding import Mesh
from jax.sharding import PartitionSpec as P

MODEL_WIDTH = 2048
QUERY_HEADS = 32
KEY_VALUE_HEADS = 4
HEAD_SIZE = 128
TOP = 8
EXPERTS = 32
DECODER_LAYERS = 2
CAP = 48


EPSILON = 1e-06
ROPE_BASE = 1000000.0


def norm_rows(operand, gain_vec):
    return (
        operand
        * lax.rsqrt(jnp.mean(operand * operand, axis=-1, keepdims=True) + EPSILON)
        * gain_vec
    )


def softmax_last(operand):
    shifted = operand - jnp.max(operand, axis=-1, keepdims=True)
    weights = jnp.exp(shifted)
    return weights / jnp.sum(weights, axis=-1, keepdims=True)


def rotate(operand, cosine, sine):
    half_size = operand.shape[-1] // 2
    front_half = operand[..., :half_size]
    back_half = operand[..., half_size:]
    return jnp.concatenate(
        [front_half * cosine - back_half * sine, back_half * cosine + front_half * sine], axis=-1
    )


def head_piece(query_pre, prerotation_key, g_query, g_key, cosine, sine):
    return (
        rotate(norm_rows(query_pre, g_query), cosine, sine),
        rotate(norm_rows(prerotation_key, g_key), cosine, sine),
    )


def geometry(lengths, local_rows):
    seq_ends = jnp.cumsum(lengths[0])
    seq_starts = seq_ends - lengths[0]
    offsets = jnp.arange(local_rows, dtype=jnp.int32)
    segment = jnp.sum((offsets[:, None] >= seq_ends[None, :]).astype(jnp.int32), axis=1)
    member = segment[:, None] == jnp.arange(seq_ends.shape[0], dtype=jnp.int32)[None, :]
    begins = jnp.sum(jnp.where(member, seq_starts[None, :], 0), axis=1)
    position = (offsets - begins).astype(jnp.float32)
    inverse = jnp.exp(
        -(2.0 * jnp.arange(HEAD_SIZE // 2, dtype=jnp.float32) / HEAD_SIZE) * math.log(ROPE_BASE)
    )
    angles = position[:, None] * inverse[None, :]
    allowed = (segment[:, None] == segment[None, :]) & (offsets[None, :] <= offsets[:, None])
    return (jnp.cos(angles)[:, None, :], jnp.sin(angles)[:, None, :], allowed)


def slot_table(route_rows):
    flat_routes = route_rows.reshape(-1)
    matches = (flat_routes[:, None] == jnp.arange(EXPERTS, dtype=jnp.int32)[None, :]).astype(
        jnp.int32
    )
    rank_in = jnp.sum((jnp.cumsum(matches, axis=0) - 1) * matches, axis=1)
    return flat_routes * CAP + rank_in


def split_gains(gain_vec):
    return (
        gain_vec[:MODEL_WIDTH],
        gain_vec[MODEL_WIDTH : 2 * MODEL_WIDTH],
        gain_vec[2 * MODEL_WIDTH : 2 * MODEL_WIDTH + HEAD_SIZE],
        gain_vec[2 * MODEL_WIDTH + HEAD_SIZE :],
    )


def score_block(query_copy, key_b, allowed):
    local_rows = query_copy.shape[0]
    grouped_rows = query_copy.reshape(
        local_rows, KEY_VALUE_HEADS, QUERY_HEADS // KEY_VALUE_HEADS, HEAD_SIZE
    )
    raw_scores = jnp.einsum(
        "tgjd,sgd->gjts", grouped_rows, key_b, preferred_element_type=jnp.float32
    ) * (1.0 / math.sqrt(HEAD_SIZE))
    return jnp.where(allowed[None, None], raw_scores, -1e30)


def layer_forward(state, dense, experts, route_rows, cosine, sine, allowed, peers):
    w_query, key_weight, value_weight, w_out, w_router, gain_raw = dense
    w_gate, w_up, w_down = experts
    local_rows = state.shape[0]
    experts_here = w_gate.shape[0]
    g_attn, g_ffn, g_query, g_key = split_gains(gain_raw.astype(jnp.float32))
    normalized_input = norm_rows(state, g_attn).astype(jnp.bfloat16)
    query_pre = jnp.dot(normalized_input, w_query, preferred_element_type=jnp.float32).reshape(
        local_rows, QUERY_HEADS, HEAD_SIZE
    )
    prerotation_key = jnp.dot(
        normalized_input, key_weight, preferred_element_type=jnp.float32
    ).reshape(local_rows, KEY_VALUE_HEADS, HEAD_SIZE)
    value_b = (
        jnp.dot(normalized_input, value_weight, preferred_element_type=jnp.float32)
        .astype(jnp.bfloat16)
        .reshape(local_rows, KEY_VALUE_HEADS, HEAD_SIZE)
    )
    query_f, key_f = head_piece(query_pre, prerotation_key, g_query, g_key, cosine, sine)
    query_copy = query_f.astype(jnp.bfloat16)
    key_b = key_f.astype(jnp.bfloat16)
    scores = score_block(query_copy, key_b, allowed)
    peaks = jnp.max(scores, axis=-1, keepdims=True)
    expos = jnp.exp(scores - peaks)
    totals = jnp.sum(expos, axis=-1, keepdims=True)
    log_total = peaks + jnp.log(totals)
    probs_b = (expos / totals).astype(jnp.bfloat16)
    attended = jnp.einsum("gjts,sgd->tgjd", probs_b, value_b, preferred_element_type=jnp.float32)
    attended = attended.reshape(local_rows, QUERY_HEADS * HEAD_SIZE).astype(jnp.bfloat16)
    middle = state + jnp.dot(attended, w_out, preferred_element_type=jnp.float32)
    mixer_in = norm_rows(middle, g_ffn).astype(jnp.bfloat16)
    logits = jnp.dot(mixer_in, w_router, preferred_element_type=jnp.float32)
    gates = softmax_last(jnp.take_along_axis(logits, route_rows, axis=1))
    slot_ids = slot_table(route_rows)
    outgoing = (
        jnp.zeros((EXPERTS * CAP, MODEL_WIDTH), jnp.bfloat16)
        .at[slot_ids]
        .set(jnp.repeat(mixer_in, TOP, axis=0))
    )
    incoming = lax.all_to_all(
        outgoing.reshape(peers, experts_here * CAP, MODEL_WIDTH),
        "expert",
        split_axis=0,
        concat_axis=0,
        tiled=True,
    )
    incoming = incoming.reshape(peers, experts_here, CAP, MODEL_WIDTH)
    gate_pre = jnp.einsum("secd,edf->secf", incoming, w_gate, preferred_element_type=jnp.float32)
    up_pre = jnp.einsum("secd,edf->secf", incoming, w_up, preferred_element_type=jnp.float32)
    hidden_b = (jax.nn.silu(gate_pre) * up_pre).astype(jnp.bfloat16)
    produced = jnp.einsum(
        "secf,efd->secd", hidden_b, w_down, preferred_element_type=jnp.float32
    ).astype(jnp.bfloat16)
    returned = lax.all_to_all(
        produced.reshape(peers, experts_here * CAP, MODEL_WIDTH),
        "expert",
        split_axis=0,
        concat_axis=0,
        tiled=True,
    )
    picked = returned.reshape(EXPERTS * CAP, MODEL_WIDTH)[slot_ids].reshape(
        local_rows, TOP, MODEL_WIDTH
    )
    new_state = middle + jnp.sum(gates[:, :, None] * picked.astype(jnp.float32), axis=1)
    memo = (
        state,
        normalized_input,
        query_pre,
        prerotation_key,
        query_copy,
        key_b,
        value_b,
        log_total,
        attended,
        middle,
        mixer_in,
        gates,
        slot_ids,
        picked,
        incoming,
        gate_pre,
        up_pre,
        hidden_b,
    )
    return (new_state, memo)


def layer_backward(grad_state, memo, dense, experts, route_rows, cosine, sine, allowed, peers):
    (
        state,
        normalized_input,
        query_pre,
        prerotation_key,
        query_copy,
        key_b,
        value_b,
        log_total,
        attended,
        middle,
        mixer_in,
        gates,
        slot_ids,
        picked,
        incoming,
        gate_pre,
        up_pre,
        hidden_b,
    ) = memo
    w_query, key_weight, value_weight, w_out, w_router, gain_raw = dense
    w_gate, w_up, w_down = experts
    local_rows = state.shape[0]
    experts_here = w_gate.shape[0]
    query_group_size = QUERY_HEADS // KEY_VALUE_HEADS
    scale = 1.0 / math.sqrt(HEAD_SIZE)
    g_attn, g_ffn, g_query, g_key = split_gains(gain_raw.astype(jnp.float32))
    grad_gates = jnp.sum(picked.astype(jnp.float32) * grad_state[:, None, :], axis=2)
    grad_chosen = gates * (grad_gates - jnp.sum(gates * grad_gates, axis=1, keepdims=True))
    choose = (route_rows[:, :, None] == jnp.arange(EXPERTS, dtype=jnp.int32)[None, None, :]).astype(
        jnp.float32
    )
    grad_logits = jnp.sum(choose * grad_chosen[:, :, None], axis=1).astype(jnp.bfloat16)
    grad_router = jnp.dot(mixer_in.T, grad_logits, preferred_element_type=jnp.float32)
    grad_mixer = jnp.dot(grad_logits, w_router.T, preferred_element_type=jnp.float32)
    grad_picked = (
        (gates[:, :, None] * grad_state[:, None, :])
        .astype(jnp.bfloat16)
        .reshape(local_rows * TOP, MODEL_WIDTH)
    )
    outgoing = jnp.zeros((EXPERTS * CAP, MODEL_WIDTH), jnp.bfloat16).at[slot_ids].set(grad_picked)
    grad_produced = lax.all_to_all(
        outgoing.reshape(peers, experts_here * CAP, MODEL_WIDTH),
        "expert",
        split_axis=0,
        concat_axis=0,
        tiled=True,
    )
    grad_produced = grad_produced.reshape(peers, experts_here, CAP, MODEL_WIDTH)
    grad_down = jnp.einsum(
        "secf,secd->efd", hidden_b, grad_produced, preferred_element_type=jnp.float32
    )
    grad_hidden = jnp.einsum(
        "secd,efd->secf", grad_produced, w_down, preferred_element_type=jnp.float32
    )
    sigmoid_gate = jax.nn.sigmoid(gate_pre)
    grad_gate_pre = (
        grad_hidden * up_pre * sigmoid_gate * (1.0 + gate_pre * (1.0 - sigmoid_gate))
    ).astype(jnp.bfloat16)
    grad_up_pre = (grad_hidden * gate_pre * sigmoid_gate).astype(jnp.bfloat16)
    grad_wgate = jnp.einsum(
        "secd,secf->edf", incoming, grad_gate_pre, preferred_element_type=jnp.float32
    )
    grad_wup = jnp.einsum(
        "secd,secf->edf", incoming, grad_up_pre, preferred_element_type=jnp.float32
    )
    grad_incoming = jnp.einsum(
        "secf,edf->secd", grad_gate_pre, w_gate, preferred_element_type=jnp.float32
    )
    grad_incoming = grad_incoming + jnp.einsum(
        "secf,edf->secd", grad_up_pre, w_up, preferred_element_type=jnp.float32
    )
    grad_incoming = grad_incoming.astype(jnp.bfloat16).reshape(
        peers, experts_here * CAP, MODEL_WIDTH
    )
    grad_returned = lax.all_to_all(
        grad_incoming, "expert", split_axis=0, concat_axis=0, tiled=True
    ).reshape(EXPERTS * CAP, MODEL_WIDTH)
    grad_mixer = grad_mixer + jnp.sum(
        grad_returned[slot_ids].reshape(local_rows, TOP, MODEL_WIDTH).astype(jnp.float32), axis=1
    )
    unused_mid, norm_back = jax.vjp(norm_rows, middle, g_ffn)
    grad_mid_part, grad_g_ffn = norm_back(grad_mixer)
    grad_middle = grad_state + grad_mid_part
    grad_middle_low = grad_middle.astype(jnp.bfloat16)
    grad_wout = jnp.dot(attended.T, grad_middle_low, preferred_element_type=jnp.float32)
    attended_gradient = jnp.dot(
        grad_middle_low, w_out.T, preferred_element_type=jnp.float32
    ).astype(jnp.bfloat16)
    attended_gradient = attended_gradient.reshape(
        local_rows, KEY_VALUE_HEADS, query_group_size, HEAD_SIZE
    )
    scores = score_block(query_copy, key_b, allowed)
    probs = jnp.exp(scores - log_total)
    probs_b = probs.astype(jnp.bfloat16)
    grad_probs = jnp.einsum(
        "tgjd,sgd->gjts", attended_gradient, value_b, preferred_element_type=jnp.float32
    )
    value_gradient = jnp.einsum(
        "gjts,tgjd->sgd", probs_b, attended_gradient, preferred_element_type=jnp.float32
    )
    value_gradient_copy = value_gradient.astype(jnp.bfloat16).reshape(
        local_rows, KEY_VALUE_HEADS * HEAD_SIZE
    )
    grad_scores = (
        probs * (grad_probs - jnp.sum(grad_probs * probs, axis=-1, keepdims=True))
    ).astype(jnp.bfloat16)
    grad_query = (
        jnp.einsum("gjts,sgd->tgjd", grad_scores, key_b, preferred_element_type=jnp.float32) * scale
    )
    query_grouped = query_copy.reshape(local_rows, KEY_VALUE_HEADS, query_group_size, HEAD_SIZE)
    grad_key = (
        jnp.einsum("gjts,tgjd->sgd", grad_scores, query_grouped, preferred_element_type=jnp.float32)
        * scale
    )
    unused_heads, head_back = jax.vjp(
        partial(head_piece, cosine=cosine, sine=sine), query_pre, prerotation_key, g_query, g_key
    )
    grad_qpre, prekey_gradient, grad_gq, grad_gk = head_back(
        (grad_query.reshape(local_rows, QUERY_HEADS, HEAD_SIZE), grad_key)
    )
    grad_qpre_b = grad_qpre.astype(jnp.bfloat16).reshape(local_rows, QUERY_HEADS * HEAD_SIZE)
    prekey_gradient_copy = prekey_gradient.astype(jnp.bfloat16).reshape(
        local_rows, KEY_VALUE_HEADS * HEAD_SIZE
    )
    grad_wquery = jnp.dot(normalized_input.T, grad_qpre_b, preferred_element_type=jnp.float32)
    grad_wkey = jnp.dot(
        normalized_input.T, prekey_gradient_copy, preferred_element_type=jnp.float32
    )
    grad_wvalue = jnp.dot(
        normalized_input.T, value_gradient_copy, preferred_element_type=jnp.float32
    )
    grad_normed = jnp.dot(grad_qpre_b, w_query.T, preferred_element_type=jnp.float32)
    grad_normed = grad_normed + jnp.dot(
        prekey_gradient_copy, key_weight.T, preferred_element_type=jnp.float32
    )
    grad_normed = grad_normed + jnp.dot(
        value_gradient_copy, value_weight.T, preferred_element_type=jnp.float32
    )
    unused_state, norm_front = jax.vjp(norm_rows, state, g_attn)
    grad_in_part, grad_g_attn = norm_front(grad_normed)
    grad_input = grad_middle + grad_in_part
    grad_gains = jnp.concatenate([grad_g_attn, grad_g_ffn, grad_gq, grad_gk])
    dense_grads = (grad_wquery, grad_wkey, grad_wvalue, grad_wout, grad_router, grad_gains)
    expert_grads = (grad_wgate, grad_wup, grad_down)
    return (grad_input, dense_grads, expert_grads)


def shards(
    tokens,
    cotangent,
    lengths,
    routes,
    gains,
    w_query,
    key_weight,
    value_weight,
    w_out,
    w_router,
    w_gate,
    w_up,
    w_down,
):
    local_rows = tokens.shape[0]
    peers = lax.axis_size("expert")
    cosine, sine, allowed = geometry(lengths, local_rows)
    state = tokens.astype(jnp.float32)
    memos = []
    for number in range(DECODER_LAYERS):
        dense = (
            lax.all_gather(w_query[number], ("fsdp", "expert"), axis=0, tiled=True),
            lax.all_gather(key_weight[number], ("fsdp", "expert"), axis=0, tiled=True),
            lax.all_gather(value_weight[number], ("fsdp", "expert"), axis=0, tiled=True),
            lax.all_gather(w_out[number], ("fsdp", "expert"), axis=0, tiled=True),
            lax.all_gather(w_router[number], ("fsdp", "expert"), axis=0, tiled=True),
            lax.all_gather(gains[number], ("fsdp", "expert"), axis=0, tiled=True),
        )
        experts = (
            lax.all_gather(w_gate[number], "fsdp", axis=1, tiled=True),
            lax.all_gather(w_up[number], "fsdp", axis=1, tiled=True),
            lax.all_gather(w_down[number], "fsdp", axis=2, tiled=True),
        )
        state, memo = layer_forward(
            state, dense, experts, routes[number], cosine, sine, allowed, peers
        )
        memos.append(memo)
    result = state.astype(jnp.bfloat16)
    grad_state = cotangent.astype(jnp.float32)
    dense_list = []
    expert_list = []
    for number in reversed(range(DECODER_LAYERS)):
        dense = (
            lax.all_gather(w_query[number], ("fsdp", "expert"), axis=0, tiled=True),
            lax.all_gather(key_weight[number], ("fsdp", "expert"), axis=0, tiled=True),
            lax.all_gather(value_weight[number], ("fsdp", "expert"), axis=0, tiled=True),
            lax.all_gather(w_out[number], ("fsdp", "expert"), axis=0, tiled=True),
            lax.all_gather(w_router[number], ("fsdp", "expert"), axis=0, tiled=True),
            lax.all_gather(gains[number], ("fsdp", "expert"), axis=0, tiled=True),
        )
        experts = (
            lax.all_gather(w_gate[number], "fsdp", axis=1, tiled=True),
            lax.all_gather(w_up[number], "fsdp", axis=1, tiled=True),
            lax.all_gather(w_down[number], "fsdp", axis=2, tiled=True),
        )
        grad_state, dense_grads, expert_grads = layer_backward(
            grad_state, memos[number], dense, experts, routes[number], cosine, sine, allowed, peers
        )
        dense_shards = (
            lax.psum_scatter(dense_grads[0], ("fsdp", "expert"), scatter_dimension=0, tiled=True),
            lax.psum_scatter(dense_grads[1], ("fsdp", "expert"), scatter_dimension=0, tiled=True),
            lax.psum_scatter(dense_grads[2], ("fsdp", "expert"), scatter_dimension=0, tiled=True),
            lax.psum_scatter(dense_grads[3], ("fsdp", "expert"), scatter_dimension=0, tiled=True),
            lax.psum_scatter(dense_grads[4], ("fsdp", "expert"), scatter_dimension=0, tiled=True),
            lax.psum_scatter(dense_grads[5], ("fsdp", "expert"), scatter_dimension=0, tiled=True),
        )
        expert_shards = (
            lax.psum_scatter(
                expert_grads[0].astype(jnp.bfloat16), "fsdp", scatter_dimension=1, tiled=True
            ).astype(jnp.float32),
            lax.psum_scatter(
                expert_grads[1].astype(jnp.bfloat16), "fsdp", scatter_dimension=1, tiled=True
            ).astype(jnp.float32),
            lax.psum_scatter(
                expert_grads[2].astype(jnp.bfloat16), "fsdp", scatter_dimension=2, tiled=True
            ).astype(jnp.float32),
        )
        dense_list.insert(0, dense_shards)
        expert_list.insert(0, expert_shards)
    d_gains = jnp.stack([entry[5] for entry in dense_list])
    d_query = jnp.stack([entry[0] for entry in dense_list])
    d_key = jnp.stack([entry[1] for entry in dense_list])
    d_value = jnp.stack([entry[2] for entry in dense_list])
    d_out = jnp.stack([entry[3] for entry in dense_list])
    d_router = jnp.stack([entry[4] for entry in dense_list])
    d_gate = jnp.stack([entry[0] for entry in expert_list])
    d_up = jnp.stack([entry[1] for entry in expert_list])
    d_down = jnp.stack([entry[2] for entry in expert_list])
    return (
        result,
        grad_state.astype(jnp.bfloat16),
        d_gains,
        d_query,
        d_key,
        d_value,
        d_out,
        d_router,
        d_gate,
        d_up,
        d_down,
    )


def general(mesh):
    return jax.shard_map(
        shards,
        mesh=mesh,
        in_specs=(
            P(("fsdp", "expert"), None),
            P(("fsdp", "expert"), None),
            P(("fsdp", "expert"), None),
            P(None, ("fsdp", "expert"), None),
            P(None, ("fsdp", "expert")),
            P(None, ("fsdp", "expert"), None),
            P(None, ("fsdp", "expert"), None),
            P(None, ("fsdp", "expert"), None),
            P(None, ("fsdp", "expert"), None),
            P(None, ("fsdp", "expert"), None),
            P(None, "expert", "fsdp", None),
            P(None, "expert", "fsdp", None),
            P(None, "expert", None, "fsdp"),
        ),
        out_specs=(
            P(("fsdp", "expert"), None),
            P(("fsdp", "expert"), None),
            P(None, ("fsdp", "expert")),
            P(None, ("fsdp", "expert"), None),
            P(None, ("fsdp", "expert"), None),
            P(None, ("fsdp", "expert"), None),
            P(None, ("fsdp", "expert"), None),
            P(None, ("fsdp", "expert"), None),
            P(None, "expert", "fsdp", None),
            P(None, "expert", "fsdp", None),
            P(None, "expert", None, "fsdp"),
        ),
        check_vma=False,
    )


FSDP, LINE, CORE = "fsdp", "line", "core"
CHIPS = (FSDP, LINE)
EVERY = (FSDP, LINE, CORE)
X, Y, ABOVE, BELOW = range(4)
GATE_COLUMNS = 128
PICK, SPREAD = "bst,btd->bsd", "bst,bsd->btd"


def swap(operand):
    return lax.ppermute(operand, CORE, [(0, 1), (1, 0)])


def by_core(core, mine, other, axis):
    return jnp.where(
        core == 0,
        jnp.concatenate([mine, other], axis=axis),
        jnp.concatenate([other, mine], axis=axis),
    )


def turned(operand):
    half_rows = operand.shape[0] // 2
    return jnp.concatenate([operand[half_rows:], operand[:half_rows]], axis=0)


def offload_gather(operand):
    return lax.all_gather(operand, CHIPS, axis=0, tiled=True)


PAIR = 4
ROW_UNITS = 8


ALL_CHIPS, PLANE, LINE_ONLY = range(3)


def routes_of_shards(grid, depth):
    depth = 1 if grid == PLANE else depth
    offsets = [s * k for k in range(1, depth) for s in (-1, 1)]

    def source(offset):
        return BELOW if offset < 0 else ABOVE

    def onward(offset):
        return ABOVE if offset < 0 else BELOW

    def further(offset):
        return offset - 1 if offset < 0 else offset + 1

    def line_hops(bits, first, last, offset):
        if depth == 1:
            return []
        if offset == 0:
            return [
                (ABOVE, first, last, (bits, -1, first, last, BELOW)),
                (BELOW, first, last, (bits, 1, first, last, ABOVE)),
            ]
        if abs(further(offset)) >= depth:
            return []
        return [(onward(offset), first, last, (bits, further(offset), first, last, source(offset)))]

    if grid == LINE_ONLY:
        return [(None, line_hops(0, 0, 8, 0))] + [
            ((0, offset, 0, 8, source(offset)), line_hops(0, 0, 8, offset)) for offset in offsets
        ]
    plan = []
    own = [(X, 0, 8, (1, 0, 0, 8, X)), (Y, 0, 8, (2, 0, 0, 8, Y))]
    plan.append((None, own + line_hops(0, 0, 8, 0)))
    plan.append(
        ((1, 0, 0, 8, X), [(Y, 3, 7, (3, 0, 3, 7, Y))] + line_hops(1, 6, 8, 0))
    )
    plan.append(
        (
            (2, 0, 0, 8, Y),
            [(X, 0, 3, (3, 0, 0, 3, X)), (X, 7, 8, (3, 0, 7, 8, X))]
            + line_hops(2, 6, 8, 0),
        )
    )

    def spread(offset):
        return (
            (0, offset, 0, 8, source(offset)),
            line_hops(0, 0, 8, offset)
            + [(X, 0, 6, (1, offset, 0, 6, X)), (Y, 0, 6, (2, offset, 0, 6, Y))],
        )

    def crossed(offset):
        return [
            ((1, offset, 0, 6, X), [(Y, 3, 6, (3, offset, 3, 6, Y))]),
            ((2, offset, 0, 6, Y), [(X, 0, 3, (3, offset, 0, 3, X))]),
        ]

    def lined(offset):
        return [
            ((bits, offset, 6, 8, source(offset)), line_hops(bits, 6, 8, offset))
            for bits in (1, 2, 3)
        ]

    def last(offset):
        return [((3, offset, 3, 6, Y), []), ((3, offset, 0, 3, X), [])]

    steps = [(-k, k) for k in range(1, depth)]
    plan += [spread(o) for pair in steps[:1] for o in pair]
    plan += [
        ((3, 0, 3, 7, Y), []),
        ((3, 0, 0, 3, X), []),
        ((3, 0, 7, 8, X), line_hops(3, 6, 8, 0)),
    ]
    for number, pair in enumerate(steps):
        for offset in pair:
            plan += crossed(offset)
        if number + 1 < len(steps):
            plan += [spread(o) for o in steps[number + 1]]
        for offset in pair:
            plan += lined(offset)
        for offset in pair:
            plan += last(offset)
    return plan


class Place:
    def __init__(self, grid, depth):
        self.grid = grid
        self.depth = depth
        self.pair = lax.axis_index(FSDP)
        self.line = lax.axis_index(LINE)
        self.core = lax.axis_index(CORE)
        x = lax.rem(self.pair, 2)
        y = lax.div(self.pair, 2)
        self.pairs = [
            self.pair,
            self.pair + 1 - 2 * x,
            self.pair + 2 - 4 * y,
            PAIR - 1 - self.pair,
        ]

    def shard(self, bits, offset):
        if self.grid == PLANE:
            return self.pairs[bits]
        if self.grid == LINE_ONLY:
            return self.line + offset
        return self.pairs[bits] * self.depth + self.line + offset

    def device(self, neighbour):
        if neighbour == X:
            return (self.pairs[1], self.line, self.core)
        if neighbour == Y:
            return (self.pairs[2], self.line, self.core)
        step = 1 if neighbour == ABOVE else -1
        return (self.pair, self.line + step, self.core)

    def holds(self, offset, neighbour=None):
        low, high = min(offset, 0), max(offset, 0)
        if neighbour == ABOVE:
            high = max(high, 1)
        if neighbour == BELOW:
            low = min(low, -1)
        tests = []
        if low < 0:
            tests.append(self.line >= -low)
        if high > 0:
            tests.append(self.line < self.depth - high)
        if not tests:
            return None
        return tests[0] if len(tests) == 1 else jnp.logical_and(tests[0], tests[1])

    def meet(self):
        barrier = pltpu.get_barrier_semaphore()
        neighbours = (() if self.grid == LINE_ONLY else (X, Y)) + (
            () if self.grid == PLANE else (ABOVE, BELOW)
        )
        for neighbour in neighbours:

            def greet(neighbour=neighbour):
                pl.semaphore_signal(
                    barrier,
                    inc=1,
                    device_id=self.device(neighbour),
                    device_id_type=pl.DeviceIdType.MESH,
                )

            when(self.holds(0, neighbour), greet)
        ends = 0
        if self.grid != PLANE:
            ends = (self.line == 0).astype(jnp.int32) + (self.line == self.depth - 1).astype(
                jnp.int32
            )
        pl.semaphore_wait(barrier, len(neighbours) - ends)


def when(test, action):
    if test is None:
        action()
    else:
        pl.when(test)(action)


def gather_kernel(grid, depth, x_ref, out_ref, own_sem, send_sems, recv_sems):
    plan = routes_of_shards(grid, depth)
    number_of = {item: i for i, (item, _) in enumerate(plan)}
    unit = x_ref.shape[0] // ROW_UNITS
    here = Place(grid, depth)
    own = pltpu.make_async_copy(x_ref, out_ref.at[here.shard(0, 0)], own_sem)
    own.start()
    here.meet()
    sent = []
    for item, hops in plan:
        bits, offset = (0, 0) if item is None else item[:2]

        def step(item=item, hops=hops, bits=bits, offset=offset, site=len(sent)):
            if item is not None:
                piece = out_ref.at[
                    here.shard(bits, offset), pl.ds(item[2] * unit, (item[3] - item[2]) * unit)
                ]
                pltpu.make_async_remote_copy(
                    src_ref=piece,
                    dst_ref=piece,
                    send_sem=send_sems.at[0],
                    recv_sem=recv_sems.at[number_of[item]],
                    device_id=here.device(X),
                    device_id_type=pl.DeviceIdType.MESH,
                ).wait_recv()
            for hop, (neighbour, first, last, there) in enumerate(hops):
                when(
                    here.holds(0, neighbour) if neighbour in (ABOVE, BELOW) else None,
                    lambda n=neighbour, f=first, l=last, t=there, s=site + hop: passing(
                        bits, offset, n, f, l, t, s, item is None
                    ).start(),
                )

        def passing(bits, offset, neighbour, first, last, there, site, own_piece):
            rows = pl.ds(first * unit, (last - first) * unit)
            target = out_ref.at[here.shard(bits, offset), rows]
            return pltpu.make_async_remote_copy(
                src_ref=x_ref.at[rows] if own_piece else target,
                dst_ref=target,
                send_sem=send_sems.at[site],
                recv_sem=recv_sems.at[number_of[there]],
                device_id=here.device(neighbour),
                device_id_type=pl.DeviceIdType.MESH,
            )

        when(None if item is None else here.holds(offset), step)
        for neighbour, first, last, there in hops:
            sent.append((bits, offset, neighbour, first, last, there, len(sent), item is None))
    for bits, offset, neighbour, first, last, there, site, own_piece in sent:

        def finish(a=(bits, offset, neighbour, first, last, there, site, own_piece)):
            passing(*a).wait_send()

        when(here.holds(offset, neighbour), finish)
    own.wait()


def count_plan(grid, depth):
    plan = routes_of_shards(grid, depth)
    return len(plan), sum(len(hops) for _, hops in plan)


def chips_in(grid, depth):
    return {ALL_CHIPS: PAIR * depth, PLANE: PAIR, LINE_ONLY: depth}[grid]


def gather_chips(operand, collective_id, grid=ALL_CHIPS):
    depth = lax.axis_size(LINE)
    items, hops = count_plan(grid, depth)
    chips = chips_in(grid, depth)
    rows, columns = operand.shape
    return pl.pallas_call(
        partial(gather_kernel, grid, depth),
        out_shape=jax.ShapeDtypeStruct((chips, rows, columns), operand.dtype),
        in_specs=[pl.BlockSpec(memory_space=pl.ANY)],
        out_specs=pl.BlockSpec(memory_space=pl.ANY),
        scratch_shapes=[
            pltpu.SemaphoreType.DMA,
            pltpu.SemaphoreType.DMA((hops,)),
            pltpu.SemaphoreType.DMA((items,)),
        ],
        compiler_params=pltpu.CompilerParams(collective_id=collective_id, has_side_effects=True),
        cost_estimate=pl.CostEstimate(
            flops=0, bytes_accessed=66 * chips * rows * columns, transcendentals=0
        ),
    )(operand).reshape(chips * rows, columns)


def scatter_kernel(grid, depth, x_ref, out_ref, sums, landed, own_sem, send_sems, recv_sems):
    plan = routes_of_shards(grid, depth)
    number_of = {item: i for i, (item, _) in enumerate(plan)}
    unit = x_ref.shape[1] // ROW_UNITS
    here = Place(grid, depth)
    own = pltpu.make_async_copy(x_ref, sums, own_sem)
    own.start()
    here.meet()
    own.wait()
    sites = {}
    start = 0
    for item, hops in plan:
        for neighbour, first, last, there in hops:
            sites[there] = (number_of[there] - 1, start)
            start += (last - first) * unit

    def total(shard, first, last, base):
        @pl.loop(0, (last - first) * unit // 16)
        def _(i):
            rows = pl.ds(first * unit + i * 16, 16)
            value = sums[shard, rows].astype(jnp.float32)
            value = value + landed[pl.ds(base + i * 16, 16)].astype(jnp.float32)
            sums[shard, rows] = value.astype(sums.dtype)

    def sending(item):
        bits, offset, first, last, neighbour = item
        sem, base = sites[item]
        size = (last - first) * unit
        return pltpu.make_async_remote_copy(
            src_ref=sums.at[here.shard(bits, offset), pl.ds(first * unit, size)],
            dst_ref=landed.at[pl.ds(base, size)],
            send_sem=send_sems.at[number_of[item]],
            recv_sem=recv_sems.at[sem],
            device_id=here.device(neighbour),
            device_id_type=pl.DeviceIdType.MESH,
        )

    for item, hops in reversed(plan):
        bits, offset = (0, 0) if item is None else item[:2]

        def step(item=item, hops=hops, bits=bits, offset=offset):
            for neighbour, first, last, there in hops:

                def take(first=first, last=last, there=there):
                    sem, base = sites[there]
                    size = (last - first) * unit
                    pltpu.make_async_remote_copy(
                        src_ref=landed.at[pl.ds(base, size)],
                        dst_ref=landed.at[pl.ds(base, size)],
                        send_sem=send_sems.at[0],
                        recv_sem=recv_sems.at[sem],
                        device_id=here.device(X),
                        device_id_type=pl.DeviceIdType.MESH,
                    ).wait_recv()
                    total(here.shard(bits, offset), first, last, base)

                when(
                    here.holds(0, neighbour) if neighbour in (ABOVE, BELOW) else None,
                    take,
                )
            if item is not None:
                sending(item).start()

        when(None if item is None else here.holds(offset), step)
    out_ref[...] = sums[here.shard(0, 0)]
    for item, hops in plan:
        if item is not None:
            when(here.holds(item[1]), lambda item=item: sending(item).wait_send())


def scatter_chips(operand, collective_id, grid=ALL_CHIPS):
    depth = lax.axis_size(LINE)
    chips = chips_in(grid, depth)
    items, hops = count_plan(grid, depth)
    rows, columns = operand.shape[0] // chips, operand.shape[1]
    landed = sum(
        (last - first) * rows // ROW_UNITS
        for _, row in routes_of_shards(grid, depth)
        for _, first, last, _ in row
    )
    return pl.pallas_call(
        partial(scatter_kernel, grid, depth),
        out_shape=jax.ShapeDtypeStruct((rows, columns), operand.dtype),
        in_specs=[pl.BlockSpec(memory_space=pl.ANY)],
        out_specs=pl.BlockSpec(memory_space=pltpu.VMEM),
        scratch_shapes=[
            pltpu.VMEM((chips, rows, columns), operand.dtype),
            pltpu.VMEM((landed, columns), operand.dtype),
            pltpu.SemaphoreType.DMA,
            pltpu.SemaphoreType.DMA((items,)),
            pltpu.SemaphoreType.DMA((hops,)),
        ],
        compiler_params=pltpu.CompilerParams(
            collective_id=collective_id, has_side_effects=True, vmem_limit_bytes=50 * 2**20
        ),
        cost_estimate=pl.CostEstimate(
            flops=0, bytes_accessed=66 * chips * rows * columns, transcendentals=0
        ),
    )(operand.reshape(chips, rows, columns))


def after(operand, *others):
    there = None
    for other in others:
        corner = other[(0,) * other.ndim].astype(jnp.float32)
        there = (corner == corner) if there is None else there & (corner == corner)
    return jnp.where(there, operand, jnp.zeros_like(operand))


def swap_pieces(piece_of, place, width):
    pieces = [(place, piece_of(place))]
    for step in range(1, width):
        sent = piece_of(place ^ step)
        got = lax.ppermute(sent, FSDP, [(i, i ^ step) for i in range(width)])
        pieces.append((place ^ step, got))
    return pieces


def block_scores(query_copy, key_b, allowed):
    return jnp.where(
        allowed[:, None],
        jnp.einsum("btjd,bsd->bjts", query_copy, key_b, preferred_element_type=jnp.float32)
        * (1.0 / math.sqrt(HEAD_SIZE)),
        -1e30,
    )


def by_owner(operand, width):
    rows = operand.shape[0]
    depth = lax.axis_size(LINE)
    return (
        operand.reshape(rows, width, depth, 2, -1).transpose(0, 3, 2, 1, 4).reshape(rows, -1)
    )


def by_place(operand, width):
    rows = operand.shape[0]
    depth = lax.axis_size(LINE)
    return (
        operand.reshape(rows, 2, depth, width, -1).transpose(0, 3, 2, 1, 4).reshape(rows, -1)
    )


def attention_forward(state, dense, angles):
    cosine, sine, allowed = angles
    w_qkv, w_out, normed, g_query, g_key = dense
    rows = state.shape[0]
    blocks = allowed.shape[0]
    heads = QUERY_HEADS // KEY_VALUE_HEADS
    cut = heads * HEAD_SIZE
    qkv = jnp.dot(normed, w_qkv, preferred_element_type=jnp.float32)
    query_pre = qkv[:, :cut].reshape(-1, heads, HEAD_SIZE)
    key_pre = qkv[:, cut : cut + HEAD_SIZE].reshape(-1, 1, HEAD_SIZE)
    value_b = qkv[:, cut + HEAD_SIZE :].astype(jnp.bfloat16).reshape(blocks, rows, HEAD_SIZE)
    query_f, key_f = head_piece(query_pre, key_pre, g_query, g_key, cosine, sine)
    query_b = query_f.astype(jnp.bfloat16).reshape(blocks, rows, heads, HEAD_SIZE)
    key_b = key_f.astype(jnp.bfloat16).reshape(blocks, rows, HEAD_SIZE)
    scores = block_scores(query_b, key_b, allowed)
    peaks = jnp.max(scores, axis=-1, keepdims=True)
    expos = jnp.exp(scores - peaks)
    totals = jnp.sum(expos, axis=-1, keepdims=True)
    log_total = peaks + jnp.log(totals)
    probs_b = (expos / totals).astype(jnp.bfloat16)
    attended = jnp.einsum("bjts,bsd->btjd", probs_b, value_b, preferred_element_type=jnp.float32)
    attended = attended.reshape(blocks * rows, cut).astype(jnp.bfloat16)
    partial_out = jnp.dot(attended, w_out, preferred_element_type=jnp.float32)
    middle = state + scatter_chips(partial_out.astype(jnp.bfloat16), 7, PLANE).astype(jnp.float32)
    return middle, (normed, query_pre, key_pre, query_b, key_b, value_b, log_total, attended)


def attention_backward(low, memo, dense, angles):
    cosine, sine, allowed = angles
    normed, query_pre, key_pre, query_b, key_b, value_b, log_total, attended = memo
    w_qkv, w_out, unused_normed, g_query, g_key = dense
    blocks, rows, heads, size = query_b.shape
    scale = 1.0 / math.sqrt(HEAD_SIZE)
    grad_attended = lax.dot_general(
        low, w_out, (((1,), (1,)), ((), ())), preferred_element_type=jnp.float32
    ).astype(jnp.bfloat16)
    grad_wout = lax.dot_general(
        attended, low, (((0,), (0,)), ((), ())), preferred_element_type=jnp.float32
    ).astype(jnp.bfloat16)
    grad_attended = grad_attended.reshape(query_b.shape)
    probs = jnp.exp(block_scores(query_b, key_b, allowed) - log_total)
    probs_b = probs.astype(jnp.bfloat16)
    grad_probs = jnp.einsum(
        "btjd,bsd->bjts", grad_attended, value_b, preferred_element_type=jnp.float32
    )
    grad_value = jnp.einsum(
        "bjts,btjd->bsd", probs_b, grad_attended, preferred_element_type=jnp.float32
    )
    grad_scores = (
        probs * (grad_probs - jnp.sum(grad_probs * probs, axis=-1, keepdims=True))
    ).astype(jnp.bfloat16)
    grad_query = (
        jnp.einsum("bjts,bsd->btjd", grad_scores, key_b, preferred_element_type=jnp.float32) * scale
    )
    grad_key = (
        jnp.einsum("bjts,btjd->bsd", grad_scores, query_b, preferred_element_type=jnp.float32)
        * scale
    )
    unused_heads, head_back = jax.vjp(
        partial(head_piece, cosine=cosine, sine=sine), query_pre, key_pre, g_query, g_key
    )
    grad_qpre, grad_kpre, grad_gq, grad_gk = head_back(
        (grad_query.reshape(query_pre.shape), grad_key.reshape(key_pre.shape))
    )
    grad_qkv = jnp.concatenate(
        [
            grad_qpre.astype(jnp.bfloat16).reshape(blocks * rows, heads * size),
            grad_kpre.astype(jnp.bfloat16).reshape(blocks * rows, size),
            grad_value.astype(jnp.bfloat16).reshape(blocks * rows, size),
        ],
        axis=1,
    )
    grad_wqkv = lax.dot_general(
        normed, grad_qkv, (((0,), (0,)), ((), ())), preferred_element_type=jnp.float32
    ).astype(jnp.bfloat16)
    grad_normed = lax.dot_general(
        grad_qkv, w_qkv, (((1,), (1,)), ((), ())), preferred_element_type=jnp.float32
    ).astype(jnp.bfloat16)
    return scatter_chips(grad_normed, 7, PLANE), grad_wqkv, grad_wout, grad_gq, grad_gk


def send_back(picks, pieces):
    return (
        jnp.einsum(
            SPREAD,
            jnp.concatenate(picks, axis=1),
            jnp.concatenate(pieces, axis=1),
            preferred_element_type=jnp.float32,
        )
        .astype(jnp.bfloat16)
        .reshape(-1, pieces[0].shape[2])
    )


def expert_forward(gathered, picks, row_gates, weights):
    blocks = picks[0].shape[0]
    width = gathered.shape[1]
    grouped = gathered.reshape(blocks, -1, width)
    memo = []
    pieces = []
    for pick, row_gate, (w_up_gate, w_down) in zip(picks, row_gates, weights):
        hidden_size = w_down.shape[0]
        rows = jnp.einsum(PICK, pick, grouped, preferred_element_type=jnp.float32)
        rows = rows.astype(jnp.bfloat16).reshape(-1, width)
        pre = jnp.dot(rows, w_up_gate, preferred_element_type=jnp.float32)
        gate_pre = pre[:, :hidden_size]
        up_pre = pre[:, hidden_size:]
        hidden = (jax.nn.silu(gate_pre) * up_pre).astype(jnp.bfloat16)
        produced = jnp.dot(hidden, w_down, preferred_element_type=jnp.float32)
        produced = (produced * row_gate).astype(jnp.bfloat16)
        pieces.append(produced.reshape(blocks, -1, width))
        memo.append((rows, gate_pre, up_pre, hidden))
    return send_back(picks, pieces), memo


def expert_backward(gathered, picks, row_gates, weights, memo, experts):
    blocks = picks[0].shape[0]
    width = gathered.shape[1]
    grouped = gathered.reshape(blocks, -1, width)
    pieces = []
    grads = []
    for pick, row_gate, (w_up_gate, w_down), kept, expert in zip(
        picks, row_gates, weights, memo, experts
    ):
        rows, gate_pre, up_pre, hidden = kept
        grad_rows = jnp.einsum(PICK, pick, grouped, preferred_element_type=jnp.float32)
        grad_rows = grad_rows.astype(jnp.bfloat16).reshape(-1, width)
        through = lax.dot_general(
            grad_rows, w_down, (((1,), (1,)), ((), ())), preferred_element_type=jnp.float32
        )
        hidden_f = hidden.astype(jnp.float32)
        gate_grad = jnp.sum(hidden_f * through, axis=1, keepdims=True)
        high = gate_grad.astype(jnp.bfloat16)
        low = (gate_grad - high.astype(jnp.float32)).astype(jnp.bfloat16)
        column = jnp.arange(GATE_COLUMNS, dtype=jnp.int32)[None, :]
        gate_part = jnp.where(
            column == expert, high, jnp.where(column == expert + EXPERTS, low, 0)
        )
        grad_hidden = through * row_gate
        sigmoid_gate = jax.nn.sigmoid(gate_pre)
        grad_pre = jnp.concatenate(
            [
                (
                    grad_hidden * up_pre * sigmoid_gate * (1.0 + gate_pre * (1.0 - sigmoid_gate))
                ).astype(jnp.bfloat16),
                (grad_hidden * gate_pre * sigmoid_gate).astype(jnp.bfloat16),
            ],
            axis=1,
        )
        grad_down = lax.dot_general(
            (hidden_f * row_gate).astype(jnp.bfloat16),
            grad_rows,
            (((0,), (0,)), ((), ())),
            preferred_element_type=jnp.float32,
        ).astype(jnp.bfloat16)
        grad_up_gate = lax.dot_general(
            rows, grad_pre, (((0,), (0,)), ((), ())), preferred_element_type=jnp.float32
        ).astype(jnp.bfloat16)
        grad_in = lax.dot_general(
            grad_pre, w_up_gate, (((1,), (1,)), ((), ())), preferred_element_type=jnp.float32
        ).astype(jnp.bfloat16)
        piece = jnp.concatenate([grad_in, gate_part], axis=1)
        pieces.append(piece.reshape(blocks, -1, width + GATE_COLUMNS))
        grads.append((grad_up_gate, grad_down))
    return send_back(picks, pieces), grads


def chip_shards(
    tokens,
    cotangent,
    lengths,
    routes,
    gains,
    w_query,
    key_weight,
    value_weight,
    w_out,
    w_router,
    w_gate,
    w_up,
    w_down,
):
    rows = tokens.shape[0]
    width = lax.axis_size(FSDP)
    place = lax.axis_index(FSDP)
    line = lax.axis_index(LINE)
    core = lax.axis_index(CORE)
    devices = width * lax.axis_size(LINE) * 2
    chips = devices // 2
    chip = place * lax.axis_size(LINE) + line
    depth = lax.axis_size(LINE)
    group = QUERY_HEADS // KEY_VALUE_HEADS
    ff = w_gate.shape[3]
    short = w_query.shape[1]
    experts_here = w_gate.shape[1]
    gain_columns = -(-gains.size // short)
    side = jnp.concatenate(
        [w_router[number] for number in range(DECODER_LAYERS)]
        + [jnp.pad(gains.reshape(-1), (0, gain_columns * short - gains.size)).reshape(short, -1)],
        axis=1,
    )
    side = by_core(core, side, swap(side), 0)
    router_columns = DECODER_LAYERS * EXPERTS
    cut = side.shape[1]
    small = jnp.concatenate(
        [side]
        + [routes[number].astype(jnp.bfloat16) for number in range(DECODER_LAYERS)]
        + [jnp.broadcast_to(lengths.astype(jnp.bfloat16), (rows, lengths.shape[1]))],
        axis=1,
    )
    small = jnp.pad(small, ((0, 0), (0, -small.shape[1] % 128)))

    small = gather_chips(small, 1)

    qkv_columns = (group + 2) * HEAD_SIZE

    def columns_of(number):
        return jnp.concatenate(
            [
                w_query[number]
                .reshape(short, width, depth, 2, HEAD_SIZE)
                .transpose(1, 0, 3, 2, 4)
                .reshape(width, short, group * HEAD_SIZE),
                key_weight[number].reshape(short, width, HEAD_SIZE).transpose(1, 0, 2),
                value_weight[number].reshape(short, width, HEAD_SIZE).transpose(1, 0, 2),
            ],
            axis=2,
        )

    def rows_by_source(source):
        whole = jnp.zeros((width, short, qkv_columns), jnp.bfloat16)
        for origin, piece in swap_pieces(
            lambda to: lax.dynamic_index_in_dim(source, to, 0, keepdims=False), place, width
        ):
            whole = lax.dynamic_update_index_in_dim(whole, piece, origin, 0)
        return whole.reshape(width * short, qkv_columns)

    def line_gather(operand):
        return lax.all_gather(operand, LINE, axis=0, tiled=True)

    def both_cores(operand):
        return by_core(core, operand, swap(operand), 0)

    first_rows = gather_chips(rows_by_source(columns_of(0)), 8, LINE_ONLY)
    dense_qkv = [both_cores(first_rows)]
    dense_out = [both_cores(line_gather(w_out[0]))]
    for number in range(1, DECODER_LAYERS):
        dense_qkv.append(
            both_cores(line_gather(after(rows_by_source(columns_of(number)), first_rows)))
        )
        dense_out.append(both_cores(line_gather(after(w_out[number], first_rows))))
    cotangent_all = offload_gather(after(cotangent, first_rows))
    routers = [
        small[:, number * EXPERTS : (number + 1) * EXPERTS] for number in range(DECODER_LAYERS)
    ]
    all_gains = (
        small[:, router_columns:cut]
        .reshape(devices, -1)[:, : gains.size]
        .reshape(devices, DECODER_LAYERS, -1)
        .transpose(1, 0, 2)
        .reshape(DECODER_LAYERS, -1)
        .astype(jnp.float32)
    )
    all_routes = (
        small[:, cut : cut + DECODER_LAYERS * TOP]
        .reshape(chips, rows, DECODER_LAYERS, TOP)
        .transpose(0, 2, 1, 3)
    )
    cut = cut + DECODER_LAYERS * TOP
    all_lengths = (
        small.reshape(width, depth, rows, -1)[:, :, 0, cut : cut + lengths.shape[1]]
        .astype(jnp.int32)
    )
    all_lengths = lax.dynamic_index_in_dim(all_lengths, line, 1, keepdims=False)
    chosen = jnp.any(
        all_routes[..., None] == jnp.arange(EXPERTS, dtype=jnp.bfloat16), axis=3
    )
    chosen_f = chosen.astype(jnp.bfloat16)
    before = jnp.tril(jnp.ones((rows, rows), jnp.bfloat16), -1)
    ranks = jnp.einsum(
        "ts,clse->clte", before, chosen_f, preferred_element_type=jnp.float32
    )
    first = (line * 2 + core) * experts_here + place
    second = (line * 2 + (1 - core)) * experts_here + place
    slots = jnp.arange(CAP, dtype=jnp.float32)

    def pick_of(number, expert):
        named = lax.dynamic_index_in_dim(chosen[:, number], expert, 2, keepdims=False)
        rank = lax.dynamic_index_in_dim(ranks[:, number], expert, 2, keepdims=False)
        return (
            (rank[:, None, :] == slots[None, :, None]) & named[:, None, :]
        ).astype(jnp.bfloat16)

    picks = [(pick_of(number, first), pick_of(number, second)) for number in range(DECODER_LAYERS)]

    cosine, sine, allowed = jax.vmap(lambda own: geometry(own[None], rows))(all_lengths)
    angles = (
        cosine.reshape(width * rows, 1, -1),
        sine.reshape(width * rows, 1, -1),
        allowed,
    )
    g_attn, g_ffn, g_query, g_key = zip(*[split_gains(all_gains[i]) for i in range(DECODER_LAYERS)])

    state = tokens.astype(jnp.float32)
    kept = []
    for number in range(DECODER_LAYERS):
        normed = norm_rows(state, g_attn[number]).astype(jnp.bfloat16)
        normed = gather_chips(by_owner(normed, width), 6, PLANE)
        dense = (dense_qkv[number], dense_out[number], normed, g_query[number], g_key[number])
        ready = small if number == 0 else gathered
        gate_up_source = after(
            jnp.concatenate([w_gate[number], w_up[number]], axis=2).reshape(-1, 2 * ff), ready
        ).reshape(width, -1, 2 * ff)
        down_source = after(w_down[number].reshape(-1, w_down.shape[3]), ready).reshape(
            width, ff, -1
        )
        up_gate = jnp.zeros((width, MODEL_WIDTH // width, 2 * ff), jnp.bfloat16)
        for origin, piece in swap_pieces(
            lambda to: lax.dynamic_index_in_dim(gate_up_source, to, 0, keepdims=False), place, width
        ):
            up_gate = lax.dynamic_update_index_in_dim(up_gate, piece, origin, 0)
        up_gate = up_gate.reshape(MODEL_WIDTH, 2 * ff)
        down = jnp.zeros((ff, MODEL_WIDTH), jnp.bfloat16)
        for origin, piece in swap_pieces(
            lambda to: lax.dynamic_index_in_dim(down_source, to, 0, keepdims=False), place, width
        ):
            down = lax.dynamic_update_slice_in_dim(down, piece, origin * piece.shape[1], 1)
        weights = ((up_gate, down), (swap(up_gate), swap(down)))
        middle, memo = attention_forward(state, dense, angles)
        mixer_in = norm_rows(middle, g_ffn[number]).astype(jnp.bfloat16)
        gathered = gather_chips(mixer_in, 2)
        logits = jnp.dot(gathered, routers[number], preferred_element_type=jnp.float32)
        named = chosen[:, number].reshape(chips * rows, EXPERTS)
        gates = softmax_last(jnp.where(named, logits, -1e30))
        row_gates = []
        for pick, expert in zip(picks[number], (first, second)):
            gate = lax.dynamic_index_in_dim(gates, expert, 1, keepdims=False)
            row_gates.append(
                jnp.sum(
                    pick.astype(jnp.float32) * gate.reshape(chips, 1, rows), axis=2
                ).reshape(-1, 1)
            )
        produced, expert_memo = expert_forward(gathered, picks[number], row_gates, weights)
        new_state = middle + scatter_chips(produced, 3).astype(jnp.float32)
        own_gates = lax.dynamic_slice_in_dim(gates, chip * rows, rows, 0)
        kept.append(
            (state, middle, mixer_in, own_gates, row_gates, dense, weights, memo, expert_memo)
        )
        state = new_state
    result = state.astype(jnp.bfloat16)

    grad_state = cotangent.astype(jnp.float32)
    grad_low = cotangent
    grad_gathered = cotangent_all
    small_grads = []
    d_out = []
    d_qkv = []
    share = MODEL_WIDTH // width
    d_up_gate = jnp.zeros((DECODER_LAYERS, width, share, 2 * ff), jnp.bfloat16)
    d_down = jnp.zeros((DECODER_LAYERS, width, ff, share), jnp.bfloat16)
    for number in reversed(range(DECODER_LAYERS)):
        state, middle, mixer_in, own_gates, row_gates, dense, weights, memo, expert_memo = kept[
            number
        ]
        back, expert_grads = expert_backward(
            grad_gathered, picks[number], row_gates, weights, expert_memo, (first, second)
        )
        (own_up_gate, own_down), (other_up_gate, other_down) = expert_grads
        grad_up_gate = own_up_gate + swap(other_up_gate)
        grad_down = own_down + swap(other_down)
        received = []
        for origin, piece in swap_pieces(
            lambda to: lax.dynamic_slice_in_dim(grad_up_gate, to * share, share, 0), place, width
        ):
            received.append(piece)
            d_up_gate = lax.dynamic_update_slice(
                d_up_gate, piece[None, None], (number, origin, 0, 0)
            )
        for origin, piece in swap_pieces(
            lambda to: lax.dynamic_slice_in_dim(grad_down, to * share, share, 1), place, width
        ):
            received.append(piece)
            d_down = lax.dynamic_update_slice(d_down, piece[None, None], (number, origin, 0, 0))
        back = scatter_chips(back, 5).astype(jnp.float32)
        grad_gates = (
            back[:, MODEL_WIDTH : MODEL_WIDTH + EXPERTS]
            + back[:, MODEL_WIDTH + EXPERTS : MODEL_WIDTH + 2 * EXPERTS]
        )
        grad_logits = (
            own_gates
            * (grad_gates - jnp.sum(own_gates * grad_gates, axis=1, keepdims=True))
        ).astype(jnp.bfloat16)
        grad_router = lax.dot_general(
            mixer_in, grad_logits, (((0,), (0,)), ((), ())), preferred_element_type=jnp.float32
        )
        grad_mixer = back[:, :MODEL_WIDTH] + lax.dot_general(
            grad_logits,
            routers[number],
            (((1,), (1,)), ((), ())),
            preferred_element_type=jnp.float32,
        )
        unused_mid, norm_back = jax.vjp(norm_rows, middle, g_ffn[number])
        grad_mid_part, grad_g_ffn = norm_back(grad_mixer)
        grad_middle = grad_state + grad_mid_part
        low = gather_chips(after(grad_middle.astype(jnp.bfloat16), grad_up_gate, grad_down), 6, PLANE)
        grad_normed, grad_wqkv, grad_wout, grad_gq, grad_gk = attention_backward(
            low, memo, dense, angles
        )
        grad_normed = by_place(grad_normed.astype(jnp.float32), width)
        unused_state, norm_front = jax.vjp(norm_rows, state, g_attn[number])
        grad_in_part, grad_g_attn = norm_front(grad_normed)
        grad_state = grad_middle + grad_in_part
        grad_low = grad_state.astype(jnp.bfloat16)
        if number > 0:
            grad_gathered = gather_chips(after(grad_low, *received), 2)

        def line_sum(operand):
            half = operand.shape[0] // 2
            mine = lax.dynamic_slice_in_dim(operand, core * half, half, 0)
            other = swap(lax.dynamic_slice_in_dim(operand, (1 - core) * half, half, 0))
            return lax.psum_scatter(mine + other, LINE, scatter_dimension=0, tiled=True)

        d_out.insert(0, line_sum(grad_wout).astype(jnp.float32))
        summed = line_sum(grad_wqkv).reshape(width, short, qkv_columns)
        whole = jnp.zeros_like(summed)
        for origin, piece in swap_pieces(
            lambda to: lax.dynamic_index_in_dim(summed, to, 0, keepdims=False), place, width
        ):
            whole = lax.dynamic_update_index_in_dim(whole, piece, origin, 0)
        d_qkv.insert(0, whole)
        gain_grads = jnp.concatenate([grad_g_attn, grad_g_ffn, grad_gq, grad_gk])
        small_grads.insert(0, (grad_router, gain_grads.reshape(devices, -1)))
    d_out = jnp.stack(d_out)
    d_gate = d_up_gate[..., :ff].astype(jnp.float32)
    d_up = d_up_gate[..., ff:].astype(jnp.float32)
    d_down = d_down.astype(jnp.float32)
    own_gains = jnp.concatenate([gain_grad for _, gain_grad in small_grads], axis=1)
    own_gains = jnp.pad(own_gains, ((0, 0), (0, gain_columns * short - gains.size)))
    side = jnp.concatenate(
        [router_grad for router_grad, _ in small_grads] + [own_gains.reshape(MODEL_WIDTH, -1)],
        axis=1,
    ).astype(jnp.bfloat16)
    side = jnp.pad(side, ((0, 0), (0, -side.shape[1] % 128)))
    side = scatter_chips(side, 4).astype(jnp.float32)
    small = lax.dynamic_slice_in_dim(side, core * short, short, 0) + swap(
        lax.dynamic_slice_in_dim(side, (1 - core) * short, short, 0)
    )
    d_router = jnp.stack(
        [small[:, number * EXPERTS : (number + 1) * EXPERTS] for number in range(DECODER_LAYERS)]
    )
    d_gains = small[:, router_columns : router_columns + gain_columns].reshape(-1)[: gains.size]
    d_gains = d_gains.reshape(gains.shape)
    d_qkv = jnp.stack(d_qkv).astype(jnp.float32)
    cut = group * HEAD_SIZE
    d_query = (
        d_qkv[..., :cut]
        .reshape(DECODER_LAYERS, width, short, 2, depth, HEAD_SIZE)
        .transpose(0, 2, 1, 4, 3, 5)
        .reshape(w_query.shape)
    )
    d_key = d_qkv[..., cut : cut + HEAD_SIZE].transpose(0, 2, 1, 3).reshape(key_weight.shape)
    d_value = d_qkv[..., cut + HEAD_SIZE :].transpose(0, 2, 1, 3).reshape(value_weight.shape)
    return (
        result,
        grad_low,
        d_gains,
        d_query,
        d_key,
        d_value,
        d_out,
        d_router,
        d_gate,
        d_up,
        d_down,
    )


def by_chip(mesh):
    grid = Mesh(
        mesh.devices.reshape(mesh.shape[FSDP], mesh.shape["expert"] // 2, 2),
        EVERY,
    )
    experts = (LINE, CORE)
    return jax.shard_map(
        chip_shards,
        mesh=grid,
        in_specs=(
            P(EVERY, None),
            P(EVERY, None),
            P(EVERY, None),
            P(None, EVERY, None),
            P(None, EVERY),
            P(None, EVERY, None),
            P(None, EVERY, None),
            P(None, EVERY, None),
            P(None, EVERY, None),
            P(None, EVERY, None),
            P(None, experts, FSDP, None),
            P(None, experts, FSDP, None),
            P(None, experts, None, FSDP),
        ),
        out_specs=(
            P(EVERY, None),
            P(EVERY, None),
            P(None, EVERY),
            P(None, EVERY, None),
            P(None, EVERY, None),
            P(None, EVERY, None),
            P(None, EVERY, None),
            P(None, EVERY, None),
            P(None, experts, FSDP, None),
            P(None, experts, FSDP, None),
            P(None, experts, None, FSDP),
        ),
        check_vma=False,
    )


def solution(mesh):
    width = mesh.shape[FSDP]
    peers = mesh.shape["expert"]
    if width == KEY_VALUE_HEADS == PAIR and peers * width == EXPERTS == QUERY_HEADS:
        return by_chip(mesh)
    return general(mesh)
```

```python
from functools import partial
import math

import jax
import jax.numpy as jnp
from jax import lax
from jax.experimental import pallas as pl
from jax.experimental.pallas import tpu as pltpu
from jax.sharding import Mesh
from jax.sharding import PartitionSpec as P

MODEL_WIDTH = 2048
QUERY_HEADS = 32
KEY_VALUE_HEADS = 4
HEAD_SIZE = 128
TOP = 8
EXPERTS = 32
DECODER_LAYERS = 2
CAP = 48


EPSILON = 1e-06
ROPE_BASE = 1000000.0


def norm_rows(operand, gain_vec):
    return (
        operand
        * lax.rsqrt(jnp.mean(operand * operand, axis=-1, keepdims=True) + EPSILON)
        * gain_vec
    )


def softmax_last(operand):
    shifted = operand - jnp.max(operand, axis=-1, keepdims=True)
    weights = jnp.exp(shifted)
    return weights / jnp.sum(weights, axis=-1, keepdims=True)


def rotate(operand, cosine, sine):
    half_size = operand.shape[-1] // 2
    front_half = operand[..., :half_size]
    back_half = operand[..., half_size:]
    return jnp.concatenate(
        [front_half * cosine - back_half * sine, back_half * cosine + front_half * sine], axis=-1
    )


def head_piece(query_pre, prerotation_key, g_query, g_key, cosine, sine):
    return (
        rotate(norm_rows(query_pre, g_query), cosine, sine),
        rotate(norm_rows(prerotation_key, g_key), cosine, sine),
    )


def geometry(lengths, local_rows):
    seq_ends = jnp.cumsum(lengths[0])
    seq_starts = seq_ends - lengths[0]
    offsets = jnp.arange(local_rows, dtype=jnp.int32)
    segment = jnp.sum((offsets[:, None] >= seq_ends[None, :]).astype(jnp.int32), axis=1)
    member = segment[:, None] == jnp.arange(seq_ends.shape[0], dtype=jnp.int32)[None, :]
    begins = jnp.sum(jnp.where(member, seq_starts[None, :], 0), axis=1)
    position = (offsets - begins).astype(jnp.float32)
    inverse = jnp.exp(
        -(2.0 * jnp.arange(HEAD_SIZE // 2, dtype=jnp.float32) / HEAD_SIZE) * math.log(ROPE_BASE)
    )
    angles = position[:, None] * inverse[None, :]
    allowed = (segment[:, None] == segment[None, :]) & (offsets[None, :] <= offsets[:, None])
    return (jnp.cos(angles)[:, None, :], jnp.sin(angles)[:, None, :], allowed)


def slot_table(route_rows):
    flat_routes = route_rows.reshape(-1)
    matches = (flat_routes[:, None] == jnp.arange(EXPERTS, dtype=jnp.int32)[None, :]).astype(
        jnp.int32
    )
    rank_in = jnp.sum((jnp.cumsum(matches, axis=0) - 1) * matches, axis=1)
    return flat_routes * CAP + rank_in


def split_gains(gain_vec):
    return (
        gain_vec[:MODEL_WIDTH],
        gain_vec[MODEL_WIDTH : 2 * MODEL_WIDTH],
        gain_vec[2 * MODEL_WIDTH : 2 * MODEL_WIDTH + HEAD_SIZE],
        gain_vec[2 * MODEL_WIDTH + HEAD_SIZE :],
    )


def score_block(query_copy, key_b, allowed):
    local_rows = query_copy.shape[0]
    grouped_rows = query_copy.reshape(
        local_rows, KEY_VALUE_HEADS, QUERY_HEADS // KEY_VALUE_HEADS, HEAD_SIZE
    )
    raw_scores = jnp.einsum(
        "tgjd,sgd->gjts", grouped_rows, key_b, preferred_element_type=jnp.float32
    ) * (1.0 / math.sqrt(HEAD_SIZE))
    return jnp.where(allowed[None, None], raw_scores, -1e30)


def layer_forward(state, dense, experts, route_rows, cosine, sine, allowed, peers):
    w_query, key_weight, value_weight, w_out, w_router, gain_raw = dense
    w_gate, w_up, w_down = experts
    local_rows = state.shape[0]
    experts_here = w_gate.shape[0]
    g_attn, g_ffn, g_query, g_key = split_gains(gain_raw.astype(jnp.float32))
    normalized_input = norm_rows(state, g_attn).astype(jnp.bfloat16)
    query_pre = jnp.dot(normalized_input, w_query, preferred_element_type=jnp.float32).reshape(
        local_rows, QUERY_HEADS, HEAD_SIZE
    )
    prerotation_key = jnp.dot(
        normalized_input, key_weight, preferred_element_type=jnp.float32
    ).reshape(local_rows, KEY_VALUE_HEADS, HEAD_SIZE)
    value_b = (
        jnp.dot(normalized_input, value_weight, preferred_element_type=jnp.float32)
        .astype(jnp.bfloat16)
        .reshape(local_rows, KEY_VALUE_HEADS, HEAD_SIZE)
    )
    query_f, key_f = head_piece(query_pre, prerotation_key, g_query, g_key, cosine, sine)
    query_copy = query_f.astype(jnp.bfloat16)
    key_b = key_f.astype(jnp.bfloat16)
    scores = score_block(query_copy, key_b, allowed)
    peaks = jnp.max(scores, axis=-1, keepdims=True)
    expos = jnp.exp(scores - peaks)
    totals = jnp.sum(expos, axis=-1, keepdims=True)
    log_total = peaks + jnp.log(totals)
    probs_b = (expos / totals).astype(jnp.bfloat16)
    attended = jnp.einsum("gjts,sgd->tgjd", probs_b, value_b, preferred_element_type=jnp.float32)
    attended = attended.reshape(local_rows, QUERY_HEADS * HEAD_SIZE).astype(jnp.bfloat16)
    middle = state + jnp.dot(attended, w_out, preferred_element_type=jnp.float32)
    mixer_in = norm_rows(middle, g_ffn).astype(jnp.bfloat16)
    logits = jnp.dot(mixer_in, w_router, preferred_element_type=jnp.float32)
    gates = softmax_last(jnp.take_along_axis(logits, route_rows, axis=1))
    slot_ids = slot_table(route_rows)
    outgoing = (
        jnp.zeros((EXPERTS * CAP, MODEL_WIDTH), jnp.bfloat16)
        .at[slot_ids]
        .set(jnp.repeat(mixer_in, TOP, axis=0))
    )
    incoming = lax.all_to_all(
        outgoing.reshape(peers, experts_here * CAP, MODEL_WIDTH),
        "expert",
        split_axis=0,
        concat_axis=0,
        tiled=True,
    )
    incoming = incoming.reshape(peers, experts_here, CAP, MODEL_WIDTH)
    gate_pre = jnp.einsum("secd,edf->secf", incoming, w_gate, preferred_element_type=jnp.float32)
    up_pre = jnp.einsum("secd,edf->secf", incoming, w_up, preferred_element_type=jnp.float32)
    hidden_b = (jax.nn.silu(gate_pre) * up_pre).astype(jnp.bfloat16)
    produced = jnp.einsum(
        "secf,efd->secd", hidden_b, w_down, preferred_element_type=jnp.float32
    ).astype(jnp.bfloat16)
    returned = lax.all_to_all(
        produced.reshape(peers, experts_here * CAP, MODEL_WIDTH),
        "expert",
        split_axis=0,
        concat_axis=0,
        tiled=True,
    )
    picked = returned.reshape(EXPERTS * CAP, MODEL_WIDTH)[slot_ids].reshape(
        local_rows, TOP, MODEL_WIDTH
    )
    new_state = middle + jnp.sum(gates[:, :, None] * picked.astype(jnp.float32), axis=1)
    memo = (
        state,
        normalized_input,
        query_pre,
        prerotation_key,
        query_copy,
        key_b,
        value_b,
        log_total,
        attended,
        middle,
        mixer_in,
        gates,
        slot_ids,
        picked,
        incoming,
        gate_pre,
        up_pre,
        hidden_b,
    )
    return (new_state, memo)


def layer_backward(grad_state, memo, dense, experts, route_rows, cosine, sine, allowed, peers):
    (
        state,
        normalized_input,
        query_pre,
        prerotation_key,
        query_copy,
        key_b,
        value_b,
        log_total,
        attended,
        middle,
        mixer_in,
        gates,
        slot_ids,
        picked,
        incoming,
        gate_pre,
        up_pre,
        hidden_b,
    ) = memo
    w_query, key_weight, value_weight, w_out, w_router, gain_raw = dense
    w_gate, w_up, w_down = experts
    local_rows = state.shape[0]
    experts_here = w_gate.shape[0]
    query_group_size = QUERY_HEADS // KEY_VALUE_HEADS
    scale = 1.0 / math.sqrt(HEAD_SIZE)
    g_attn, g_ffn, g_query, g_key = split_gains(gain_raw.astype(jnp.float32))
    grad_gates = jnp.sum(picked.astype(jnp.float32) * grad_state[:, None, :], axis=2)
    grad_chosen = gates * (grad_gates - jnp.sum(gates * grad_gates, axis=1, keepdims=True))
    choose = (route_rows[:, :, None] == jnp.arange(EXPERTS, dtype=jnp.int32)[None, None, :]).astype(
        jnp.float32
    )
    grad_logits = jnp.sum(choose * grad_chosen[:, :, None], axis=1).astype(jnp.bfloat16)
    grad_router = jnp.dot(mixer_in.T, grad_logits, preferred_element_type=jnp.float32)
    grad_mixer = jnp.dot(grad_logits, w_router.T, preferred_element_type=jnp.float32)
    grad_picked = (
        (gates[:, :, None] * grad_state[:, None, :])
        .astype(jnp.bfloat16)
        .reshape(local_rows * TOP, MODEL_WIDTH)
    )
    outgoing = jnp.zeros((EXPERTS * CAP, MODEL_WIDTH), jnp.bfloat16).at[slot_ids].set(grad_picked)
    grad_produced = lax.all_to_all(
        outgoing.reshape(peers, experts_here * CAP, MODEL_WIDTH),
        "expert",
        split_axis=0,
        concat_axis=0,
        tiled=True,
    )
    grad_produced = grad_produced.reshape(peers, experts_here, CAP, MODEL_WIDTH)
    grad_down = jnp.einsum(
        "secf,secd->efd", hidden_b, grad_produced, preferred_element_type=jnp.float32
    )
    grad_hidden = jnp.einsum(
        "secd,efd->secf", grad_produced, w_down, preferred_element_type=jnp.float32
    )
    sigmoid_gate = jax.nn.sigmoid(gate_pre)
    grad_gate_pre = (
        grad_hidden * up_pre * sigmoid_gate * (1.0 + gate_pre * (1.0 - sigmoid_gate))
    ).astype(jnp.bfloat16)
    grad_up_pre = (grad_hidden * gate_pre * sigmoid_gate).astype(jnp.bfloat16)
    grad_wgate = jnp.einsum(
        "secd,secf->edf", incoming, grad_gate_pre, preferred_element_type=jnp.float32
    )
    grad_wup = jnp.einsum(
        "secd,secf->edf", incoming, grad_up_pre, preferred_element_type=jnp.float32
    )
    grad_incoming = jnp.einsum(
        "secf,edf->secd", grad_gate_pre, w_gate, preferred_element_type=jnp.float32
    )
    grad_incoming = grad_incoming + jnp.einsum(
        "secf,edf->secd", grad_up_pre, w_up, preferred_element_type=jnp.float32
    )
    grad_incoming = grad_incoming.astype(jnp.bfloat16).reshape(
        peers, experts_here * CAP, MODEL_WIDTH
    )
    grad_returned = lax.all_to_all(
        grad_incoming, "expert", split_axis=0, concat_axis=0, tiled=True
    ).reshape(EXPERTS * CAP, MODEL_WIDTH)
    grad_mixer = grad_mixer + jnp.sum(
        grad_returned[slot_ids].reshape(local_rows, TOP, MODEL_WIDTH).astype(jnp.float32), axis=1
    )
    unused_mid, norm_back = jax.vjp(norm_rows, middle, g_ffn)
    grad_mid_part, grad_g_ffn = norm_back(grad_mixer)
    grad_middle = grad_state + grad_mid_part
    grad_middle_low = grad_middle.astype(jnp.bfloat16)
    grad_wout = jnp.dot(attended.T, grad_middle_low, preferred_element_type=jnp.float32)
    attended_gradient = jnp.dot(
        grad_middle_low, w_out.T, preferred_element_type=jnp.float32
    ).astype(jnp.bfloat16)
    attended_gradient = attended_gradient.reshape(
        local_rows, KEY_VALUE_HEADS, query_group_size, HEAD_SIZE
    )
    scores = score_block(query_copy, key_b, allowed)
    probs = jnp.exp(scores - log_total)
    probs_b = probs.astype(jnp.bfloat16)
    grad_probs = jnp.einsum(
        "tgjd,sgd->gjts", attended_gradient, value_b, preferred_element_type=jnp.float32
    )
    value_gradient = jnp.einsum(
        "gjts,tgjd->sgd", probs_b, attended_gradient, preferred_element_type=jnp.float32
    )
    value_gradient_copy = value_gradient.astype(jnp.bfloat16).reshape(
        local_rows, KEY_VALUE_HEADS * HEAD_SIZE
    )
    grad_scores = (
        probs * (grad_probs - jnp.sum(grad_probs * probs, axis=-1, keepdims=True))
    ).astype(jnp.bfloat16)
    grad_query = (
        jnp.einsum("gjts,sgd->tgjd", grad_scores, key_b, preferred_element_type=jnp.float32) * scale
    )
    query_grouped = query_copy.reshape(local_rows, KEY_VALUE_HEADS, query_group_size, HEAD_SIZE)
    grad_key = (
        jnp.einsum("gjts,tgjd->sgd", grad_scores, query_grouped, preferred_element_type=jnp.float32)
        * scale
    )
    unused_heads, head_back = jax.vjp(
        partial(head_piece, cosine=cosine, sine=sine), query_pre, prerotation_key, g_query, g_key
    )
    grad_qpre, prekey_gradient, grad_gq, grad_gk = head_back(
        (grad_query.reshape(local_rows, QUERY_HEADS, HEAD_SIZE), grad_key)
    )
    grad_qpre_b = grad_qpre.astype(jnp.bfloat16).reshape(local_rows, QUERY_HEADS * HEAD_SIZE)
    prekey_gradient_copy = prekey_gradient.astype(jnp.bfloat16).reshape(
        local_rows, KEY_VALUE_HEADS * HEAD_SIZE
    )
    grad_wquery = jnp.dot(normalized_input.T, grad_qpre_b, preferred_element_type=jnp.float32)
    grad_wkey = jnp.dot(
        normalized_input.T, prekey_gradient_copy, preferred_element_type=jnp.float32
    )
    grad_wvalue = jnp.dot(
        normalized_input.T, value_gradient_copy, preferred_element_type=jnp.float32
    )
    grad_normed = jnp.dot(grad_qpre_b, w_query.T, preferred_element_type=jnp.float32)
    grad_normed = grad_normed + jnp.dot(
        prekey_gradient_copy, key_weight.T, preferred_element_type=jnp.float32
    )
    grad_normed = grad_normed + jnp.dot(
        value_gradient_copy, value_weight.T, preferred_element_type=jnp.float32
    )
    unused_state, norm_front = jax.vjp(norm_rows, state, g_attn)
    grad_in_part, grad_g_attn = norm_front(grad_normed)
    grad_input = grad_middle + grad_in_part
    grad_gains = jnp.concatenate([grad_g_attn, grad_g_ffn, grad_gq, grad_gk])
    dense_grads = (grad_wquery, grad_wkey, grad_wvalue, grad_wout, grad_router, grad_gains)
    expert_grads = (grad_wgate, grad_wup, grad_down)
    return (grad_input, dense_grads, expert_grads)


def shards(
    tokens,
    cotangent,
    lengths,
    routes,
    gains,
    w_query,
    key_weight,
    value_weight,
    w_out,
    w_router,
    w_gate,
    w_up,
    w_down,
):
    local_rows = tokens.shape[0]
    peers = lax.axis_size("expert")
    cosine, sine, allowed = geometry(lengths, local_rows)
    state = tokens.astype(jnp.float32)
    memos = []
    for number in range(DECODER_LAYERS):
        dense = (
            lax.all_gather(w_query[number], ("fsdp", "expert"), axis=0, tiled=True),
            lax.all_gather(key_weight[number], ("fsdp", "expert"), axis=0, tiled=True),
            lax.all_gather(value_weight[number], ("fsdp", "expert"), axis=0, tiled=True),
            lax.all_gather(w_out[number], ("fsdp", "expert"), axis=0, tiled=True),
            lax.all_gather(w_router[number], ("fsdp", "expert"), axis=0, tiled=True),
            lax.all_gather(gains[number], ("fsdp", "expert"), axis=0, tiled=True),
        )
        experts = (
            lax.all_gather(w_gate[number], "fsdp", axis=1, tiled=True),
            lax.all_gather(w_up[number], "fsdp", axis=1, tiled=True),
            lax.all_gather(w_down[number], "fsdp", axis=2, tiled=True),
        )
        state, memo = layer_forward(
            state, dense, experts, routes[number], cosine, sine, allowed, peers
        )
        memos.append(memo)
    result = state.astype(jnp.bfloat16)
    grad_state = cotangent.astype(jnp.float32)
    dense_list = []
    expert_list = []
    for number in reversed(range(DECODER_LAYERS)):
        dense = (
            lax.all_gather(w_query[number], ("fsdp", "expert"), axis=0, tiled=True),
            lax.all_gather(key_weight[number], ("fsdp", "expert"), axis=0, tiled=True),
            lax.all_gather(value_weight[number], ("fsdp", "expert"), axis=0, tiled=True),
            lax.all_gather(w_out[number], ("fsdp", "expert"), axis=0, tiled=True),
            lax.all_gather(w_router[number], ("fsdp", "expert"), axis=0, tiled=True),
            lax.all_gather(gains[number], ("fsdp", "expert"), axis=0, tiled=True),
        )
        experts = (
            lax.all_gather(w_gate[number], "fsdp", axis=1, tiled=True),
            lax.all_gather(w_up[number], "fsdp", axis=1, tiled=True),
            lax.all_gather(w_down[number], "fsdp", axis=2, tiled=True),
        )
        grad_state, dense_grads, expert_grads = layer_backward(
            grad_state, memos[number], dense, experts, routes[number], cosine, sine, allowed, peers
        )
        dense_shards = (
            lax.psum_scatter(dense_grads[0], ("fsdp", "expert"), scatter_dimension=0, tiled=True),
            lax.psum_scatter(dense_grads[1], ("fsdp", "expert"), scatter_dimension=0, tiled=True),
            lax.psum_scatter(dense_grads[2], ("fsdp", "expert"), scatter_dimension=0, tiled=True),
            lax.psum_scatter(dense_grads[3], ("fsdp", "expert"), scatter_dimension=0, tiled=True),
            lax.psum_scatter(dense_grads[4], ("fsdp", "expert"), scatter_dimension=0, tiled=True),
            lax.psum_scatter(dense_grads[5], ("fsdp", "expert"), scatter_dimension=0, tiled=True),
        )
        expert_shards = (
            lax.psum_scatter(
                expert_grads[0].astype(jnp.bfloat16), "fsdp", scatter_dimension=1, tiled=True
            ).astype(jnp.float32),
            lax.psum_scatter(
                expert_grads[1].astype(jnp.bfloat16), "fsdp", scatter_dimension=1, tiled=True
            ).astype(jnp.float32),
            lax.psum_scatter(
                expert_grads[2].astype(jnp.bfloat16), "fsdp", scatter_dimension=2, tiled=True
            ).astype(jnp.float32),
        )
        dense_list.insert(0, dense_shards)
        expert_list.insert(0, expert_shards)
    d_gains = jnp.stack([entry[5] for entry in dense_list])
    d_query = jnp.stack([entry[0] for entry in dense_list])
    d_key = jnp.stack([entry[1] for entry in dense_list])
    d_value = jnp.stack([entry[2] for entry in dense_list])
    d_out = jnp.stack([entry[3] for entry in dense_list])
    d_router = jnp.stack([entry[4] for entry in dense_list])
    d_gate = jnp.stack([entry[0] for entry in expert_list])
    d_up = jnp.stack([entry[1] for entry in expert_list])
    d_down = jnp.stack([entry[2] for entry in expert_list])
    return (
        result,
        grad_state.astype(jnp.bfloat16),
        d_gains,
        d_query,
        d_key,
        d_value,
        d_out,
        d_router,
        d_gate,
        d_up,
        d_down,
    )


def general(mesh):
    return jax.shard_map(
        shards,
        mesh=mesh,
        in_specs=(
            P(("fsdp", "expert"), None),
            P(("fsdp", "expert"), None),
            P(("fsdp", "expert"), None),
            P(None, ("fsdp", "expert"), None),
            P(None, ("fsdp", "expert")),
            P(None, ("fsdp", "expert"), None),
            P(None, ("fsdp", "expert"), None),
            P(None, ("fsdp", "expert"), None),
            P(None, ("fsdp", "expert"), None),
            P(None, ("fsdp", "expert"), None),
            P(None, "expert", "fsdp", None),
            P(None, "expert", "fsdp", None),
            P(None, "expert", None, "fsdp"),
        ),
        out_specs=(
            P(("fsdp", "expert"), None),
            P(("fsdp", "expert"), None),
            P(None, ("fsdp", "expert")),
            P(None, ("fsdp", "expert"), None),
            P(None, ("fsdp", "expert"), None),
            P(None, ("fsdp", "expert"), None),
            P(None, ("fsdp", "expert"), None),
            P(None, ("fsdp", "expert"), None),
            P(None, "expert", "fsdp", None),
            P(None, "expert", "fsdp", None),
            P(None, "expert", None, "fsdp"),
        ),
        check_vma=False,
    )


FSDP, LINE, CORE = "fsdp", "line", "core"
CHIPS = (FSDP, LINE)
EVERY = (FSDP, LINE, CORE)
X, Y, ABOVE, BELOW = range(4)
GATE_COLUMNS = 128
PICK, SPREAD = "bst,btd->bsd", "bst,bsd->btd"


def swap(operand):
    return lax.ppermute(operand, CORE, [(0, 1), (1, 0)])


def by_core(core, mine, other, axis):
    return jnp.where(
        core == 0,
        jnp.concatenate([mine, other], axis=axis),
        jnp.concatenate([other, mine], axis=axis),
    )


def turned(operand):
    half_rows = operand.shape[0] // 2
    return jnp.concatenate([operand[half_rows:], operand[:half_rows]], axis=0)


def offload_gather(operand):
    return lax.all_gather(operand, CHIPS, axis=0, tiled=True)


PAIR = 4
ROW_UNITS = 8


ALL_CHIPS, PLANE, LINE_ONLY = range(3)


def routes_of_shards(grid, depth):
    depth = 1 if grid == PLANE else depth
    offsets = [s * k for k in range(1, depth) for s in (-1, 1)]

    def source(offset):
        return BELOW if offset < 0 else ABOVE

    def onward(offset):
        return ABOVE if offset < 0 else BELOW

    def further(offset):
        return offset - 1 if offset < 0 else offset + 1

    def line_hops(bits, first, last, offset):
        if depth == 1:
            return []
        if offset == 0:
            return [
                (ABOVE, first, last, (bits, -1, first, last, BELOW)),
                (BELOW, first, last, (bits, 1, first, last, ABOVE)),
            ]
        if abs(further(offset)) >= depth:
            return []
        return [(onward(offset), first, last, (bits, further(offset), first, last, source(offset)))]

    if grid == LINE_ONLY:
        return [(None, line_hops(0, 0, 8, 0))] + [
            ((0, offset, 0, 8, source(offset)), line_hops(0, 0, 8, offset)) for offset in offsets
        ]
    plan = []
    own = [(X, 0, 8, (1, 0, 0, 8, X)), (Y, 0, 8, (2, 0, 0, 8, Y))]
    plan.append((None, own + line_hops(0, 0, 8, 0)))
    plan.append(
        ((1, 0, 0, 8, X), [(Y, 3, 7, (3, 0, 3, 7, Y))] + line_hops(1, 6, 8, 0))
    )
    plan.append(
        (
            (2, 0, 0, 8, Y),
            [(X, 0, 3, (3, 0, 0, 3, X)), (X, 7, 8, (3, 0, 7, 8, X))]
            + line_hops(2, 6, 8, 0),
        )
    )

    def spread(offset):
        return (
            (0, offset, 0, 8, source(offset)),
            line_hops(0, 0, 8, offset)
            + [(X, 0, 6, (1, offset, 0, 6, X)), (Y, 0, 6, (2, offset, 0, 6, Y))],
        )

    def crossed(offset):
        return [
            ((1, offset, 0, 6, X), [(Y, 3, 6, (3, offset, 3, 6, Y))]),
            ((2, offset, 0, 6, Y), [(X, 0, 3, (3, offset, 0, 3, X))]),
        ]

    def lined(offset):
        return [
            ((bits, offset, 6, 8, source(offset)), line_hops(bits, 6, 8, offset))
            for bits in (1, 2, 3)
        ]

    def last(offset):
        return [((3, offset, 3, 6, Y), []), ((3, offset, 0, 3, X), [])]

    steps = [(-k, k) for k in range(1, depth)]
    plan += [spread(o) for pair in steps[:1] for o in pair]
    plan += [
        ((3, 0, 3, 7, Y), []),
        ((3, 0, 0, 3, X), []),
        ((3, 0, 7, 8, X), line_hops(3, 6, 8, 0)),
    ]
    for number, pair in enumerate(steps):
        for offset in pair:
            plan += crossed(offset)
        if number + 1 < len(steps):
            plan += [spread(o) for o in steps[number + 1]]
        for offset in pair:
            plan += lined(offset)
        for offset in pair:
            plan += last(offset)
    return plan


class Place:
    def __init__(self, grid, depth):
        self.grid = grid
        self.depth = depth
        self.pair = lax.axis_index(FSDP)
        self.line = lax.axis_index(LINE)
        self.core = lax.axis_index(CORE)
        x = lax.rem(self.pair, 2)
        y = lax.div(self.pair, 2)
        self.pairs = [
            self.pair,
            self.pair + 1 - 2 * x,
            self.pair + 2 - 4 * y,
            PAIR - 1 - self.pair,
        ]

    def shard(self, bits, offset):
        if self.grid == PLANE:
            return self.pairs[bits]
        if self.grid == LINE_ONLY:
            return self.line + offset
        return self.pairs[bits] * self.depth + self.line + offset

    def device(self, neighbour):
        if neighbour == X:
            return (self.pairs[1], self.line, self.core)
        if neighbour == Y:
            return (self.pairs[2], self.line, self.core)
        step = 1 if neighbour == ABOVE else -1
        return (self.pair, self.line + step, self.core)

    def holds(self, offset, neighbour=None):
        low, high = min(offset, 0), max(offset, 0)
        if neighbour == ABOVE:
            high = max(high, 1)
        if neighbour == BELOW:
            low = min(low, -1)
        tests = []
        if low < 0:
            tests.append(self.line >= -low)
        if high > 0:
            tests.append(self.line < self.depth - high)
        if not tests:
            return None
        return tests[0] if len(tests) == 1 else jnp.logical_and(tests[0], tests[1])

    def meet(self):
        barrier = pltpu.get_barrier_semaphore()
        neighbours = (() if self.grid == LINE_ONLY else (X, Y)) + (
            () if self.grid == PLANE else (ABOVE, BELOW)
        )
        for neighbour in neighbours:

            def greet(neighbour=neighbour):
                pl.semaphore_signal(
                    barrier,
                    inc=1,
                    device_id=self.device(neighbour),
                    device_id_type=pl.DeviceIdType.MESH,
                )

            when(self.holds(0, neighbour), greet)
        ends = 0
        if self.grid != PLANE:
            ends = (self.line == 0).astype(jnp.int32) + (self.line == self.depth - 1).astype(
                jnp.int32
            )
        pl.semaphore_wait(barrier, len(neighbours) - ends)


def when(test, action):
    if test is None:
        action()
    else:
        pl.when(test)(action)


def gather_kernel(grid, depth, x_ref, out_ref, own_sem, send_sems, recv_sems):
    plan = routes_of_shards(grid, depth)
    number_of = {item: i for i, (item, _) in enumerate(plan)}
    unit = x_ref.shape[0] // ROW_UNITS
    here = Place(grid, depth)
    own = pltpu.make_async_copy(x_ref, out_ref.at[here.shard(0, 0)], own_sem)
    own.start()
    here.meet()
    sent = []
    for item, hops in plan:
        bits, offset = (0, 0) if item is None else item[:2]

        def step(item=item, hops=hops, bits=bits, offset=offset, site=len(sent)):
            if item is not None:
                piece = out_ref.at[
                    here.shard(bits, offset), pl.ds(item[2] * unit, (item[3] - item[2]) * unit)
                ]
                pltpu.make_async_remote_copy(
                    src_ref=piece,
                    dst_ref=piece,
                    send_sem=send_sems.at[0],
                    recv_sem=recv_sems.at[number_of[item]],
                    device_id=here.device(X),
                    device_id_type=pl.DeviceIdType.MESH,
                ).wait_recv()
            for hop, (neighbour, first, last, there) in enumerate(hops):
                when(
                    here.holds(0, neighbour) if neighbour in (ABOVE, BELOW) else None,
                    lambda n=neighbour, f=first, l=last, t=there, s=site + hop: passing(
                        bits, offset, n, f, l, t, s, item is None
                    ).start(),
                )

        def passing(bits, offset, neighbour, first, last, there, site, own_piece):
            rows = pl.ds(first * unit, (last - first) * unit)
            target = out_ref.at[here.shard(bits, offset), rows]
            return pltpu.make_async_remote_copy(
                src_ref=x_ref.at[rows] if own_piece else target,
                dst_ref=target,
                send_sem=send_sems.at[site],
                recv_sem=recv_sems.at[number_of[there]],
                device_id=here.device(neighbour),
                device_id_type=pl.DeviceIdType.MESH,
            )

        when(None if item is None else here.holds(offset), step)
        for neighbour, first, last, there in hops:
            sent.append((bits, offset, neighbour, first, last, there, len(sent), item is None))
    for bits, offset, neighbour, first, last, there, site, own_piece in sent:

        def finish(a=(bits, offset, neighbour, first, last, there, site, own_piece)):
            passing(*a).wait_send()

        when(here.holds(offset, neighbour), finish)
    own.wait()


def count_plan(grid, depth):
    plan = routes_of_shards(grid, depth)
    return len(plan), sum(len(hops) for _, hops in plan)


def chips_in(grid, depth):
    return {ALL_CHIPS: PAIR * depth, PLANE: PAIR, LINE_ONLY: depth}[grid]


def gather_chips(operand, collective_id, grid=ALL_CHIPS):
    depth = lax.axis_size(LINE)
    items, hops = count_plan(grid, depth)
    chips = chips_in(grid, depth)
    rows, columns = operand.shape
    return pl.pallas_call(
        partial(gather_kernel, grid, depth),
        out_shape=jax.ShapeDtypeStruct((chips, rows, columns), operand.dtype),
        in_specs=[pl.BlockSpec(memory_space=pl.ANY)],
        out_specs=pl.BlockSpec(memory_space=pl.ANY),
        scratch_shapes=[
            pltpu.SemaphoreType.DMA,
            pltpu.SemaphoreType.DMA((hops,)),
            pltpu.SemaphoreType.DMA((items,)),
        ],
        compiler_params=pltpu.CompilerParams(collective_id=collective_id, has_side_effects=True),
        cost_estimate=pl.CostEstimate(
            flops=0, bytes_accessed=66 * chips * rows * columns, transcendentals=0
        ),
    )(operand).reshape(chips * rows, columns)


def scatter_kernel(grid, depth, x_ref, out_ref, sums, landed, own_sem, send_sems, recv_sems):
    plan = routes_of_shards(grid, depth)
    number_of = {item: i for i, (item, _) in enumerate(plan)}
    unit = x_ref.shape[1] // ROW_UNITS
    here = Place(grid, depth)
    own = pltpu.make_async_copy(x_ref, sums, own_sem)
    own.start()
    here.meet()
    own.wait()
    sites = {}
    start = 0
    for item, hops in plan:
        for neighbour, first, last, there in hops:
            sites[there] = (number_of[there] - 1, start)
            start += (last - first) * unit

    def total(shard, first, last, base):
        @pl.loop(0, (last - first) * unit // 16)
        def _(i):
            rows = pl.ds(first * unit + i * 16, 16)
            value = sums[shard, rows].astype(jnp.float32)
            value = value + landed[pl.ds(base + i * 16, 16)].astype(jnp.float32)
            sums[shard, rows] = value.astype(sums.dtype)

    def sending(item):
        bits, offset, first, last, neighbour = item
        sem, base = sites[item]
        size = (last - first) * unit
        return pltpu.make_async_remote_copy(
            src_ref=sums.at[here.shard(bits, offset), pl.ds(first * unit, size)],
            dst_ref=landed.at[pl.ds(base, size)],
            send_sem=send_sems.at[number_of[item]],
            recv_sem=recv_sems.at[sem],
            device_id=here.device(neighbour),
            device_id_type=pl.DeviceIdType.MESH,
        )

    for item, hops in reversed(plan):
        bits, offset = (0, 0) if item is None else item[:2]

        def step(item=item, hops=hops, bits=bits, offset=offset):
            for neighbour, first, last, there in hops:

                def take(first=first, last=last, there=there):
                    sem, base = sites[there]
                    size = (last - first) * unit
                    pltpu.make_async_remote_copy(
                        src_ref=landed.at[pl.ds(base, size)],
                        dst_ref=landed.at[pl.ds(base, size)],
                        send_sem=send_sems.at[0],
                        recv_sem=recv_sems.at[sem],
                        device_id=here.device(X),
                        device_id_type=pl.DeviceIdType.MESH,
                    ).wait_recv()
                    total(here.shard(bits, offset), first, last, base)

                when(
                    here.holds(0, neighbour) if neighbour in (ABOVE, BELOW) else None,
                    take,
                )
            if item is not None:
                sending(item).start()

        when(None if item is None else here.holds(offset), step)
    out_ref[...] = sums[here.shard(0, 0)]
    for item, hops in plan:
        if item is not None:
            when(here.holds(item[1]), lambda item=item: sending(item).wait_send())


def scatter_chips(operand, collective_id, grid=ALL_CHIPS):
    depth = lax.axis_size(LINE)
    chips = chips_in(grid, depth)
    items, hops = count_plan(grid, depth)
    rows, columns = operand.shape[0] // chips, operand.shape[1]
    landed = sum(
        (last - first) * rows // ROW_UNITS
        for _, row in routes_of_shards(grid, depth)
        for _, first, last, _ in row
    )
    return pl.pallas_call(
        partial(scatter_kernel, grid, depth),
        out_shape=jax.ShapeDtypeStruct((rows, columns), operand.dtype),
        in_specs=[pl.BlockSpec(memory_space=pl.ANY)],
        out_specs=pl.BlockSpec(memory_space=pltpu.VMEM),
        scratch_shapes=[
            pltpu.VMEM((chips, rows, columns), operand.dtype),
            pltpu.VMEM((landed, columns), operand.dtype),
            pltpu.SemaphoreType.DMA,
            pltpu.SemaphoreType.DMA((items,)),
            pltpu.SemaphoreType.DMA((hops,)),
        ],
        compiler_params=pltpu.CompilerParams(
            collective_id=collective_id, has_side_effects=True, vmem_limit_bytes=50 * 2**20
        ),
        cost_estimate=pl.CostEstimate(
            flops=0, bytes_accessed=66 * chips * rows * columns, transcendentals=0
        ),
    )(operand.reshape(chips, rows, columns))


def expert_work(x_ref, first, second, produced, out_ref, between):
    blocks, cap, tokens = first[0].shape
    ff = first[3].shape[0]
    group = PAIR
    count = group * cap

    @pl.loop(0, blocks // group)
    def _(g):
        at = pl.ds(pl.multiple_of(g * count, 16), count)
        for k, refs in enumerate((first, second)):
            pick_ref, gate_ref, up_gate_ref, down_ref, rows_ref, pre_ref, hidden_ref = refs

            for i in range(group):
                rows_ref[pl.ds(pl.multiple_of(g * count + i * cap, 16), cap)] = jnp.dot(
                    pick_ref[g * group + i],
                    x_ref[g * group + i],
                    preferred_element_type=jnp.float32,
                ).astype(jnp.bfloat16)
            pre = jnp.dot(rows_ref[at], up_gate_ref[...], preferred_element_type=jnp.float32)
            pre_ref[at] = pre.astype(pre_ref.dtype)
            gate_pre, up_pre = pre[:, :ff], pre[:, ff:]
            hidden = (gate_pre * (1.0 / (1.0 + jnp.exp(-gate_pre))) * up_pre).astype(jnp.bfloat16)
            hidden_ref[at] = hidden
            made = jnp.dot(hidden, down_ref[...], preferred_element_type=jnp.float32)
            produced[k] = (made * gate_ref[at]).astype(jnp.bfloat16)
        for i in range(group):
            total = None
            for k, refs in enumerate((first, second)):
                part = lax.dot_general(
                    refs[0][g * group + i],
                    produced[k, pl.ds(i * cap, cap)],
                    (((0,), (0,)), ((), ())),
                    preferred_element_type=jnp.float32,
                )
                total = part if total is None else total + part
            out_ref[g * group + i] = total.astype(jnp.bfloat16)
        for number, action in between:
            pl.when(g == number)(action)


def weights_kernel(layer, depth, working, *refs):
    refs = list(refs)

    def take(count):
        taken = refs[:count]
        del refs[:count]
        return taken

    w_gate, w_up, w_down, qkv_ref, w_out_ref = take(5)
    inputs = take(9) if working else []
    up_gate_refs = take(2)
    down_refs = take(2)
    dense_refs = take(2)
    outputs = take(7) if working else []
    own_sems, send_sems, recv_sems, side_send, side_recv, line_send, line_recv = take(7)
    here = Place(ALL_CHIPS, depth)
    share = w_gate.shape[2]
    ff = w_gate.shape[3]
    sibling = (here.pair, here.line, 1 - here.core)
    dense_sources = (qkv_ref, w_out_ref.at[layer])

    def device(bits):
        return (here.pairs[bits], here.line, here.core)

    def remote(source, target, send, recv, to):
        return pltpu.make_async_remote_copy(
            src_ref=source,
            dst_ref=target,
            send_sem=send,
            recv_sem=recv,
            device_id=to,
            device_id_type=pl.DeviceIdType.MESH,
        )

    barrier = pltpu.get_barrier_semaphore()
    greeted = [device(1), device(2), device(3), sibling]
    for to in greeted:
        pl.semaphore_signal(barrier, inc=1, device_id=to, device_id_type=pl.DeviceIdType.MESH)
    for neighbour in (ABOVE, BELOW):

        def greet(neighbour=neighbour):
            pl.semaphore_signal(
                barrier,
                inc=1,
                device_id=here.device(neighbour),
                device_id_type=pl.DeviceIdType.MESH,
            )

        when(here.holds(0, neighbour), greet)
    ends = (here.line == 0).astype(jnp.int32) + (here.line == depth - 1).astype(jnp.int32)
    pl.semaphore_wait(barrier, len(greeted) + 2 - ends)

    def shard(k, expert):
        return (w_gate, w_up, w_down)[k].at[layer, expert]

    def spot(which, k, origin):
        start = pl.ds(pl.multiple_of(origin * share, share), share)
        if k == 2:
            return down_refs[which].at[:, start]
        return up_gate_refs[which].at[start, pl.ds(k * ff, ff)]

    def across(bits, k):
        return remote(
            shard(k, here.pairs[bits]),
            spot(0, k, here.pair),
            send_sems.at[bits - 1, k],
            recv_sems.at[bits - 1, k],
            device(bits),
        )

    def beside(bits, k):
        source = shard(k, here.pair) if bits == 0 else spot(0, k, here.pairs[bits])
        return remote(
            source,
            spot(1, k, here.pairs[bits]),
            side_send.at[bits, k],
            side_recv.at[bits, k],
            sibling,
        )

    offsets = [0] + [s * k for k in range(1, depth) for s in (-1, 1)]

    def slab(k, offset):
        return dense_refs[k].at[here.core, here.line + offset]

    def along(k, offset, neighbour):
        number = offsets.index(offset)
        there = offset - 1 if neighbour == ABOVE else offset + 1
        return remote(
            dense_sources[k] if offset == 0 else slab(k, offset),
            slab(k, offset),
            line_send.at[k, number if offset else (0 if neighbour == ABOVE else len(offsets))],
            line_recv.at[k, offsets.index(there)],
            here.device(neighbour),
        )

    def dense_beside(k, offset):
        number = PAIR + offsets.index(offset)
        return remote(
            dense_sources[k] if offset == 0 else slab(k, offset),
            slab(k, offset),
            side_send.at[number, k],
            side_recv.at[number, k],
            sibling,
        )

    def dense_beside_landed(k, offset):
        number = PAIR + offsets.index(offset)
        target = dense_refs[k].at[1 - here.core, here.line + offset]
        return remote(target, target, side_send.at[number, k], side_recv.at[number, k], sibling)

    def onward(offset):
        neighbour = ABOVE if offset < 0 else BELOW
        return neighbour if abs(offset) + 1 < depth else None

    kept = [
        pltpu.make_async_copy(shard(k, here.pair), spot(0, k, here.pair), own_sems.at[k])
        for k in range(3)
    ] + [
        pltpu.make_async_copy(dense_sources[k], slab(k, 0), own_sems.at[3 + k]) for k in range(2)
    ]
    for k in range(2):
        for neighbour in (ABOVE, BELOW):
            when(here.holds(0, neighbour), lambda k=k, n=neighbour: along(k, 0, n).start())
    for k in range(3):
        for bits in (3, 1, 2):
            across(bits, k).start()
    for copy in kept:
        copy.start()
    for k in range(3):
        beside(0, k).start()
    for k in range(2):
        dense_beside(k, 0).start()
    def arrived(offset):
        for k in range(2):
            remote(
                slab(k, offset),
                slab(k, offset),
                line_send.at[k, 0],
                line_recv.at[k, offsets.index(offset)],
                sibling,
            ).wait_recv()
            neighbour = onward(offset)
            if neighbour is not None:
                when(
                    here.holds(0, neighbour),
                    lambda k=k, n=neighbour: along(k, offset, n).start(),
                )
            dense_beside(k, offset).start()

    def line_step(distance):
        for offset in offsets:
            if abs(offset) == distance:
                when(here.holds(offset), lambda offset=offset: arrived(offset))

    def crossed(k):
        for bits in (1, 2, 3):
            remote(
                spot(0, k, here.pairs[bits]),
                spot(0, k, here.pairs[bits]),
                send_sems.at[bits - 1, k],
                recv_sems.at[bits - 1, k],
                sibling,
            ).wait_recv()
            beside(bits, k).start()

    steps = [lambda distance=distance: line_step(distance) for distance in range(1, depth)]
    if working:
        x_ref, picks, gates, ups, downs = (
            inputs[0],
            inputs[1:3],
            inputs[3:5],
            inputs[5:7],
            inputs[7:9],
        )
        experts = [
            (picks[i], gates[i], ups[i], downs[i], outputs[i], outputs[2 + i], outputs[4 + i])
            for i in range(2)
        ]
        turns = x_ref.shape[0] // PAIR
        between = [(turns - len(steps) + i, step) for i, step in enumerate(steps)]
        expert_work(x_ref, *experts, refs[0], outputs[6], between)
    else:
        for step in steps:
            step()
    for k in range(3):
        crossed(k)
    for bits in range(PAIR):
        for k in range(3):
            beside(bits, k).wait_recv()
    for offset in offsets:

        def landed(offset=offset):
            for k in range(2):
                dense_beside_landed(k, offset).wait_recv()

        when(here.holds(offset), landed)
    for bits in (1, 2, 3):
        for k in range(3):
            across(bits, k).wait_send()
    for bits in range(PAIR):
        for k in range(3):
            beside(bits, k).wait_send()
    for offset in offsets:

        def left(offset=offset):
            for k in range(2):
                dense_beside(k, offset).wait_send()
                neighbours = (ABOVE, BELOW) if offset == 0 else (onward(offset),)
                for neighbour in neighbours:
                    if neighbour is not None:
                        when(
                            here.holds(0, neighbour),
                            lambda k=k, n=neighbour: along(k, offset, n).wait_send(),
                        )

        when(here.holds(offset), left)
    for copy in kept:
        copy.wait()


def layer_weights(layer, w_gate, w_up, w_down, qkv_rows, w_out, collective_id, work=None):
    depth = lax.axis_size(LINE)
    share, ff = w_gate.shape[2:]
    model = PAIR * share
    low = jnp.bfloat16
    shapes = [
        jax.ShapeDtypeStruct((model, 2 * ff), low),
        jax.ShapeDtypeStruct((model, 2 * ff), low),
        jax.ShapeDtypeStruct((ff, model), low),
        jax.ShapeDtypeStruct((ff, model), low),
        jax.ShapeDtypeStruct((2, depth) + qkv_rows.shape, low),
        jax.ShapeDtypeStruct((2, depth) + w_out.shape[1:], low),
    ]
    operands = [w_gate, w_up, w_down, qkv_rows, w_out]
    in_specs = [pl.BlockSpec(memory_space=pl.ANY)] * len(operands)
    out_specs = [pl.BlockSpec(memory_space=pl.ANY)] * len(shapes)
    offsets = 2 * depth - 1
    scratch = [
        pltpu.SemaphoreType.DMA((5,)),
        pltpu.SemaphoreType.DMA((3, 3)),
        pltpu.SemaphoreType.DMA((3, 3)),
        pltpu.SemaphoreType.DMA((PAIR + offsets, 3)),
        pltpu.SemaphoreType.DMA((PAIR + offsets, 3)),
        pltpu.SemaphoreType.DMA((2, offsets + 1)),
        pltpu.SemaphoreType.DMA((2, offsets)),
    ]
    if work is not None:
        gathered, picks, row_gates, weights = work
        blocks, cap, rows = picks[0].shape
        count = blocks * cap
        operands += [
            gathered.reshape(blocks, rows, model),
            *picks,
            *row_gates,
            weights[0][0],
            weights[1][0],
            weights[0][1],
            weights[1][1],
        ]
        in_specs += [pl.BlockSpec(memory_space=pltpu.VMEM)] * 9
        shapes += (
            [jax.ShapeDtypeStruct((count, model), low)] * 2
            + [jax.ShapeDtypeStruct((count, 2 * ff), low)] * 2
            + [jax.ShapeDtypeStruct((count, ff), low)] * 2
            + [jax.ShapeDtypeStruct((blocks, rows, model), low)]
        )
        out_specs += [pl.BlockSpec(memory_space=pltpu.VMEM)] * 7
        scratch.append(pltpu.VMEM((2, PAIR * cap, model), low))
    made = pl.pallas_call(
        partial(weights_kernel, layer, depth, work is not None),
        out_shape=shapes,
        in_specs=in_specs,
        out_specs=out_specs,
        scratch_shapes=scratch,
        compiler_params=pltpu.CompilerParams(
            collective_id=collective_id, has_side_effects=True, vmem_limit_bytes=58 * 2**20
        ),
        cost_estimate=pl.CostEstimate(flops=0, bytes_accessed=400 * 2**20, transcendentals=0),
    )(*operands)
    qkv = made[4].reshape(-1, qkv_rows.shape[1])
    out = made[5].reshape(-1, w_out.shape[2])
    return ((made[0], made[2]), (made[1], made[3])), qkv, out, made[6:]


def after(operand, *others):
    there = None
    for other in others:
        corner = other[(0,) * other.ndim].astype(jnp.float32)
        there = (corner == corner) if there is None else there & (corner == corner)
    return jnp.where(there, operand, jnp.zeros_like(operand))


def swap_pieces(piece_of, place, width):
    pieces = [(place, piece_of(place))]
    for step in range(1, width):
        sent = piece_of(place ^ step)
        got = lax.ppermute(sent, FSDP, [(i, i ^ step) for i in range(width)])
        pieces.append((place ^ step, got))
    return pieces


def block_scores(query_copy, key_b, allowed):
    return jnp.where(
        allowed[:, None],
        jnp.einsum("btjd,bsd->bjts", query_copy, key_b, preferred_element_type=jnp.float32)
        * (1.0 / math.sqrt(HEAD_SIZE)),
        -1e30,
    )


def by_owner(operand, width):
    rows = operand.shape[0]
    depth = lax.axis_size(LINE)
    return (
        operand.reshape(rows, width, depth, 2, -1).transpose(0, 3, 2, 1, 4).reshape(rows, -1)
    )


def by_place(operand, width):
    rows = operand.shape[0]
    depth = lax.axis_size(LINE)
    return (
        operand.reshape(rows, 2, depth, width, -1).transpose(0, 3, 2, 1, 4).reshape(rows, -1)
    )


def attention_forward(state, dense, angles):
    cosine, sine, allowed = angles
    w_qkv, w_out, normed, g_query, g_key = dense
    rows = state.shape[0]
    blocks = allowed.shape[0]
    heads = QUERY_HEADS // KEY_VALUE_HEADS
    cut = heads * HEAD_SIZE
    qkv = jnp.dot(normed, w_qkv, preferred_element_type=jnp.float32)
    query_pre = qkv[:, :cut].reshape(-1, heads, HEAD_SIZE)
    key_pre = qkv[:, cut : cut + HEAD_SIZE].reshape(-1, 1, HEAD_SIZE)
    value_b = qkv[:, cut + HEAD_SIZE :].astype(jnp.bfloat16).reshape(blocks, rows, HEAD_SIZE)
    query_f, key_f = head_piece(query_pre, key_pre, g_query, g_key, cosine, sine)
    query_b = query_f.astype(jnp.bfloat16).reshape(blocks, rows, heads, HEAD_SIZE)
    key_b = key_f.astype(jnp.bfloat16).reshape(blocks, rows, HEAD_SIZE)
    scores = block_scores(query_b, key_b, allowed)
    peaks = jnp.max(scores, axis=-1, keepdims=True)
    expos = jnp.exp(scores - peaks)
    totals = jnp.sum(expos, axis=-1, keepdims=True)
    log_total = peaks + jnp.log(totals)
    probs_b = (expos / totals).astype(jnp.bfloat16)
    attended = jnp.einsum("bjts,bsd->btjd", probs_b, value_b, preferred_element_type=jnp.float32)
    attended = attended.reshape(blocks * rows, cut).astype(jnp.bfloat16)
    partial_out = jnp.dot(attended, w_out, preferred_element_type=jnp.float32)
    middle = state + scatter_chips(partial_out.astype(jnp.bfloat16), 7, PLANE).astype(jnp.float32)
    return middle, (normed, query_pre, key_pre, query_b, key_b, value_b, log_total, attended)


def attention_backward(low, memo, dense, angles):
    cosine, sine, allowed = angles
    normed, query_pre, key_pre, query_b, key_b, value_b, log_total, attended = memo
    w_qkv, w_out, unused_normed, g_query, g_key = dense
    blocks, rows, heads, size = query_b.shape
    scale = 1.0 / math.sqrt(HEAD_SIZE)
    grad_attended = lax.dot_general(
        low, w_out, (((1,), (1,)), ((), ())), preferred_element_type=jnp.float32
    ).astype(jnp.bfloat16)
    grad_wout = lax.dot_general(
        attended, low, (((0,), (0,)), ((), ())), preferred_element_type=jnp.float32
    ).astype(jnp.bfloat16)
    grad_attended = grad_attended.reshape(query_b.shape)
    probs = jnp.exp(block_scores(query_b, key_b, allowed) - log_total)
    probs_b = probs.astype(jnp.bfloat16)
    grad_probs = jnp.einsum(
        "btjd,bsd->bjts", grad_attended, value_b, preferred_element_type=jnp.float32
    )
    grad_value = jnp.einsum(
        "bjts,btjd->bsd", probs_b, grad_attended, preferred_element_type=jnp.float32
    )
    grad_scores = (
        probs * (grad_probs - jnp.sum(grad_probs * probs, axis=-1, keepdims=True))
    ).astype(jnp.bfloat16)
    grad_query = (
        jnp.einsum("bjts,bsd->btjd", grad_scores, key_b, preferred_element_type=jnp.float32) * scale
    )
    grad_key = (
        jnp.einsum("bjts,btjd->bsd", grad_scores, query_b, preferred_element_type=jnp.float32)
        * scale
    )
    unused_heads, head_back = jax.vjp(
        partial(head_piece, cosine=cosine, sine=sine), query_pre, key_pre, g_query, g_key
    )
    grad_qpre, grad_kpre, grad_gq, grad_gk = head_back(
        (grad_query.reshape(query_pre.shape), grad_key.reshape(key_pre.shape))
    )
    grad_qkv = jnp.concatenate(
        [
            grad_qpre.astype(jnp.bfloat16).reshape(blocks * rows, heads * size),
            grad_kpre.astype(jnp.bfloat16).reshape(blocks * rows, size),
            grad_value.astype(jnp.bfloat16).reshape(blocks * rows, size),
        ],
        axis=1,
    )
    grad_wqkv = lax.dot_general(
        normed, grad_qkv, (((0,), (0,)), ((), ())), preferred_element_type=jnp.float32
    ).astype(jnp.bfloat16)
    return grad_qkv, grad_wqkv, grad_wout, grad_gq, grad_gk


def send_back(picks, pieces):
    return (
        jnp.einsum(
            SPREAD,
            jnp.concatenate(picks, axis=1),
            jnp.concatenate(pieces, axis=1),
            preferred_element_type=jnp.float32,
        )
        .astype(jnp.bfloat16)
        .reshape(-1, pieces[0].shape[2])
    )


def expert_forward(gathered, picks, row_gates, weights):
    blocks = picks[0].shape[0]
    width = gathered.shape[1]
    grouped = gathered.reshape(blocks, -1, width)
    memo = []
    pieces = []
    for pick, row_gate, (w_up_gate, w_down) in zip(picks, row_gates, weights):
        ff = w_down.shape[0]
        rows = jnp.einsum(PICK, pick, grouped, preferred_element_type=jnp.float32)
        rows = rows.astype(jnp.bfloat16).reshape(-1, width)
        pre = jnp.dot(rows, w_up_gate, preferred_element_type=jnp.float32)
        gate_pre, up_pre = pre[:, :ff], pre[:, ff:]
        hidden = (jax.nn.silu(gate_pre) * up_pre).astype(jnp.bfloat16)
        produced = jnp.dot(hidden, w_down, preferred_element_type=jnp.float32)
        produced = (produced * row_gate).astype(jnp.bfloat16)
        pieces.append(produced.reshape(blocks, -1, width))
        memo.append((rows, pre, hidden))
    return send_back(picks, pieces), memo


def expert_backward(gathered, picks, row_gates, weights, memo, experts):
    blocks = picks[0].shape[0]
    width = gathered.shape[1]
    grouped = gathered.reshape(blocks, -1, width)
    pieces = []
    grads = []
    for pick, row_gate, (w_up_gate, w_down), kept, expert in zip(
        picks, row_gates, weights, memo, experts
    ):
        rows, pre, hidden = kept
        ff = hidden.shape[1]
        gate_pre, up_pre = pre[:, :ff].astype(jnp.float32), pre[:, ff:].astype(jnp.float32)
        grad_rows = jnp.einsum(PICK, pick, grouped, preferred_element_type=jnp.float32)
        grad_rows = grad_rows.astype(jnp.bfloat16).reshape(-1, width)
        through = lax.dot_general(
            grad_rows, w_down, (((1,), (1,)), ((), ())), preferred_element_type=jnp.float32
        )
        hidden_f = hidden.astype(jnp.float32)
        gate_grad = jnp.sum(hidden_f * through, axis=1, keepdims=True)
        high = gate_grad.astype(jnp.bfloat16)
        low = (gate_grad - high.astype(jnp.float32)).astype(jnp.bfloat16)
        column = jnp.arange(GATE_COLUMNS, dtype=jnp.int32)[None, :]
        gate_part = jnp.where(
            column == expert, high, jnp.where(column == expert + EXPERTS, low, 0)
        )
        grad_hidden = through * row_gate
        sigmoid_gate = jax.nn.sigmoid(gate_pre)
        grad_gate_pre = (
            grad_hidden * up_pre * sigmoid_gate * (1.0 + gate_pre * (1.0 - sigmoid_gate))
        ).astype(jnp.bfloat16)
        grad_up_pre = (grad_hidden * gate_pre * sigmoid_gate).astype(jnp.bfloat16)
        grad_down = lax.dot_general(
            (hidden_f * row_gate).astype(jnp.bfloat16),
            grad_rows,
            (((0,), (0,)), ((), ())),
            preferred_element_type=jnp.float32,
        ).astype(jnp.bfloat16)
        grad_gate, grad_up = [
            lax.dot_general(
                rows, part, (((0,), (0,)), ((), ())), preferred_element_type=jnp.float32
            ).astype(jnp.bfloat16)
            for part in (grad_gate_pre, grad_up_pre)
        ]
        grad_in = lax.dot_general(
            jnp.concatenate([grad_gate_pre, grad_up_pre], axis=1),
            w_up_gate,
            (((1,), (1,)), ((), ())),
            preferred_element_type=jnp.float32,
        ).astype(jnp.bfloat16)
        piece = jnp.concatenate([grad_in, gate_part], axis=1)
        pieces.append(piece.reshape(blocks, -1, width + GATE_COLUMNS))
        grads.append((grad_gate, grad_up, grad_down))
    return send_back(picks, pieces), grads


def chip_shards(
    tokens,
    cotangent,
    lengths,
    routes,
    gains,
    w_query,
    key_weight,
    value_weight,
    w_out,
    w_router,
    w_gate,
    w_up,
    w_down,
):
    rows = tokens.shape[0]
    width = lax.axis_size(FSDP)
    place = lax.axis_index(FSDP)
    line = lax.axis_index(LINE)
    core = lax.axis_index(CORE)
    devices = width * lax.axis_size(LINE) * 2
    chips = devices // 2
    chip = place * lax.axis_size(LINE) + line
    depth = lax.axis_size(LINE)
    group = QUERY_HEADS // KEY_VALUE_HEADS
    ff = w_gate.shape[3]
    short = w_query.shape[1]
    experts_here = w_gate.shape[1]
    gain_columns = -(-gains.size // short)
    side = jnp.concatenate(
        [w_router[number] for number in range(DECODER_LAYERS)]
        + [jnp.pad(gains.reshape(-1), (0, gain_columns * short - gains.size)).reshape(short, -1)],
        axis=1,
    )
    side = by_core(core, side, swap(side), 0)
    router_columns = DECODER_LAYERS * EXPERTS
    cut = side.shape[1]
    small = jnp.concatenate(
        [side]
        + [routes[number].astype(jnp.bfloat16) for number in range(DECODER_LAYERS)]
        + [jnp.broadcast_to(lengths.astype(jnp.bfloat16), (rows, lengths.shape[1]))],
        axis=1,
    )
    small = jnp.pad(small, ((0, 0), (0, -small.shape[1] % 128)))

    small = gather_chips(small, 1)

    qkv_columns = (group + 2) * HEAD_SIZE

    def columns_of(number):
        return jnp.concatenate(
            [
                w_query[number]
                .reshape(short, width, depth, 2, HEAD_SIZE)
                .transpose(1, 0, 3, 2, 4)
                .reshape(width, short, group * HEAD_SIZE),
                key_weight[number].reshape(short, width, HEAD_SIZE).transpose(1, 0, 2),
                value_weight[number].reshape(short, width, HEAD_SIZE).transpose(1, 0, 2),
            ],
            axis=2,
        )

    columns = jnp.stack([columns_of(number) for number in range(DECODER_LAYERS)], axis=1)
    by_source = jnp.zeros_like(columns)
    for origin, piece in swap_pieces(
        lambda to: lax.dynamic_index_in_dim(columns, to, 0, keepdims=False), place, width
    ):
        by_source = lax.dynamic_update_index_in_dim(by_source, piece, origin, 0)

    def rows_by_source(number):
        return by_source[:, number].reshape(width * short, qkv_columns)

    routers = [
        small[:, number * EXPERTS : (number + 1) * EXPERTS] for number in range(DECODER_LAYERS)
    ]
    all_gains = (
        small[:, router_columns:cut]
        .reshape(devices, -1)[:, : gains.size]
        .reshape(devices, DECODER_LAYERS, -1)
        .transpose(1, 0, 2)
        .reshape(DECODER_LAYERS, -1)
        .astype(jnp.float32)
    )
    all_routes = (
        small[:, cut : cut + DECODER_LAYERS * TOP]
        .reshape(chips, rows, DECODER_LAYERS, TOP)
        .transpose(0, 2, 1, 3)
    )
    cut = cut + DECODER_LAYERS * TOP
    all_lengths = (
        small.reshape(width, depth, rows, -1)[:, :, 0, cut : cut + lengths.shape[1]]
        .astype(jnp.int32)
    )
    all_lengths = lax.dynamic_index_in_dim(all_lengths, line, 1, keepdims=False)
    chosen = jnp.any(
        all_routes[..., None] == jnp.arange(EXPERTS, dtype=jnp.bfloat16), axis=3
    )
    chosen_f = chosen.astype(jnp.bfloat16)
    before = jnp.tril(jnp.ones((rows, rows), jnp.bfloat16), -1)
    ranks = jnp.einsum(
        "ts,clse->clte", before, chosen_f, preferred_element_type=jnp.float32
    )
    first = (line * 2 + core) * experts_here + place
    second = (line * 2 + (1 - core)) * experts_here + place
    slots = jnp.arange(CAP, dtype=jnp.float32)

    def pick_of(number, expert):
        named = lax.dynamic_index_in_dim(chosen[:, number], expert, 2, keepdims=False)
        rank = lax.dynamic_index_in_dim(ranks[:, number], expert, 2, keepdims=False)
        return (
            (rank[:, None, :] == slots[None, :, None]) & named[:, None, :]
        ).astype(jnp.bfloat16)

    picks = [(pick_of(number, first), pick_of(number, second)) for number in range(DECODER_LAYERS)]

    cosine, sine, allowed = jax.vmap(lambda own: geometry(own[None], rows))(all_lengths)
    angles = (
        cosine.reshape(width * rows, 1, -1),
        sine.reshape(width * rows, 1, -1),
        allowed,
    )
    g_attn, g_ffn, g_query, g_key = zip(*[split_gains(all_gains[i]) for i in range(DECODER_LAYERS)])

    share = MODEL_WIDTH // width

    def to_experts(part):
        return lax.all_to_all(part, FSDP, split_axis=0, concat_axis=0, tiled=True)

    def weights_of(number, work=None):
        return layer_weights(
            number, w_gate, w_up, w_down, rows_by_source(number), w_out, 10 + number, work
        )

    weights, qkv_whole, out_whole, unused_made = weights_of(0)
    state = tokens.astype(jnp.float32)
    kept = []
    for number in range(DECODER_LAYERS):
        normed = norm_rows(state, g_attn[number]).astype(jnp.bfloat16)
        normed = gather_chips(by_owner(normed, width), 6, PLANE)
        dense = (qkv_whole, out_whole, normed, g_query[number], g_key[number])
        middle, memo = attention_forward(state, dense, angles)
        mixer_in = norm_rows(middle, g_ffn[number]).astype(jnp.bfloat16)
        gathered = gather_chips(mixer_in, 2)
        if number == 0:
            cotangent_all = offload_gather(after(cotangent, gathered))
        logits = jnp.dot(gathered, routers[number], preferred_element_type=jnp.float32)
        named = chosen[:, number].reshape(chips * rows, EXPERTS)
        gates = softmax_last(jnp.where(named, logits, -1e30))
        row_gates = []
        for pick, expert in zip(picks[number], (first, second)):
            gate = lax.dynamic_index_in_dim(gates, expert, 1, keepdims=False)
            row_gates.append(
                jnp.sum(
                    pick.astype(jnp.float32) * gate.reshape(chips, 1, rows), axis=2
                ).reshape(-1, 1)
            )
        layer_experts = weights
        if number + 1 < DECODER_LAYERS:
            weights, qkv_whole, out_whole, made = weights_of(
                number + 1, (gathered, picks[number], row_gates, weights)
            )
            expert_memo = [(made[i], made[2 + i], made[4 + i]) for i in range(2)]
            produced = made[6].reshape(gathered.shape)
        else:
            produced, expert_memo = expert_forward(gathered, picks[number], row_gates, weights)
        new_state = middle + scatter_chips(produced, 3).astype(jnp.float32)
        own_gates = lax.dynamic_slice_in_dim(gates, chip * rows, rows, 0)
        kept.append(
            (state, middle, mixer_in, own_gates, row_gates, dense, layer_experts, memo, expert_memo)
        )
        state = new_state
    result = state.astype(jnp.bfloat16)

    def half_sum(operand):
        half = operand.shape[0] // 2
        mine = lax.dynamic_slice_in_dim(operand, core * half, half, 0)
        return mine, swap(lax.dynamic_slice_in_dim(operand, (1 - core) * half, half, 0))

    def line_sum(mine, other):
        return lax.psum_scatter(mine + other, LINE, scatter_dimension=0, tiled=True)

    grad_state = cotangent.astype(jnp.float32)
    grad_low = cotangent
    grad_gathered = cotangent_all
    small_grads = []
    d_out = []
    back_qkv = []
    d_experts = []
    for number in reversed(range(DECODER_LAYERS)):
        state, middle, mixer_in, own_gates, row_gates, dense, weights, memo, expert_memo = kept[
            number
        ]
        back, expert_grads = expert_backward(
            grad_gathered, picks[number], row_gates, weights, expert_memo, (first, second)
        )
        d_expert = [mine + swap(other) for mine, other in zip(*expert_grads)]
        d_expert[2] = d_expert[2].reshape(ff, width, share).transpose(1, 0, 2)
        d_experts.insert(0, [to_experts(part.reshape(width, -1, part.shape[-1])) for part in d_expert])
        back = scatter_chips(back, 5).astype(jnp.float32)
        grad_gates = (
            back[:, MODEL_WIDTH : MODEL_WIDTH + EXPERTS]
            + back[:, MODEL_WIDTH + EXPERTS : MODEL_WIDTH + 2 * EXPERTS]
        )
        grad_logits = (
            own_gates
            * (grad_gates - jnp.sum(own_gates * grad_gates, axis=1, keepdims=True))
        ).astype(jnp.bfloat16)
        grad_router = lax.dot_general(
            mixer_in, grad_logits, (((0,), (0,)), ((), ())), preferred_element_type=jnp.float32
        )
        grad_mixer = back[:, :MODEL_WIDTH] + lax.dot_general(
            grad_logits,
            routers[number],
            (((1,), (1,)), ((), ())),
            preferred_element_type=jnp.float32,
        )
        unused_mid, norm_back = jax.vjp(norm_rows, middle, g_ffn[number])
        grad_mid_part, grad_g_ffn = norm_back(grad_mixer)
        grad_middle = grad_state + grad_mid_part
        low = gather_chips(after(grad_middle.astype(jnp.bfloat16), *d_expert), 6, PLANE)
        grad_qkv, grad_wqkv, grad_wout, grad_gq, grad_gk = attention_backward(
            low, memo, dense, angles
        )
        d_out.insert(0, line_sum(*half_sum(grad_wout)).astype(jnp.float32))
        mine, other = half_sum(grad_wqkv)
        summed = line_sum(mine, other).reshape(width, short, qkv_columns)
        grad_normed = lax.dot_general(
            after(grad_qkv, other),
            dense[0],
            (((1,), (1,)), ((), ())),
            preferred_element_type=jnp.float32,
        ).astype(jnp.bfloat16)
        grad_normed = scatter_chips(grad_normed, 7, PLANE)
        grad_normed = by_place(grad_normed.astype(jnp.float32), width)
        unused_state, norm_front = jax.vjp(norm_rows, state, g_attn[number])
        grad_in_part, grad_g_attn = norm_front(grad_normed)
        grad_state = grad_middle + grad_in_part
        grad_low = grad_state.astype(jnp.bfloat16)
        if number > 0:
            grad_gathered = gather_chips(grad_low, 2)
        back_qkv.insert(
            0,
            swap_pieces(
                lambda to: lax.dynamic_index_in_dim(summed, to, 0, keepdims=False), place, width
            ),
        )
        gain_grads = jnp.concatenate([grad_g_attn, grad_g_ffn, grad_gq, grad_gk])
        small_grads.insert(0, (grad_router, gain_grads.reshape(devices, -1)))
    d_out = jnp.stack(d_out)
    d_gate, d_up, d_down = [
        jnp.stack([entry[i].astype(jnp.float32) for entry in d_experts]) for i in range(3)
    ]
    own_gains = jnp.concatenate([gain_grad for _, gain_grad in small_grads], axis=1)
    own_gains = jnp.pad(own_gains, ((0, 0), (0, gain_columns * short - gains.size)))
    side = jnp.concatenate(
        [router_grad for router_grad, _ in small_grads] + [own_gains.reshape(MODEL_WIDTH, -1)],
        axis=1,
    ).astype(jnp.bfloat16)
    side = jnp.pad(side, ((0, 0), (0, -side.shape[1] % 128)))
    side = scatter_chips(side, 4).astype(jnp.float32)
    small = lax.dynamic_slice_in_dim(side, core * short, short, 0) + swap(
        lax.dynamic_slice_in_dim(side, (1 - core) * short, short, 0)
    )
    d_router = jnp.stack(
        [small[:, number * EXPERTS : (number + 1) * EXPERTS] for number in range(DECODER_LAYERS)]
    )
    d_gains = small[:, router_columns : router_columns + gain_columns].reshape(-1)[: gains.size]
    d_gains = d_gains.reshape(gains.shape)
    d_qkv = jnp.zeros((DECODER_LAYERS, width, short, qkv_columns), jnp.bfloat16)
    for number in reversed(range(DECODER_LAYERS)):
        for origin, piece in back_qkv[number]:
            if number > 0:
                piece = after(piece, side)
            d_qkv = lax.dynamic_update_slice(d_qkv, piece[None, None], (number, origin, 0, 0))
    d_qkv = d_qkv.astype(jnp.float32)
    cut = group * HEAD_SIZE
    d_query = (
        d_qkv[..., :cut]
        .reshape(DECODER_LAYERS, width, short, 2, depth, HEAD_SIZE)
        .transpose(0, 2, 1, 4, 3, 5)
        .reshape(w_query.shape)
    )
    d_key = d_qkv[..., cut : cut + HEAD_SIZE].transpose(0, 2, 1, 3).reshape(key_weight.shape)
    d_value = d_qkv[..., cut + HEAD_SIZE :].transpose(0, 2, 1, 3).reshape(value_weight.shape)
    return (
        result,
        grad_low,
        d_gains,
        d_query,
        d_key,
        d_value,
        d_out,
        d_router,
        d_gate,
        d_up,
        d_down,
    )


def by_chip(mesh):
    grid = Mesh(
        mesh.devices.reshape(mesh.shape[FSDP], mesh.shape["expert"] // 2, 2),
        EVERY,
    )
    experts = (LINE, CORE)
    return jax.shard_map(
        chip_shards,
        mesh=grid,
        in_specs=(
            P(EVERY, None),
            P(EVERY, None),
            P(EVERY, None),
            P(None, EVERY, None),
            P(None, EVERY),
            P(None, EVERY, None),
            P(None, EVERY, None),
            P(None, EVERY, None),
            P(None, EVERY, None),
            P(None, EVERY, None),
            P(None, experts, FSDP, None),
            P(None, experts, FSDP, None),
            P(None, experts, None, FSDP),
        ),
        out_specs=(
            P(EVERY, None),
            P(EVERY, None),
            P(None, EVERY),
            P(None, EVERY, None),
            P(None, EVERY, None),
            P(None, EVERY, None),
            P(None, EVERY, None),
            P(None, EVERY, None),
            P(None, experts, FSDP, None),
            P(None, experts, FSDP, None),
            P(None, experts, None, FSDP),
        ),
        check_vma=False,
    )


def solution(mesh):
    width = mesh.shape[FSDP]
    peers = mesh.shape["expert"]
    if width == KEY_VALUE_HEADS == PAIR and peers * width == EXPERTS == QUERY_HEADS:
        return by_chip(mesh)
    return general(mesh)
```

```python
from functools import partial
import math

import jax
import jax.numpy as jnp
from jax import lax
from jax.experimental import pallas as pl
from jax.experimental.pallas import tpu as pltpu
from jax.sharding import Mesh
from jax.sharding import PartitionSpec as P

MODEL_WIDTH = 2048
QUERY_HEADS = 32
KEY_VALUE_HEADS = 4
HEAD_SIZE = 128
TOP = 8
EXPERTS = 32
DECODER_LAYERS = 2
CAP = 48


EPSILON = 1e-06
ROPE_BASE = 1000000.0


def norm_rows(operand, gain_vec):
    return (
        operand
        * lax.rsqrt(jnp.mean(operand * operand, axis=-1, keepdims=True) + EPSILON)
        * gain_vec
    )


def softmax_last(operand):
    shifted = operand - jnp.max(operand, axis=-1, keepdims=True)
    weights = jnp.exp(shifted)
    return weights / jnp.sum(weights, axis=-1, keepdims=True)


def rotate(operand, cosine, sine):
    half_size = operand.shape[-1] // 2
    front_half = operand[..., :half_size]
    back_half = operand[..., half_size:]
    return jnp.concatenate(
        [front_half * cosine - back_half * sine, back_half * cosine + front_half * sine], axis=-1
    )


def head_piece(query_pre, prerotation_key, g_query, g_key, cosine, sine):
    return (
        rotate(norm_rows(query_pre, g_query), cosine, sine),
        rotate(norm_rows(prerotation_key, g_key), cosine, sine),
    )


def geometry(lengths, local_rows):
    seq_ends = jnp.cumsum(lengths[0])
    seq_starts = seq_ends - lengths[0]
    offsets = jnp.arange(local_rows, dtype=jnp.int32)
    segment = jnp.sum((offsets[:, None] >= seq_ends[None, :]).astype(jnp.int32), axis=1)
    member = segment[:, None] == jnp.arange(seq_ends.shape[0], dtype=jnp.int32)[None, :]
    begins = jnp.sum(jnp.where(member, seq_starts[None, :], 0), axis=1)
    position = (offsets - begins).astype(jnp.float32)
    inverse = jnp.exp(
        -(2.0 * jnp.arange(HEAD_SIZE // 2, dtype=jnp.float32) / HEAD_SIZE) * math.log(ROPE_BASE)
    )
    angles = position[:, None] * inverse[None, :]
    allowed = (segment[:, None] == segment[None, :]) & (offsets[None, :] <= offsets[:, None])
    return (jnp.cos(angles)[:, None, :], jnp.sin(angles)[:, None, :], allowed)


def slot_table(route_rows):
    flat_routes = route_rows.reshape(-1)
    matches = (flat_routes[:, None] == jnp.arange(EXPERTS, dtype=jnp.int32)[None, :]).astype(
        jnp.int32
    )
    rank_in = jnp.sum((jnp.cumsum(matches, axis=0) - 1) * matches, axis=1)
    return flat_routes * CAP + rank_in


def split_gains(gain_vec):
    return (
        gain_vec[:MODEL_WIDTH],
        gain_vec[MODEL_WIDTH : 2 * MODEL_WIDTH],
        gain_vec[2 * MODEL_WIDTH : 2 * MODEL_WIDTH + HEAD_SIZE],
        gain_vec[2 * MODEL_WIDTH + HEAD_SIZE :],
    )


def score_block(query_copy, key_b, allowed):
    local_rows = query_copy.shape[0]
    grouped_rows = query_copy.reshape(
        local_rows, KEY_VALUE_HEADS, QUERY_HEADS // KEY_VALUE_HEADS, HEAD_SIZE
    )
    raw_scores = jnp.einsum(
        "tgjd,sgd->gjts", grouped_rows, key_b, preferred_element_type=jnp.float32
    ) * (1.0 / math.sqrt(HEAD_SIZE))
    return jnp.where(allowed[None, None], raw_scores, -1e30)


def layer_forward(state, dense, experts, route_rows, cosine, sine, allowed, peers):
    w_query, key_weight, value_weight, w_out, w_router, gain_raw = dense
    w_gate, w_up, w_down = experts
    local_rows = state.shape[0]
    experts_here = w_gate.shape[0]
    g_attn, g_ffn, g_query, g_key = split_gains(gain_raw.astype(jnp.float32))
    normalized_input = norm_rows(state, g_attn).astype(jnp.bfloat16)
    query_pre = jnp.dot(normalized_input, w_query, preferred_element_type=jnp.float32).reshape(
        local_rows, QUERY_HEADS, HEAD_SIZE
    )
    prerotation_key = jnp.dot(
        normalized_input, key_weight, preferred_element_type=jnp.float32
    ).reshape(local_rows, KEY_VALUE_HEADS, HEAD_SIZE)
    value_b = (
        jnp.dot(normalized_input, value_weight, preferred_element_type=jnp.float32)
        .astype(jnp.bfloat16)
        .reshape(local_rows, KEY_VALUE_HEADS, HEAD_SIZE)
    )
    query_f, key_f = head_piece(query_pre, prerotation_key, g_query, g_key, cosine, sine)
    query_copy = query_f.astype(jnp.bfloat16)
    key_b = key_f.astype(jnp.bfloat16)
    scores = score_block(query_copy, key_b, allowed)
    peaks = jnp.max(scores, axis=-1, keepdims=True)
    expos = jnp.exp(scores - peaks)
    totals = jnp.sum(expos, axis=-1, keepdims=True)
    log_total = peaks + jnp.log(totals)
    probs_b = (expos / totals).astype(jnp.bfloat16)
    attended = jnp.einsum("gjts,sgd->tgjd", probs_b, value_b, preferred_element_type=jnp.float32)
    attended = attended.reshape(local_rows, QUERY_HEADS * HEAD_SIZE).astype(jnp.bfloat16)
    middle = state + jnp.dot(attended, w_out, preferred_element_type=jnp.float32)
    mixer_in = norm_rows(middle, g_ffn).astype(jnp.bfloat16)
    logits = jnp.dot(mixer_in, w_router, preferred_element_type=jnp.float32)
    gates = softmax_last(jnp.take_along_axis(logits, route_rows, axis=1))
    slot_ids = slot_table(route_rows)
    outgoing = (
        jnp.zeros((EXPERTS * CAP, MODEL_WIDTH), jnp.bfloat16)
        .at[slot_ids]
        .set(jnp.repeat(mixer_in, TOP, axis=0))
    )
    incoming = lax.all_to_all(
        outgoing.reshape(peers, experts_here * CAP, MODEL_WIDTH),
        "expert",
        split_axis=0,
        concat_axis=0,
        tiled=True,
    )
    incoming = incoming.reshape(peers, experts_here, CAP, MODEL_WIDTH)
    gate_pre = jnp.einsum("secd,edf->secf", incoming, w_gate, preferred_element_type=jnp.float32)
    up_pre = jnp.einsum("secd,edf->secf", incoming, w_up, preferred_element_type=jnp.float32)
    hidden_b = (jax.nn.silu(gate_pre) * up_pre).astype(jnp.bfloat16)
    produced = jnp.einsum(
        "secf,efd->secd", hidden_b, w_down, preferred_element_type=jnp.float32
    ).astype(jnp.bfloat16)
    returned = lax.all_to_all(
        produced.reshape(peers, experts_here * CAP, MODEL_WIDTH),
        "expert",
        split_axis=0,
        concat_axis=0,
        tiled=True,
    )
    picked = returned.reshape(EXPERTS * CAP, MODEL_WIDTH)[slot_ids].reshape(
        local_rows, TOP, MODEL_WIDTH
    )
    new_state = middle + jnp.sum(gates[:, :, None] * picked.astype(jnp.float32), axis=1)
    memo = (
        state,
        normalized_input,
        query_pre,
        prerotation_key,
        query_copy,
        key_b,
        value_b,
        log_total,
        attended,
        middle,
        mixer_in,
        gates,
        slot_ids,
        picked,
        incoming,
        gate_pre,
        up_pre,
        hidden_b,
    )
    return (new_state, memo)


def layer_backward(grad_state, memo, dense, experts, route_rows, cosine, sine, allowed, peers):
    (
        state,
        normalized_input,
        query_pre,
        prerotation_key,
        query_copy,
        key_b,
        value_b,
        log_total,
        attended,
        middle,
        mixer_in,
        gates,
        slot_ids,
        picked,
        incoming,
        gate_pre,
        up_pre,
        hidden_b,
    ) = memo
    w_query, key_weight, value_weight, w_out, w_router, gain_raw = dense
    w_gate, w_up, w_down = experts
    local_rows = state.shape[0]
    experts_here = w_gate.shape[0]
    query_group_size = QUERY_HEADS // KEY_VALUE_HEADS
    scale = 1.0 / math.sqrt(HEAD_SIZE)
    g_attn, g_ffn, g_query, g_key = split_gains(gain_raw.astype(jnp.float32))
    grad_gates = jnp.sum(picked.astype(jnp.float32) * grad_state[:, None, :], axis=2)
    grad_chosen = gates * (grad_gates - jnp.sum(gates * grad_gates, axis=1, keepdims=True))
    choose = (route_rows[:, :, None] == jnp.arange(EXPERTS, dtype=jnp.int32)[None, None, :]).astype(
        jnp.float32
    )
    grad_logits = jnp.sum(choose * grad_chosen[:, :, None], axis=1).astype(jnp.bfloat16)
    grad_router = jnp.dot(mixer_in.T, grad_logits, preferred_element_type=jnp.float32)
    grad_mixer = jnp.dot(grad_logits, w_router.T, preferred_element_type=jnp.float32)
    grad_picked = (
        (gates[:, :, None] * grad_state[:, None, :])
        .astype(jnp.bfloat16)
        .reshape(local_rows * TOP, MODEL_WIDTH)
    )
    outgoing = jnp.zeros((EXPERTS * CAP, MODEL_WIDTH), jnp.bfloat16).at[slot_ids].set(grad_picked)
    grad_produced = lax.all_to_all(
        outgoing.reshape(peers, experts_here * CAP, MODEL_WIDTH),
        "expert",
        split_axis=0,
        concat_axis=0,
        tiled=True,
    )
    grad_produced = grad_produced.reshape(peers, experts_here, CAP, MODEL_WIDTH)
    grad_down = jnp.einsum(
        "secf,secd->efd", hidden_b, grad_produced, preferred_element_type=jnp.float32
    )
    grad_hidden = jnp.einsum(
        "secd,efd->secf", grad_produced, w_down, preferred_element_type=jnp.float32
    )
    sigmoid_gate = jax.nn.sigmoid(gate_pre)
    grad_gate_pre = (
        grad_hidden * up_pre * sigmoid_gate * (1.0 + gate_pre * (1.0 - sigmoid_gate))
    ).astype(jnp.bfloat16)
    grad_up_pre = (grad_hidden * gate_pre * sigmoid_gate).astype(jnp.bfloat16)
    grad_wgate = jnp.einsum(
        "secd,secf->edf", incoming, grad_gate_pre, preferred_element_type=jnp.float32
    )
    grad_wup = jnp.einsum(
        "secd,secf->edf", incoming, grad_up_pre, preferred_element_type=jnp.float32
    )
    grad_incoming = jnp.einsum(
        "secf,edf->secd", grad_gate_pre, w_gate, preferred_element_type=jnp.float32
    )
    grad_incoming = grad_incoming + jnp.einsum(
        "secf,edf->secd", grad_up_pre, w_up, preferred_element_type=jnp.float32
    )
    grad_incoming = grad_incoming.astype(jnp.bfloat16).reshape(
        peers, experts_here * CAP, MODEL_WIDTH
    )
    grad_returned = lax.all_to_all(
        grad_incoming, "expert", split_axis=0, concat_axis=0, tiled=True
    ).reshape(EXPERTS * CAP, MODEL_WIDTH)
    grad_mixer = grad_mixer + jnp.sum(
        grad_returned[slot_ids].reshape(local_rows, TOP, MODEL_WIDTH).astype(jnp.float32), axis=1
    )
    unused_mid, norm_back = jax.vjp(norm_rows, middle, g_ffn)
    grad_mid_part, grad_g_ffn = norm_back(grad_mixer)
    grad_middle = grad_state + grad_mid_part
    grad_middle_low = grad_middle.astype(jnp.bfloat16)
    grad_wout = jnp.dot(attended.T, grad_middle_low, preferred_element_type=jnp.float32)
    attended_gradient = jnp.dot(
        grad_middle_low, w_out.T, preferred_element_type=jnp.float32
    ).astype(jnp.bfloat16)
    attended_gradient = attended_gradient.reshape(
        local_rows, KEY_VALUE_HEADS, query_group_size, HEAD_SIZE
    )
    scores = score_block(query_copy, key_b, allowed)
    probs = jnp.exp(scores - log_total)
    probs_b = probs.astype(jnp.bfloat16)
    grad_probs = jnp.einsum(
        "tgjd,sgd->gjts", attended_gradient, value_b, preferred_element_type=jnp.float32
    )
    value_gradient = jnp.einsum(
        "gjts,tgjd->sgd", probs_b, attended_gradient, preferred_element_type=jnp.float32
    )
    value_gradient_copy = value_gradient.astype(jnp.bfloat16).reshape(
        local_rows, KEY_VALUE_HEADS * HEAD_SIZE
    )
    grad_scores = (
        probs * (grad_probs - jnp.sum(grad_probs * probs, axis=-1, keepdims=True))
    ).astype(jnp.bfloat16)
    grad_query = (
        jnp.einsum("gjts,sgd->tgjd", grad_scores, key_b, preferred_element_type=jnp.float32) * scale
    )
    query_grouped = query_copy.reshape(local_rows, KEY_VALUE_HEADS, query_group_size, HEAD_SIZE)
    grad_key = (
        jnp.einsum("gjts,tgjd->sgd", grad_scores, query_grouped, preferred_element_type=jnp.float32)
        * scale
    )
    unused_heads, head_back = jax.vjp(
        partial(head_piece, cosine=cosine, sine=sine), query_pre, prerotation_key, g_query, g_key
    )
    grad_qpre, prekey_gradient, grad_gq, grad_gk = head_back(
        (grad_query.reshape(local_rows, QUERY_HEADS, HEAD_SIZE), grad_key)
    )
    grad_qpre_b = grad_qpre.astype(jnp.bfloat16).reshape(local_rows, QUERY_HEADS * HEAD_SIZE)
    prekey_gradient_copy = prekey_gradient.astype(jnp.bfloat16).reshape(
        local_rows, KEY_VALUE_HEADS * HEAD_SIZE
    )
    grad_wquery = jnp.dot(normalized_input.T, grad_qpre_b, preferred_element_type=jnp.float32)
    grad_wkey = jnp.dot(
        normalized_input.T, prekey_gradient_copy, preferred_element_type=jnp.float32
    )
    grad_wvalue = jnp.dot(
        normalized_input.T, value_gradient_copy, preferred_element_type=jnp.float32
    )
    grad_normed = jnp.dot(grad_qpre_b, w_query.T, preferred_element_type=jnp.float32)
    grad_normed = grad_normed + jnp.dot(
        prekey_gradient_copy, key_weight.T, preferred_element_type=jnp.float32
    )
    grad_normed = grad_normed + jnp.dot(
        value_gradient_copy, value_weight.T, preferred_element_type=jnp.float32
    )
    unused_state, norm_front = jax.vjp(norm_rows, state, g_attn)
    grad_in_part, grad_g_attn = norm_front(grad_normed)
    grad_input = grad_middle + grad_in_part
    grad_gains = jnp.concatenate([grad_g_attn, grad_g_ffn, grad_gq, grad_gk])
    dense_grads = (grad_wquery, grad_wkey, grad_wvalue, grad_wout, grad_router, grad_gains)
    expert_grads = (grad_wgate, grad_wup, grad_down)
    return (grad_input, dense_grads, expert_grads)


def shards(
    tokens,
    cotangent,
    lengths,
    routes,
    gains,
    w_query,
    key_weight,
    value_weight,
    w_out,
    w_router,
    w_gate,
    w_up,
    w_down,
):
    local_rows = tokens.shape[0]
    peers = lax.axis_size("expert")
    cosine, sine, allowed = geometry(lengths, local_rows)
    state = tokens.astype(jnp.float32)
    memos = []
    for number in range(DECODER_LAYERS):
        dense = (
            lax.all_gather(w_query[number], ("fsdp", "expert"), axis=0, tiled=True),
            lax.all_gather(key_weight[number], ("fsdp", "expert"), axis=0, tiled=True),
            lax.all_gather(value_weight[number], ("fsdp", "expert"), axis=0, tiled=True),
            lax.all_gather(w_out[number], ("fsdp", "expert"), axis=0, tiled=True),
            lax.all_gather(w_router[number], ("fsdp", "expert"), axis=0, tiled=True),
            lax.all_gather(gains[number], ("fsdp", "expert"), axis=0, tiled=True),
        )
        experts = (
            lax.all_gather(w_gate[number], "fsdp", axis=1, tiled=True),
            lax.all_gather(w_up[number], "fsdp", axis=1, tiled=True),
            lax.all_gather(w_down[number], "fsdp", axis=2, tiled=True),
        )
        state, memo = layer_forward(
            state, dense, experts, routes[number], cosine, sine, allowed, peers
        )
        memos.append(memo)
    result = state.astype(jnp.bfloat16)
    grad_state = cotangent.astype(jnp.float32)
    dense_list = []
    expert_list = []
    for number in reversed(range(DECODER_LAYERS)):
        dense = (
            lax.all_gather(w_query[number], ("fsdp", "expert"), axis=0, tiled=True),
            lax.all_gather(key_weight[number], ("fsdp", "expert"), axis=0, tiled=True),
            lax.all_gather(value_weight[number], ("fsdp", "expert"), axis=0, tiled=True),
            lax.all_gather(w_out[number], ("fsdp", "expert"), axis=0, tiled=True),
            lax.all_gather(w_router[number], ("fsdp", "expert"), axis=0, tiled=True),
            lax.all_gather(gains[number], ("fsdp", "expert"), axis=0, tiled=True),
        )
        experts = (
            lax.all_gather(w_gate[number], "fsdp", axis=1, tiled=True),
            lax.all_gather(w_up[number], "fsdp", axis=1, tiled=True),
            lax.all_gather(w_down[number], "fsdp", axis=2, tiled=True),
        )
        grad_state, dense_grads, expert_grads = layer_backward(
            grad_state, memos[number], dense, experts, routes[number], cosine, sine, allowed, peers
        )
        dense_shards = (
            lax.psum_scatter(dense_grads[0], ("fsdp", "expert"), scatter_dimension=0, tiled=True),
            lax.psum_scatter(dense_grads[1], ("fsdp", "expert"), scatter_dimension=0, tiled=True),
            lax.psum_scatter(dense_grads[2], ("fsdp", "expert"), scatter_dimension=0, tiled=True),
            lax.psum_scatter(dense_grads[3], ("fsdp", "expert"), scatter_dimension=0, tiled=True),
            lax.psum_scatter(dense_grads[4], ("fsdp", "expert"), scatter_dimension=0, tiled=True),
            lax.psum_scatter(dense_grads[5], ("fsdp", "expert"), scatter_dimension=0, tiled=True),
        )
        expert_shards = (
            lax.psum_scatter(
                expert_grads[0].astype(jnp.bfloat16), "fsdp", scatter_dimension=1, tiled=True
            ).astype(jnp.float32),
            lax.psum_scatter(
                expert_grads[1].astype(jnp.bfloat16), "fsdp", scatter_dimension=1, tiled=True
            ).astype(jnp.float32),
            lax.psum_scatter(
                expert_grads[2].astype(jnp.bfloat16), "fsdp", scatter_dimension=2, tiled=True
            ).astype(jnp.float32),
        )
        dense_list.insert(0, dense_shards)
        expert_list.insert(0, expert_shards)
    d_gains = jnp.stack([entry[5] for entry in dense_list])
    d_query = jnp.stack([entry[0] for entry in dense_list])
    d_key = jnp.stack([entry[1] for entry in dense_list])
    d_value = jnp.stack([entry[2] for entry in dense_list])
    d_out = jnp.stack([entry[3] for entry in dense_list])
    d_router = jnp.stack([entry[4] for entry in dense_list])
    d_gate = jnp.stack([entry[0] for entry in expert_list])
    d_up = jnp.stack([entry[1] for entry in expert_list])
    d_down = jnp.stack([entry[2] for entry in expert_list])
    return (
        result,
        grad_state.astype(jnp.bfloat16),
        d_gains,
        d_query,
        d_key,
        d_value,
        d_out,
        d_router,
        d_gate,
        d_up,
        d_down,
    )


def general(mesh):
    return jax.shard_map(
        shards,
        mesh=mesh,
        in_specs=(
            P(("fsdp", "expert"), None),
            P(("fsdp", "expert"), None),
            P(("fsdp", "expert"), None),
            P(None, ("fsdp", "expert"), None),
            P(None, ("fsdp", "expert")),
            P(None, ("fsdp", "expert"), None),
            P(None, ("fsdp", "expert"), None),
            P(None, ("fsdp", "expert"), None),
            P(None, ("fsdp", "expert"), None),
            P(None, ("fsdp", "expert"), None),
            P(None, "expert", "fsdp", None),
            P(None, "expert", "fsdp", None),
            P(None, "expert", None, "fsdp"),
        ),
        out_specs=(
            P(("fsdp", "expert"), None),
            P(("fsdp", "expert"), None),
            P(None, ("fsdp", "expert")),
            P(None, ("fsdp", "expert"), None),
            P(None, ("fsdp", "expert"), None),
            P(None, ("fsdp", "expert"), None),
            P(None, ("fsdp", "expert"), None),
            P(None, ("fsdp", "expert"), None),
            P(None, "expert", "fsdp", None),
            P(None, "expert", "fsdp", None),
            P(None, "expert", None, "fsdp"),
        ),
        check_vma=False,
    )


FSDP, LINE, CORE = "fsdp", "line", "core"
CHIPS = (FSDP, LINE)
EVERY = (FSDP, LINE, CORE)
X, Y, ABOVE, BELOW = range(4)
GATE_COLUMNS = 128
PICK, SPREAD = "bst,btd->bsd", "bst,bsd->btd"


def swap(operand):
    return lax.ppermute(operand, CORE, [(0, 1), (1, 0)])


def by_core(core, mine, other, axis):
    return jnp.where(
        core == 0,
        jnp.concatenate([mine, other], axis=axis),
        jnp.concatenate([other, mine], axis=axis),
    )


def turned(operand):
    half_rows = operand.shape[0] // 2
    return jnp.concatenate([operand[half_rows:], operand[:half_rows]], axis=0)


def offload_gather(operand):
    return lax.all_gather(operand, CHIPS, axis=0, tiled=True)


PAIR = 4
ROW_UNITS = 8


ALL_CHIPS, PLANE, LINE_ONLY = range(3)


def routes_of_shards(grid, depth):
    depth = 1 if grid == PLANE else depth
    offsets = [s * k for k in range(1, depth) for s in (-1, 1)]

    def source(offset):
        return BELOW if offset < 0 else ABOVE

    def onward(offset):
        return ABOVE if offset < 0 else BELOW

    def further(offset):
        return offset - 1 if offset < 0 else offset + 1

    def line_hops(bits, first, last, offset):
        if depth == 1:
            return []
        if offset == 0:
            return [
                (ABOVE, first, last, (bits, -1, first, last, BELOW)),
                (BELOW, first, last, (bits, 1, first, last, ABOVE)),
            ]
        if abs(further(offset)) >= depth:
            return []
        return [(onward(offset), first, last, (bits, further(offset), first, last, source(offset)))]

    if grid == LINE_ONLY:
        return [(None, line_hops(0, 0, 8, 0))] + [
            ((0, offset, 0, 8, source(offset)), line_hops(0, 0, 8, offset)) for offset in offsets
        ]
    plan = []
    own = [(X, 0, 8, (1, 0, 0, 8, X)), (Y, 0, 8, (2, 0, 0, 8, Y))]
    plan.append((None, own + line_hops(0, 0, 8, 0)))
    plan.append(
        ((1, 0, 0, 8, X), [(Y, 3, 7, (3, 0, 3, 7, Y))] + line_hops(1, 6, 8, 0))
    )
    plan.append(
        (
            (2, 0, 0, 8, Y),
            [(X, 0, 3, (3, 0, 0, 3, X)), (X, 7, 8, (3, 0, 7, 8, X))]
            + line_hops(2, 6, 8, 0),
        )
    )

    def spread(offset):
        return (
            (0, offset, 0, 8, source(offset)),
            line_hops(0, 0, 8, offset)
            + [(X, 0, 6, (1, offset, 0, 6, X)), (Y, 0, 6, (2, offset, 0, 6, Y))],
        )

    def crossed(offset):
        return [
            ((1, offset, 0, 6, X), [(Y, 3, 6, (3, offset, 3, 6, Y))]),
            ((2, offset, 0, 6, Y), [(X, 0, 3, (3, offset, 0, 3, X))]),
        ]

    def lined(offset):
        return [
            ((bits, offset, 6, 8, source(offset)), line_hops(bits, 6, 8, offset))
            for bits in (1, 2, 3)
        ]

    def last(offset):
        return [((3, offset, 3, 6, Y), []), ((3, offset, 0, 3, X), [])]

    steps = [(-k, k) for k in range(1, depth)]
    plan += [spread(o) for pair in steps[:1] for o in pair]
    plan += [
        ((3, 0, 3, 7, Y), []),
        ((3, 0, 0, 3, X), []),
        ((3, 0, 7, 8, X), line_hops(3, 6, 8, 0)),
    ]
    for number, pair in enumerate(steps):
        for offset in pair:
            plan += crossed(offset)
        if number + 1 < len(steps):
            plan += [spread(o) for o in steps[number + 1]]
        for offset in pair:
            plan += lined(offset)
        for offset in pair:
            plan += last(offset)
    return plan


class Place:
    def __init__(self, grid, depth):
        self.grid = grid
        self.depth = depth
        self.pair = lax.axis_index(FSDP)
        self.line = lax.axis_index(LINE)
        self.core = lax.axis_index(CORE)
        x = lax.rem(self.pair, 2)
        y = lax.div(self.pair, 2)
        self.pairs = [
            self.pair,
            self.pair + 1 - 2 * x,
            self.pair + 2 - 4 * y,
            PAIR - 1 - self.pair,
        ]

    def shard(self, bits, offset):
        if self.grid == PLANE:
            return self.pairs[bits]
        if self.grid == LINE_ONLY:
            return self.line + offset
        return self.pairs[bits] * self.depth + self.line + offset

    def device(self, neighbour):
        if neighbour == X:
            return (self.pairs[1], self.line, self.core)
        if neighbour == Y:
            return (self.pairs[2], self.line, self.core)
        step = 1 if neighbour == ABOVE else -1
        return (self.pair, self.line + step, self.core)

    def holds(self, offset, neighbour=None):
        low, high = min(offset, 0), max(offset, 0)
        if neighbour == ABOVE:
            high = max(high, 1)
        if neighbour == BELOW:
            low = min(low, -1)
        tests = []
        if low < 0:
            tests.append(self.line >= -low)
        if high > 0:
            tests.append(self.line < self.depth - high)
        if not tests:
            return None
        return tests[0] if len(tests) == 1 else jnp.logical_and(tests[0], tests[1])

    def meet(self):
        barrier = pltpu.get_barrier_semaphore()
        neighbours = (() if self.grid == LINE_ONLY else (X, Y)) + (
            () if self.grid == PLANE else (ABOVE, BELOW)
        )
        for neighbour in neighbours:

            def greet(neighbour=neighbour):
                pl.semaphore_signal(
                    barrier,
                    inc=1,
                    device_id=self.device(neighbour),
                    device_id_type=pl.DeviceIdType.MESH,
                )

            when(self.holds(0, neighbour), greet)
        ends = 0
        if self.grid != PLANE:
            ends = (self.line == 0).astype(jnp.int32) + (self.line == self.depth - 1).astype(
                jnp.int32
            )
        pl.semaphore_wait(barrier, len(neighbours) - ends)


def when(test, action):
    if test is None:
        action()
    else:
        pl.when(test)(action)


def gather_steps(plan, here, x_ref, out_ref, own_sem, send_sems, recv_sems):
    number_of = {item: i for i, (item, _) in enumerate(plan)}
    unit = x_ref.shape[0] // ROW_UNITS
    own = pltpu.make_async_copy(x_ref, out_ref.at[here.shard(0, 0)], own_sem)
    sent = []
    steps = []

    def passing(bits, offset, neighbour, first, last, there, site, own_piece):
        rows = pl.ds(first * unit, (last - first) * unit)
        target = out_ref.at[here.shard(bits, offset), rows]
        return pltpu.make_async_remote_copy(
            src_ref=x_ref.at[rows] if own_piece else target,
            dst_ref=target,
            send_sem=send_sems.at[site],
            recv_sem=recv_sems.at[number_of[there]],
            device_id=here.device(neighbour),
            device_id_type=pl.DeviceIdType.MESH,
        )

    for item, hops in plan:
        bits, offset = (0, 0) if item is None else item[:2]

        def step(item=item, hops=hops, bits=bits, offset=offset, site=len(sent)):
            if item is None:
                own.start()
            else:
                piece = out_ref.at[
                    here.shard(bits, offset), pl.ds(item[2] * unit, (item[3] - item[2]) * unit)
                ]
                pltpu.make_async_remote_copy(
                    src_ref=piece,
                    dst_ref=piece,
                    send_sem=send_sems.at[0],
                    recv_sem=recv_sems.at[number_of[item]],
                    device_id=here.device(X),
                    device_id_type=pl.DeviceIdType.MESH,
                ).wait_recv()
            for hop, (neighbour, first, last, there) in enumerate(hops):
                when(
                    here.holds(0, neighbour) if neighbour in (ABOVE, BELOW) else None,
                    lambda n=neighbour, f=first, l=last, t=there, k=site + hop: passing(
                        bits, offset, n, f, l, t, k, item is None
                    ).start(),
                )

        steps.append(
            lambda step=step, item=item, offset=offset: when(
                None if item is None else here.holds(offset), step
            )
        )
        for neighbour, first, last, there in hops:
            sent.append((bits, offset, neighbour, first, last, there, len(sent), item is None))

    def finish():
        for one in sent:
            when(here.holds(one[1], one[2]), lambda one=one: passing(*one).wait_send())
        own.wait()

    return steps, finish


def gather_kernel(grid, depth, x_ref, out_ref, own_sem, send_sems, recv_sems):
    here = Place(grid, depth)
    here.meet()
    steps, finish = gather_steps(
        routes_of_shards(grid, depth), here, x_ref, out_ref, own_sem, send_sems, recv_sems
    )
    for step in steps:
        step()
    finish()


def count_plan(grid, depth):
    plan = routes_of_shards(grid, depth)
    return len(plan), sum(len(hops) for _, hops in plan)


def chips_in(grid, depth):
    return {ALL_CHIPS: PAIR * depth, PLANE: PAIR, LINE_ONLY: depth}[grid]


def gather_chips(operand, collective_id, grid=ALL_CHIPS):
    depth = lax.axis_size(LINE)
    items, hops = count_plan(grid, depth)
    chips = chips_in(grid, depth)
    rows, columns = operand.shape
    return pl.pallas_call(
        partial(gather_kernel, grid, depth),
        out_shape=jax.ShapeDtypeStruct((chips, rows, columns), operand.dtype),
        in_specs=[pl.BlockSpec(memory_space=pl.ANY)],
        out_specs=pl.BlockSpec(memory_space=pl.ANY),
        scratch_shapes=[
            pltpu.SemaphoreType.DMA,
            pltpu.SemaphoreType.DMA((hops,)),
            pltpu.SemaphoreType.DMA((items,)),
        ],
        compiler_params=pltpu.CompilerParams(collective_id=collective_id, has_side_effects=True),
        cost_estimate=pl.CostEstimate(
            flops=0, bytes_accessed=66 * chips * rows * columns, transcendentals=0
        ),
    )(operand).reshape(chips * rows, columns)


def scatter_kernel(grid, depth, x_ref, out_ref, sums, landed, own_sem, send_sems, recv_sems):
    plan = routes_of_shards(grid, depth)
    number_of = {item: i for i, (item, _) in enumerate(plan)}
    unit = x_ref.shape[1] // ROW_UNITS
    here = Place(grid, depth)
    own = pltpu.make_async_copy(x_ref, sums, own_sem)
    own.start()
    here.meet()
    own.wait()
    sites = {}
    start = 0
    for item, hops in plan:
        for neighbour, first, last, there in hops:
            sites[there] = (number_of[there] - 1, start)
            start += (last - first) * unit

    def total(shard, first, last, base):
        @pl.loop(0, (last - first) * unit // 16)
        def _(i):
            rows = pl.ds(first * unit + i * 16, 16)
            value = sums[shard, rows].astype(jnp.float32)
            value = value + landed[pl.ds(base + i * 16, 16)].astype(jnp.float32)
            sums[shard, rows] = value.astype(sums.dtype)

    def sending(item):
        bits, offset, first, last, neighbour = item
        sem, base = sites[item]
        size = (last - first) * unit
        return pltpu.make_async_remote_copy(
            src_ref=sums.at[here.shard(bits, offset), pl.ds(first * unit, size)],
            dst_ref=landed.at[pl.ds(base, size)],
            send_sem=send_sems.at[number_of[item]],
            recv_sem=recv_sems.at[sem],
            device_id=here.device(neighbour),
            device_id_type=pl.DeviceIdType.MESH,
        )

    for item, hops in reversed(plan):
        bits, offset = (0, 0) if item is None else item[:2]

        def step(item=item, hops=hops, bits=bits, offset=offset):
            for neighbour, first, last, there in hops:

                def take(first=first, last=last, there=there):
                    sem, base = sites[there]
                    size = (last - first) * unit
                    pltpu.make_async_remote_copy(
                        src_ref=landed.at[pl.ds(base, size)],
                        dst_ref=landed.at[pl.ds(base, size)],
                        send_sem=send_sems.at[0],
                        recv_sem=recv_sems.at[sem],
                        device_id=here.device(X),
                        device_id_type=pl.DeviceIdType.MESH,
                    ).wait_recv()
                    total(here.shard(bits, offset), first, last, base)

                when(
                    here.holds(0, neighbour) if neighbour in (ABOVE, BELOW) else None,
                    take,
                )
            if item is not None:
                sending(item).start()

        when(None if item is None else here.holds(offset), step)
    out_ref[...] = sums[here.shard(0, 0)]
    for item, hops in plan:
        if item is not None:
            when(here.holds(item[1]), lambda item=item: sending(item).wait_send())


def scatter_chips(operand, collective_id, grid=ALL_CHIPS):
    depth = lax.axis_size(LINE)
    chips = chips_in(grid, depth)
    items, hops = count_plan(grid, depth)
    rows, columns = operand.shape[0] // chips, operand.shape[1]
    landed = sum(
        (last - first) * rows // ROW_UNITS
        for _, row in routes_of_shards(grid, depth)
        for _, first, last, _ in row
    )
    return pl.pallas_call(
        partial(scatter_kernel, grid, depth),
        out_shape=jax.ShapeDtypeStruct((rows, columns), operand.dtype),
        in_specs=[pl.BlockSpec(memory_space=pl.ANY)],
        out_specs=pl.BlockSpec(memory_space=pltpu.VMEM),
        scratch_shapes=[
            pltpu.VMEM((chips, rows, columns), operand.dtype),
            pltpu.VMEM((landed, columns), operand.dtype),
            pltpu.SemaphoreType.DMA,
            pltpu.SemaphoreType.DMA((items,)),
            pltpu.SemaphoreType.DMA((hops,)),
        ],
        compiler_params=pltpu.CompilerParams(
            collective_id=collective_id, has_side_effects=True, vmem_limit_bytes=50 * 2**20
        ),
        cost_estimate=pl.CostEstimate(
            flops=0, bytes_accessed=66 * chips * rows * columns, transcendentals=0
        ),
    )(operand.reshape(chips, rows, columns))


def expert_work(x_ref, first, second, produced, out_ref, between):
    blocks, cap, tokens = first[0].shape
    ff = first[3].shape[0]
    group = PAIR
    count = group * cap

    @pl.loop(0, blocks // group)
    def _(g):
        at = pl.ds(pl.multiple_of(g * count, 16), count)
        for k, refs in enumerate((first, second)):
            pick_ref, gate_ref, up_gate_ref, down_ref, rows_ref, pre_ref, hidden_ref = refs

            for i in range(group):
                rows_ref[pl.ds(pl.multiple_of(g * count + i * cap, 16), cap)] = jnp.dot(
                    pick_ref[g * group + i],
                    x_ref[g * group + i],
                    preferred_element_type=jnp.float32,
                ).astype(jnp.bfloat16)
            pre = jnp.dot(rows_ref[at], up_gate_ref[...], preferred_element_type=jnp.float32)
            pre_ref[at] = pre.astype(pre_ref.dtype)
            gate_pre, up_pre = pre[:, :ff], pre[:, ff:]
            hidden = (gate_pre * (1.0 / (1.0 + jnp.exp(-gate_pre))) * up_pre).astype(jnp.bfloat16)
            hidden_ref[at] = hidden
            made = jnp.dot(hidden, down_ref[...], preferred_element_type=jnp.float32)
            produced[k] = (made * gate_ref[at]).astype(jnp.bfloat16)
        for i in range(group):
            total = None
            for k, refs in enumerate((first, second)):
                part = lax.dot_general(
                    refs[0][g * group + i],
                    produced[k, pl.ds(i * cap, cap)],
                    (((0,), (0,)), ((), ())),
                    preferred_element_type=jnp.float32,
                )
                total = part if total is None else total + part
            out_ref[g * group + i] = total.astype(jnp.bfloat16)
        for number, action in between:
            pl.when(g == number)(action)


def weights_kernel(layer, depth, working, gathering, *refs):
    refs = list(refs)

    def take(count):
        taken = refs[:count]
        del refs[:count]
        return taken

    w_gate, w_up, w_down, qkv_ref, w_out_ref = take(5)
    inputs = take(9) if working else []
    small_in = take(1) if gathering else []
    up_gate_refs = take(2)
    down_refs = take(2)
    dense_refs = take(2)
    outputs = take(7) if working else []
    small_out = take(1) if gathering else []
    own_sems, send_sems, recv_sems, side_send, side_recv, line_send, line_recv = take(7)
    here = Place(ALL_CHIPS, depth)
    share = w_gate.shape[2]
    ff = w_gate.shape[3]
    sibling = (here.pair, here.line, 1 - here.core)
    dense_sources = (qkv_ref, w_out_ref.at[layer])

    def device(bits):
        return (here.pairs[bits], here.line, here.core)

    def remote(source, target, send, recv, to):
        return pltpu.make_async_remote_copy(
            src_ref=source,
            dst_ref=target,
            send_sem=send,
            recv_sem=recv,
            device_id=to,
            device_id_type=pl.DeviceIdType.MESH,
        )

    barrier = pltpu.get_barrier_semaphore()
    greeted = [device(1), device(2), device(3), sibling]
    for to in greeted:
        pl.semaphore_signal(barrier, inc=1, device_id=to, device_id_type=pl.DeviceIdType.MESH)
    for neighbour in (ABOVE, BELOW):

        def greet(neighbour=neighbour):
            pl.semaphore_signal(
                barrier,
                inc=1,
                device_id=here.device(neighbour),
                device_id_type=pl.DeviceIdType.MESH,
            )

        when(here.holds(0, neighbour), greet)
    ends = (here.line == 0).astype(jnp.int32) + (here.line == depth - 1).astype(jnp.int32)
    pl.semaphore_wait(barrier, len(greeted) + 2 - ends)

    def shard(k, expert):
        return (w_gate, w_up, w_down)[k].at[layer, expert]

    def spot(which, k, origin):
        start = pl.ds(pl.multiple_of(origin * share, share), share)
        if k == 2:
            return down_refs[which].at[:, start]
        return up_gate_refs[which].at[start, pl.ds(k * ff, ff)]

    def across(bits, k):
        return remote(
            shard(k, here.pairs[bits]),
            spot(0, k, here.pair),
            send_sems.at[bits - 1, k],
            recv_sems.at[bits - 1, k],
            device(bits),
        )

    def beside(bits, k):
        source = shard(k, here.pair) if bits == 0 else spot(0, k, here.pairs[bits])
        return remote(
            source,
            spot(1, k, here.pairs[bits]),
            side_send.at[bits, k],
            side_recv.at[bits, k],
            sibling,
        )

    offsets = [0] + [s * k for k in range(1, depth) for s in (-1, 1)]

    def slab(k, offset):
        return dense_refs[k].at[here.core, here.line + offset]

    def along(k, offset, neighbour):
        number = offsets.index(offset)
        there = offset - 1 if neighbour == ABOVE else offset + 1
        return remote(
            dense_sources[k] if offset == 0 else slab(k, offset),
            slab(k, offset),
            line_send.at[k, number if offset else (0 if neighbour == ABOVE else len(offsets))],
            line_recv.at[k, offsets.index(there)],
            here.device(neighbour),
        )

    def dense_beside(k, offset):
        number = PAIR + offsets.index(offset)
        return remote(
            dense_sources[k] if offset == 0 else slab(k, offset),
            slab(k, offset),
            side_send.at[number, k],
            side_recv.at[number, k],
            sibling,
        )

    def dense_beside_landed(k, offset):
        number = PAIR + offsets.index(offset)
        target = dense_refs[k].at[1 - here.core, here.line + offset]
        return remote(target, target, side_send.at[number, k], side_recv.at[number, k], sibling)

    def onward(offset):
        neighbour = ABOVE if offset < 0 else BELOW
        return neighbour if abs(offset) + 1 < depth else None

    kept = [
        pltpu.make_async_copy(shard(k, here.pair), spot(0, k, here.pair), own_sems.at[k])
        for k in range(3)
    ] + [
        pltpu.make_async_copy(dense_sources[k], slab(k, 0), own_sems.at[3 + k]) for k in range(2)
    ]
    for k in range(2):
        for neighbour in (ABOVE, BELOW):
            when(here.holds(0, neighbour), lambda k=k, n=neighbour: along(k, 0, n).start())

    def send_across(k):
        for bits in (3, 1, 2):
            across(bits, k).start()

    if gathering:
        gather, gathered = gather_steps(
            routes_of_shards(ALL_CHIPS, depth), here, small_in[0], small_out[0], *refs
        )
        gather[0]()
    send_across(0)
    for copy in kept:
        copy.start()
    for k in range(3):
        beside(0, k).start()
    for k in range(2):
        dense_beside(k, 0).start()
    if gathering:
        for step in gather[1:]:
            step()
    for k in range(1, 3):
        send_across(k)
    def arrived(offset):
        for k in range(2):
            remote(
                slab(k, offset),
                slab(k, offset),
                line_send.at[k, 0],
                line_recv.at[k, offsets.index(offset)],
                sibling,
            ).wait_recv()
            neighbour = onward(offset)
            if neighbour is not None:
                when(
                    here.holds(0, neighbour),
                    lambda k=k, n=neighbour: along(k, offset, n).start(),
                )
            dense_beside(k, offset).start()

    def line_step(distance):
        for offset in offsets:
            if abs(offset) == distance:
                when(here.holds(offset), lambda offset=offset: arrived(offset))

    def crossed(k):
        for bits in (1, 2, 3):
            remote(
                spot(0, k, here.pairs[bits]),
                spot(0, k, here.pairs[bits]),
                send_sems.at[bits - 1, k],
                recv_sems.at[bits - 1, k],
                sibling,
            ).wait_recv()
            beside(bits, k).start()

    steps = [lambda distance=distance: line_step(distance) for distance in range(1, depth)]
    if working:
        x_ref, picks, gates, ups, downs = (
            inputs[0],
            inputs[1:3],
            inputs[3:5],
            inputs[5:7],
            inputs[7:9],
        )
        experts = [
            (picks[i], gates[i], ups[i], downs[i], outputs[i], outputs[2 + i], outputs[4 + i])
            for i in range(2)
        ]
        turns = x_ref.shape[0] // PAIR
        between = [(turns - len(steps) + i, step) for i, step in enumerate(steps)]
        expert_work(x_ref, *experts, refs[0], outputs[6], between)
    else:
        for step in steps:
            step()
    for k in range(3):
        crossed(k)
    for bits in range(PAIR):
        for k in range(3):
            beside(bits, k).wait_recv()
    for offset in offsets:

        def landed(offset=offset):
            for k in range(2):
                dense_beside_landed(k, offset).wait_recv()

        when(here.holds(offset), landed)
    for bits in (1, 2, 3):
        for k in range(3):
            across(bits, k).wait_send()
    for bits in range(PAIR):
        for k in range(3):
            beside(bits, k).wait_send()
    for offset in offsets:

        def left(offset=offset):
            for k in range(2):
                dense_beside(k, offset).wait_send()
                neighbours = (ABOVE, BELOW) if offset == 0 else (onward(offset),)
                for neighbour in neighbours:
                    if neighbour is not None:
                        when(
                            here.holds(0, neighbour),
                            lambda k=k, n=neighbour: along(k, offset, n).wait_send(),
                        )

        when(here.holds(offset), left)
    for copy in kept:
        copy.wait()
    if gathering:
        gathered()


def layer_weights(
    layer, w_gate, w_up, w_down, qkv_rows, w_out, collective_id, work=None, small=None
):
    depth = lax.axis_size(LINE)
    share, ff = w_gate.shape[2:]
    model = PAIR * share
    low = jnp.bfloat16
    shapes = [
        jax.ShapeDtypeStruct((model, 2 * ff), low),
        jax.ShapeDtypeStruct((model, 2 * ff), low),
        jax.ShapeDtypeStruct((ff, model), low),
        jax.ShapeDtypeStruct((ff, model), low),
        jax.ShapeDtypeStruct((2, depth) + qkv_rows.shape, low),
        jax.ShapeDtypeStruct((2, depth) + w_out.shape[1:], low),
    ]
    operands = [w_gate, w_up, w_down, qkv_rows, w_out]
    in_specs = [pl.BlockSpec(memory_space=pl.ANY)] * len(operands)
    out_specs = [pl.BlockSpec(memory_space=pl.ANY)] * len(shapes)
    offsets = 2 * depth - 1
    scratch = [
        pltpu.SemaphoreType.DMA((5,)),
        pltpu.SemaphoreType.DMA((3, 3)),
        pltpu.SemaphoreType.DMA((3, 3)),
        pltpu.SemaphoreType.DMA((PAIR + offsets, 3)),
        pltpu.SemaphoreType.DMA((PAIR + offsets, 3)),
        pltpu.SemaphoreType.DMA((2, offsets + 1)),
        pltpu.SemaphoreType.DMA((2, offsets)),
    ]
    if work is not None:
        gathered, picks, row_gates, weights = work
        blocks, cap, rows = picks[0].shape
        count = blocks * cap
        operands += [
            gathered.reshape(blocks, rows, model),
            *picks,
            *row_gates,
            weights[0][0],
            weights[1][0],
            weights[0][1],
            weights[1][1],
        ]
        in_specs += [pl.BlockSpec(memory_space=pltpu.VMEM)] * 9
        shapes += (
            [jax.ShapeDtypeStruct((count, model), low)] * 2
            + [jax.ShapeDtypeStruct((count, 2 * ff), low)] * 2
            + [jax.ShapeDtypeStruct((count, ff), low)] * 2
            + [jax.ShapeDtypeStruct((blocks, rows, model), low)]
        )
        out_specs += [pl.BlockSpec(memory_space=pltpu.VMEM)] * 7
        scratch.append(pltpu.VMEM((2, PAIR * cap, model), low))
    if small is not None:
        items, hops = count_plan(ALL_CHIPS, depth)
        operands.append(small)
        in_specs.append(pl.BlockSpec(memory_space=pl.ANY))
        shapes.append(jax.ShapeDtypeStruct((PAIR * depth,) + small.shape, small.dtype))
        out_specs.append(pl.BlockSpec(memory_space=pl.ANY))
        scratch += [
            pltpu.SemaphoreType.DMA,
            pltpu.SemaphoreType.DMA((hops,)),
            pltpu.SemaphoreType.DMA((items,)),
        ]
    made = pl.pallas_call(
        partial(weights_kernel, layer, depth, work is not None, small is not None),
        out_shape=shapes,
        in_specs=in_specs,
        out_specs=out_specs,
        scratch_shapes=scratch,
        compiler_params=pltpu.CompilerParams(
            collective_id=collective_id, has_side_effects=True, vmem_limit_bytes=58 * 2**20
        ),
        cost_estimate=pl.CostEstimate(flops=0, bytes_accessed=400 * 2**20, transcendentals=0),
    )(*operands)
    qkv = made[4].reshape(-1, qkv_rows.shape[1])
    out = made[5].reshape(-1, w_out.shape[2])
    return ((made[0], made[2]), (made[1], made[3])), qkv, out, made[6:]


def after(operand, *others):
    there = None
    for other in others:
        corner = other[(0,) * other.ndim].astype(jnp.float32)
        there = (corner == corner) if there is None else there & (corner == corner)
    return jnp.where(there, operand, jnp.zeros_like(operand))


def swap_pieces(piece_of, place, width):
    pieces = [(place, piece_of(place))]
    for step in range(1, width):
        sent = piece_of(place ^ step)
        got = lax.ppermute(sent, FSDP, [(i, i ^ step) for i in range(width)])
        pieces.append((place ^ step, got))
    return pieces


def block_scores(query_copy, key_b, allowed):
    return jnp.where(
        allowed[:, None],
        jnp.einsum("btjd,bsd->bjts", query_copy, key_b, preferred_element_type=jnp.float32)
        * (1.0 / math.sqrt(HEAD_SIZE)),
        -1e30,
    )


def by_owner(operand, width):
    rows = operand.shape[0]
    depth = lax.axis_size(LINE)
    return (
        operand.reshape(rows, width, depth, 2, -1).transpose(0, 3, 2, 1, 4).reshape(rows, -1)
    )


def by_place(operand, width):
    rows = operand.shape[0]
    depth = lax.axis_size(LINE)
    return (
        operand.reshape(rows, 2, depth, width, -1).transpose(0, 3, 2, 1, 4).reshape(rows, -1)
    )


def attention_forward(state, dense, angles):
    cosine, sine, allowed = angles
    w_qkv, w_out, normed, g_query, g_key = dense
    rows = state.shape[0]
    blocks = allowed.shape[0]
    heads = QUERY_HEADS // KEY_VALUE_HEADS
    cut = heads * HEAD_SIZE
    qkv = jnp.dot(normed, w_qkv, preferred_element_type=jnp.float32)
    query_pre = qkv[:, :cut].reshape(-1, heads, HEAD_SIZE)
    key_pre = qkv[:, cut : cut + HEAD_SIZE].reshape(-1, 1, HEAD_SIZE)
    value_b = qkv[:, cut + HEAD_SIZE :].astype(jnp.bfloat16).reshape(blocks, rows, HEAD_SIZE)
    query_f, key_f = head_piece(query_pre, key_pre, g_query, g_key, cosine, sine)
    query_b = query_f.astype(jnp.bfloat16).reshape(blocks, rows, heads, HEAD_SIZE)
    key_b = key_f.astype(jnp.bfloat16).reshape(blocks, rows, HEAD_SIZE)
    scores = block_scores(query_b, key_b, allowed)
    peaks = jnp.max(scores, axis=-1, keepdims=True)
    expos = jnp.exp(scores - peaks)
    totals = jnp.sum(expos, axis=-1, keepdims=True)
    log_total = peaks + jnp.log(totals)
    probs_b = (expos / totals).astype(jnp.bfloat16)
    attended = jnp.einsum("bjts,bsd->btjd", probs_b, value_b, preferred_element_type=jnp.float32)
    attended = attended.reshape(blocks * rows, cut).astype(jnp.bfloat16)
    partial_out = jnp.dot(attended, w_out, preferred_element_type=jnp.float32)
    middle = state + scatter_chips(partial_out.astype(jnp.bfloat16), 7, PLANE).astype(jnp.float32)
    return middle, (normed, query_pre, key_pre, query_b, key_b, value_b, log_total, attended)


def attention_backward(low, memo, dense, angles):
    cosine, sine, allowed = angles
    normed, query_pre, key_pre, query_b, key_b, value_b, log_total, attended = memo
    w_qkv, w_out, unused_normed, g_query, g_key = dense
    blocks, rows, heads, size = query_b.shape
    scale = 1.0 / math.sqrt(HEAD_SIZE)
    grad_attended = lax.dot_general(
        low, w_out, (((1,), (1,)), ((), ())), preferred_element_type=jnp.float32
    ).astype(jnp.bfloat16)
    grad_wout = lax.dot_general(
        attended, low, (((0,), (0,)), ((), ())), preferred_element_type=jnp.float32
    ).astype(jnp.bfloat16)
    grad_attended = grad_attended.reshape(query_b.shape)
    probs = jnp.exp(block_scores(query_b, key_b, allowed) - log_total)
    probs_b = probs.astype(jnp.bfloat16)
    grad_probs = jnp.einsum(
        "btjd,bsd->bjts", grad_attended, value_b, preferred_element_type=jnp.float32
    )
    grad_value = jnp.einsum(
        "bjts,btjd->bsd", probs_b, grad_attended, preferred_element_type=jnp.float32
    )
    grad_scores = (
        probs * (grad_probs - jnp.sum(grad_probs * probs, axis=-1, keepdims=True))
    ).astype(jnp.bfloat16)
    grad_query = (
        jnp.einsum("bjts,bsd->btjd", grad_scores, key_b, preferred_element_type=jnp.float32) * scale
    )
    grad_key = (
        jnp.einsum("bjts,btjd->bsd", grad_scores, query_b, preferred_element_type=jnp.float32)
        * scale
    )
    unused_heads, head_back = jax.vjp(
        partial(head_piece, cosine=cosine, sine=sine), query_pre, key_pre, g_query, g_key
    )
    grad_qpre, grad_kpre, grad_gq, grad_gk = head_back(
        (grad_query.reshape(query_pre.shape), grad_key.reshape(key_pre.shape))
    )
    grad_qkv = jnp.concatenate(
        [
            grad_qpre.astype(jnp.bfloat16).reshape(blocks * rows, heads * size),
            grad_kpre.astype(jnp.bfloat16).reshape(blocks * rows, size),
            grad_value.astype(jnp.bfloat16).reshape(blocks * rows, size),
        ],
        axis=1,
    )
    grad_wqkv = lax.dot_general(
        normed, grad_qkv, (((0,), (0,)), ((), ())), preferred_element_type=jnp.float32
    ).astype(jnp.bfloat16)
    return grad_qkv, grad_wqkv, grad_wout, grad_gq, grad_gk


def send_back(picks, pieces, waits=()):
    pick = jnp.concatenate(picks, axis=1)
    if waits:
        pick = after(pick, *waits)
    return (
        jnp.einsum(
            SPREAD,
            pick,
            jnp.concatenate(pieces, axis=1),
            preferred_element_type=jnp.float32,
        )
        .astype(jnp.bfloat16)
        .reshape(-1, pieces[0].shape[2])
    )


def expert_forward(gathered, picks, row_gates, weights):
    blocks = picks[0].shape[0]
    width = gathered.shape[1]
    grouped = gathered.reshape(blocks, -1, width)
    memo = []
    pieces = []
    for pick, row_gate, (w_up_gate, w_down) in zip(picks, row_gates, weights):
        ff = w_down.shape[0]
        rows = jnp.einsum(PICK, pick, grouped, preferred_element_type=jnp.float32)
        rows = rows.astype(jnp.bfloat16).reshape(-1, width)
        pre = jnp.dot(rows, w_up_gate, preferred_element_type=jnp.float32)
        gate_pre, up_pre = pre[:, :ff], pre[:, ff:]
        hidden = (jax.nn.silu(gate_pre) * up_pre).astype(jnp.bfloat16)
        produced = jnp.dot(hidden, w_down, preferred_element_type=jnp.float32)
        produced = (produced * row_gate).astype(jnp.bfloat16)
        pieces.append(produced.reshape(blocks, -1, width))
        memo.append((rows, pre, hidden))
    return send_back(picks, pieces), memo


def expert_backward(gathered, picks, row_gates, weights, memo, experts, waits):
    blocks = picks[0].shape[0]
    width = gathered.shape[1]
    grouped = gathered.reshape(blocks, -1, width)
    pieces = []
    grads = []
    for pick, row_gate, (w_up_gate, w_down), kept, expert in zip(
        picks, row_gates, weights, memo, experts
    ):
        rows, pre, hidden = kept
        ff = hidden.shape[1]
        gate_pre, up_pre = pre[:, :ff].astype(jnp.float32), pre[:, ff:].astype(jnp.float32)
        grad_rows = jnp.einsum(PICK, pick, grouped, preferred_element_type=jnp.float32)
        grad_rows = grad_rows.astype(jnp.bfloat16).reshape(-1, width)
        through = lax.dot_general(
            grad_rows, w_down, (((1,), (1,)), ((), ())), preferred_element_type=jnp.float32
        )
        hidden_f = hidden.astype(jnp.float32)
        gate_grad = jnp.sum(hidden_f * through, axis=1, keepdims=True)
        high = gate_grad.astype(jnp.bfloat16)
        low = (gate_grad - high.astype(jnp.float32)).astype(jnp.bfloat16)
        column = jnp.arange(GATE_COLUMNS, dtype=jnp.int32)[None, :]
        gate_part = jnp.where(
            column == expert, high, jnp.where(column == expert + EXPERTS, low, 0)
        )
        grad_hidden = through * row_gate
        sigmoid_gate = jax.nn.sigmoid(gate_pre)
        grad_gate_pre = (
            grad_hidden * up_pre * sigmoid_gate * (1.0 + gate_pre * (1.0 - sigmoid_gate))
        ).astype(jnp.bfloat16)
        grad_up_pre = (grad_hidden * gate_pre * sigmoid_gate).astype(jnp.bfloat16)
        grad_down = lax.dot_general(
            (hidden_f * row_gate).astype(jnp.bfloat16),
            grad_rows,
            (((0,), (0,)), ((), ())),
            preferred_element_type=jnp.float32,
        ).astype(jnp.bfloat16)
        grad_gate, grad_up = [
            lax.dot_general(
                rows, part, (((0,), (0,)), ((), ())), preferred_element_type=jnp.float32
            ).astype(jnp.bfloat16)
            for part in (grad_gate_pre, grad_up_pre)
        ]
        grad_in = lax.dot_general(
            jnp.concatenate([grad_gate_pre, grad_up_pre], axis=1),
            w_up_gate,
            (((1,), (1,)), ((), ())),
            preferred_element_type=jnp.float32,
        ).astype(jnp.bfloat16)
        piece = jnp.concatenate([grad_in, gate_part], axis=1)
        pieces.append(piece.reshape(blocks, -1, width + GATE_COLUMNS))
        grads.append((grad_gate, grad_up, grad_down))
    return send_back(picks, pieces, waits), grads


def chip_shards(
    tokens,
    cotangent,
    lengths,
    routes,
    gains,
    w_query,
    key_weight,
    value_weight,
    w_out,
    w_router,
    w_gate,
    w_up,
    w_down,
):
    rows = tokens.shape[0]
    width = lax.axis_size(FSDP)
    place = lax.axis_index(FSDP)
    line = lax.axis_index(LINE)
    core = lax.axis_index(CORE)
    devices = width * lax.axis_size(LINE) * 2
    chips = devices // 2
    chip = place * lax.axis_size(LINE) + line
    depth = lax.axis_size(LINE)
    group = QUERY_HEADS // KEY_VALUE_HEADS
    ff = w_gate.shape[3]
    short = w_query.shape[1]
    experts_here = w_gate.shape[1]
    gain_columns = -(-gains.size // short)
    side = jnp.concatenate(
        [w_router[number] for number in range(DECODER_LAYERS)]
        + [jnp.pad(gains.reshape(-1), (0, gain_columns * short - gains.size)).reshape(short, -1)],
        axis=1,
    )
    side = by_core(core, side, swap(side), 0)
    router_columns = DECODER_LAYERS * EXPERTS
    cut = side.shape[1]
    small = jnp.concatenate(
        [side]
        + [routes[number].astype(jnp.bfloat16) for number in range(DECODER_LAYERS)]
        + [jnp.broadcast_to(lengths.astype(jnp.bfloat16), (rows, lengths.shape[1]))],
        axis=1,
    )
    small = jnp.pad(small, ((0, 0), (0, -small.shape[1] % 128)))


    qkv_columns = (group + 2) * HEAD_SIZE

    def columns_of(number):
        return jnp.concatenate(
            [
                w_query[number]
                .reshape(short, width, depth, 2, HEAD_SIZE)
                .transpose(1, 0, 3, 2, 4)
                .reshape(width, short, group * HEAD_SIZE),
                key_weight[number].reshape(short, width, HEAD_SIZE).transpose(1, 0, 2),
                value_weight[number].reshape(short, width, HEAD_SIZE).transpose(1, 0, 2),
            ],
            axis=2,
        )

    columns = jnp.stack([columns_of(number) for number in range(DECODER_LAYERS)], axis=1)
    by_source = jnp.zeros_like(columns)
    for origin, piece in swap_pieces(
        lambda to: lax.dynamic_index_in_dim(columns, to, 0, keepdims=False), place, width
    ):
        by_source = lax.dynamic_update_index_in_dim(by_source, piece, origin, 0)

    def rows_by_source(number):
        return by_source[:, number].reshape(width * short, qkv_columns)

    def weights_of(number, work=None, beside=None):
        return layer_weights(
            number, w_gate, w_up, w_down, rows_by_source(number), w_out, 10 + number, work, beside
        )

    weights, qkv_whole, out_whole, made = weights_of(0, beside=small)
    small = made[0].reshape(chips * rows, -1)
    routers = [
        small[:, number * EXPERTS : (number + 1) * EXPERTS] for number in range(DECODER_LAYERS)
    ]
    all_gains = (
        small[:, router_columns:cut]
        .reshape(devices, -1)[:, : gains.size]
        .reshape(devices, DECODER_LAYERS, -1)
        .transpose(1, 0, 2)
        .reshape(DECODER_LAYERS, -1)
        .astype(jnp.float32)
    )
    all_routes = (
        small[:, cut : cut + DECODER_LAYERS * TOP]
        .reshape(chips, rows, DECODER_LAYERS, TOP)
        .transpose(0, 2, 1, 3)
    )
    cut = cut + DECODER_LAYERS * TOP
    all_lengths = (
        small.reshape(width, depth, rows, -1)[:, :, 0, cut : cut + lengths.shape[1]]
        .astype(jnp.int32)
    )
    all_lengths = lax.dynamic_index_in_dim(all_lengths, line, 1, keepdims=False)
    chosen = jnp.any(
        all_routes[..., None] == jnp.arange(EXPERTS, dtype=jnp.bfloat16), axis=3
    )
    chosen_f = chosen.astype(jnp.bfloat16)
    before = jnp.tril(jnp.ones((rows, rows), jnp.bfloat16), -1)
    ranks = jnp.einsum(
        "ts,clse->clte", before, chosen_f, preferred_element_type=jnp.float32
    )
    first = (line * 2 + core) * experts_here + place
    second = (line * 2 + (1 - core)) * experts_here + place
    slots = jnp.arange(CAP, dtype=jnp.float32)

    def pick_of(number, expert):
        named = lax.dynamic_index_in_dim(chosen[:, number], expert, 2, keepdims=False)
        rank = lax.dynamic_index_in_dim(ranks[:, number], expert, 2, keepdims=False)
        return (
            (rank[:, None, :] == slots[None, :, None]) & named[:, None, :]
        ).astype(jnp.bfloat16)

    picks = [(pick_of(number, first), pick_of(number, second)) for number in range(DECODER_LAYERS)]

    cosine, sine, allowed = jax.vmap(lambda own: geometry(own[None], rows))(all_lengths)
    angles = (
        cosine.reshape(width * rows, 1, -1),
        sine.reshape(width * rows, 1, -1),
        allowed,
    )
    g_attn, g_ffn, g_query, g_key = zip(*[split_gains(all_gains[i]) for i in range(DECODER_LAYERS)])

    share = MODEL_WIDTH // width

    def to_experts(part):
        return lax.all_to_all(part, FSDP, split_axis=0, concat_axis=0, tiled=True)

    state = tokens.astype(jnp.float32)
    kept = []
    for number in range(DECODER_LAYERS):
        normed = norm_rows(state, g_attn[number]).astype(jnp.bfloat16)
        normed = gather_chips(by_owner(normed, width), 6, PLANE)
        dense = (qkv_whole, out_whole, normed, g_query[number], g_key[number])
        middle, memo = attention_forward(state, dense, angles)
        mixer_in = norm_rows(middle, g_ffn[number]).astype(jnp.bfloat16)
        gathered = gather_chips(mixer_in, 2)
        if number == 0:
            cotangent_all = offload_gather(after(cotangent, gathered))
        logits = jnp.dot(gathered, routers[number], preferred_element_type=jnp.float32)
        named = chosen[:, number].reshape(chips * rows, EXPERTS)
        gates = softmax_last(jnp.where(named, logits, -1e30))
        row_gates = []
        for pick, expert in zip(picks[number], (first, second)):
            gate = lax.dynamic_index_in_dim(gates, expert, 1, keepdims=False)
            row_gates.append(
                jnp.sum(
                    pick.astype(jnp.float32) * gate.reshape(chips, 1, rows), axis=2
                ).reshape(-1, 1)
            )
        layer_experts = weights
        if number + 1 < DECODER_LAYERS:
            weights, qkv_whole, out_whole, made = weights_of(
                number + 1, (gathered, picks[number], row_gates, weights)
            )
            expert_memo = [(made[i], made[2 + i], made[4 + i]) for i in range(2)]
            produced = made[6].reshape(gathered.shape)
        else:
            produced, expert_memo = expert_forward(gathered, picks[number], row_gates, weights)
        new_state = middle + scatter_chips(produced, 3).astype(jnp.float32)
        own_gates = lax.dynamic_slice_in_dim(gates, chip * rows, rows, 0)
        kept.append(
            (state, middle, mixer_in, own_gates, row_gates, dense, layer_experts, memo, expert_memo)
        )
        state = new_state
    result = state.astype(jnp.bfloat16)

    def half_sum(operand):
        half = operand.shape[0] // 2
        mine = lax.dynamic_slice_in_dim(operand, core * half, half, 0)
        return mine, swap(lax.dynamic_slice_in_dim(operand, (1 - core) * half, half, 0))

    def line_sum(mine, other):
        return lax.psum_scatter(mine + other, LINE, scatter_dimension=0, tiled=True)

    def out_sum(mine, other):
        return line_sum(mine, other).astype(jnp.float32)

    def qkv_sum(mine, other):
        summed = line_sum(mine, other).reshape(width, short, qkv_columns)
        return swap_pieces(
            lambda to: lax.dynamic_index_in_dim(summed, to, 0, keepdims=False), place, width
        )

    grad_state = cotangent.astype(jnp.float32)
    grad_low = cotangent
    grad_gathered = cotangent_all
    small_grads = []
    d_out = []
    back_qkv = []
    d_experts = []
    earlier = []
    held = None
    for number in reversed(range(DECODER_LAYERS)):
        state, middle, mixer_in, own_gates, row_gates, dense, weights, memo, expert_memo = kept[
            number
        ]
        back, expert_grads = expert_backward(
            grad_gathered, picks[number], row_gates, weights, expert_memo, (first, second), earlier
        )
        d_expert = [mine + swap(other) for mine, other in zip(*expert_grads)]
        d_expert[2] = d_expert[2].reshape(ff, width, share).transpose(1, 0, 2)
        d_experts.insert(0, [to_experts(part.reshape(width, -1, part.shape[-1])) for part in d_expert])
        back_low = scatter_chips(back, 5)
        if held is not None:
            out_halves, qkv_halves = held
            d_out.insert(0, out_sum(after(out_halves[0], grad_gathered), out_halves[1]))
            back_qkv.insert(0, qkv_sum(after(qkv_halves[0], back_low), qkv_halves[1]))
        back = back_low.astype(jnp.float32)
        grad_gates = (
            back[:, MODEL_WIDTH : MODEL_WIDTH + EXPERTS]
            + back[:, MODEL_WIDTH + EXPERTS : MODEL_WIDTH + 2 * EXPERTS]
        )
        grad_logits = (
            own_gates
            * (grad_gates - jnp.sum(own_gates * grad_gates, axis=1, keepdims=True))
        ).astype(jnp.bfloat16)
        grad_router = lax.dot_general(
            mixer_in, grad_logits, (((0,), (0,)), ((), ())), preferred_element_type=jnp.float32
        )
        grad_mixer = back[:, :MODEL_WIDTH] + lax.dot_general(
            grad_logits,
            routers[number],
            (((1,), (1,)), ((), ())),
            preferred_element_type=jnp.float32,
        )
        unused_mid, norm_back = jax.vjp(norm_rows, middle, g_ffn[number])
        grad_mid_part, grad_g_ffn = norm_back(grad_mixer)
        grad_middle = grad_state + grad_mid_part
        low = gather_chips(
            after(grad_middle.astype(jnp.bfloat16), *d_expert), 6, PLANE
        )
        earlier = d_experts[0]
        grad_qkv, grad_wqkv, grad_wout, grad_gq, grad_gk = attention_backward(
            low, memo, dense, angles
        )
        held = half_sum(grad_wout), half_sum(grad_wqkv)
        other = held[1][1]
        if number == 0:
            d_out.insert(0, out_sum(*held[0]))
            back_qkv.insert(0, qkv_sum(*held[1]))
        grad_normed = lax.dot_general(
            after(grad_qkv, other),
            dense[0],
            (((1,), (1,)), ((), ())),
            preferred_element_type=jnp.float32,
        ).astype(jnp.bfloat16)
        grad_normed = scatter_chips(grad_normed, 7, PLANE)
        grad_normed = by_place(grad_normed.astype(jnp.float32), width)
        unused_state, norm_front = jax.vjp(norm_rows, state, g_attn[number])
        grad_in_part, grad_g_attn = norm_front(grad_normed)
        grad_state = grad_middle + grad_in_part
        grad_low = grad_state.astype(jnp.bfloat16)
        if number > 0:
            grad_gathered = gather_chips(grad_low, 2)
        gain_grads = jnp.concatenate([grad_g_attn, grad_g_ffn, grad_gq, grad_gk])
        small_grads.insert(0, (grad_router, gain_grads.reshape(devices, -1)))
    d_out = jnp.stack(d_out)
    d_gate, d_up, d_down = [
        jnp.stack([entry[i].astype(jnp.float32) for entry in d_experts]) for i in range(3)
    ]
    own_gains = jnp.concatenate([gain_grad for _, gain_grad in small_grads], axis=1)
    own_gains = jnp.pad(own_gains, ((0, 0), (0, gain_columns * short - gains.size)))
    side = jnp.concatenate(
        [router_grad for router_grad, _ in small_grads] + [own_gains.reshape(MODEL_WIDTH, -1)],
        axis=1,
    ).astype(jnp.bfloat16)
    side = jnp.pad(side, ((0, 0), (0, -side.shape[1] % 128)))
    side = scatter_chips(side, 4).astype(jnp.float32)
    small = lax.dynamic_slice_in_dim(side, core * short, short, 0) + swap(
        lax.dynamic_slice_in_dim(side, (1 - core) * short, short, 0)
    )
    d_router = jnp.stack(
        [small[:, number * EXPERTS : (number + 1) * EXPERTS] for number in range(DECODER_LAYERS)]
    )
    d_gains = small[:, router_columns : router_columns + gain_columns].reshape(-1)[: gains.size]
    d_gains = d_gains.reshape(gains.shape)
    d_qkv = jnp.zeros((DECODER_LAYERS, width, short, qkv_columns), jnp.bfloat16)
    for number in reversed(range(DECODER_LAYERS)):
        for origin, piece in back_qkv[number]:
            if number > 0:
                piece = after(piece, side)
            d_qkv = lax.dynamic_update_slice(d_qkv, piece[None, None], (number, origin, 0, 0))
    d_qkv = d_qkv.astype(jnp.float32)
    cut = group * HEAD_SIZE
    d_query = (
        d_qkv[..., :cut]
        .reshape(DECODER_LAYERS, width, short, 2, depth, HEAD_SIZE)
        .transpose(0, 2, 1, 4, 3, 5)
        .reshape(w_query.shape)
    )
    d_key = d_qkv[..., cut : cut + HEAD_SIZE].transpose(0, 2, 1, 3).reshape(key_weight.shape)
    d_value = d_qkv[..., cut + HEAD_SIZE :].transpose(0, 2, 1, 3).reshape(value_weight.shape)
    return (
        result,
        grad_low,
        d_gains,
        d_query,
        d_key,
        d_value,
        d_out,
        d_router,
        d_gate,
        d_up,
        d_down,
    )


def by_chip(mesh):
    grid = Mesh(
        mesh.devices.reshape(mesh.shape[FSDP], mesh.shape["expert"] // 2, 2),
        EVERY,
    )
    experts = (LINE, CORE)
    return jax.shard_map(
        chip_shards,
        mesh=grid,
        in_specs=(
            P(EVERY, None),
            P(EVERY, None),
            P(EVERY, None),
            P(None, EVERY, None),
            P(None, EVERY),
            P(None, EVERY, None),
            P(None, EVERY, None),
            P(None, EVERY, None),
            P(None, EVERY, None),
            P(None, EVERY, None),
            P(None, experts, FSDP, None),
            P(None, experts, FSDP, None),
            P(None, experts, None, FSDP),
        ),
        out_specs=(
            P(EVERY, None),
            P(EVERY, None),
            P(None, EVERY),
            P(None, EVERY, None),
            P(None, EVERY, None),
            P(None, EVERY, None),
            P(None, EVERY, None),
            P(None, EVERY, None),
            P(None, experts, FSDP, None),
            P(None, experts, FSDP, None),
            P(None, experts, None, FSDP),
        ),
        check_vma=False,
    )


def solution(mesh):
    width = mesh.shape[FSDP]
    peers = mesh.shape["expert"]
    if width == KEY_VALUE_HEADS == PAIR and peers * width == EXPERTS == QUERY_HEADS:
        return by_chip(mesh)
    return general(mesh)
```

```python
from functools import partial
import math

import jax
import jax.numpy as jnp
from jax import lax
from jax.experimental import pallas as pl
from jax.experimental.pallas import tpu as pltpu
from jax.sharding import Mesh
from jax.sharding import PartitionSpec as P

MODEL_WIDTH = 2048
QUERY_HEADS = 32
KEY_VALUE_HEADS = 4
HEAD_SIZE = 128
TOP = 8
EXPERTS = 32
DECODER_LAYERS = 2
CAP = 48


EPSILON = 1e-06
ROPE_BASE = 1000000.0


def norm_rows(operand, gain_vec):
    return (
        operand
        * lax.rsqrt(jnp.mean(operand * operand, axis=-1, keepdims=True) + EPSILON)
        * gain_vec
    )


def softmax_last(operand):
    shifted = operand - jnp.max(operand, axis=-1, keepdims=True)
    weights = jnp.exp(shifted)
    return weights / jnp.sum(weights, axis=-1, keepdims=True)


def rotate(operand, cosine, sine):
    half_size = operand.shape[-1] // 2
    front_half = operand[..., :half_size]
    back_half = operand[..., half_size:]
    return jnp.concatenate(
        [front_half * cosine - back_half * sine, back_half * cosine + front_half * sine], axis=-1
    )


def head_piece(query_pre, prerotation_key, g_query, g_key, cosine, sine):
    return (
        rotate(norm_rows(query_pre, g_query), cosine, sine),
        rotate(norm_rows(prerotation_key, g_key), cosine, sine),
    )


def geometry(lengths, local_rows):
    seq_ends = jnp.cumsum(lengths[0])
    seq_starts = seq_ends - lengths[0]
    offsets = jnp.arange(local_rows, dtype=jnp.int32)
    segment = jnp.sum((offsets[:, None] >= seq_ends[None, :]).astype(jnp.int32), axis=1)
    member = segment[:, None] == jnp.arange(seq_ends.shape[0], dtype=jnp.int32)[None, :]
    begins = jnp.sum(jnp.where(member, seq_starts[None, :], 0), axis=1)
    position = (offsets - begins).astype(jnp.float32)
    inverse = jnp.exp(
        -(2.0 * jnp.arange(HEAD_SIZE // 2, dtype=jnp.float32) / HEAD_SIZE) * math.log(ROPE_BASE)
    )
    angles = position[:, None] * inverse[None, :]
    allowed = (segment[:, None] == segment[None, :]) & (offsets[None, :] <= offsets[:, None])
    return (jnp.cos(angles)[:, None, :], jnp.sin(angles)[:, None, :], allowed)


def slot_table(route_rows):
    flat_routes = route_rows.reshape(-1)
    matches = (flat_routes[:, None] == jnp.arange(EXPERTS, dtype=jnp.int32)[None, :]).astype(
        jnp.int32
    )
    rank_in = jnp.sum((jnp.cumsum(matches, axis=0) - 1) * matches, axis=1)
    return flat_routes * CAP + rank_in


def split_gains(gain_vec):
    return (
        gain_vec[:MODEL_WIDTH],
        gain_vec[MODEL_WIDTH : 2 * MODEL_WIDTH],
        gain_vec[2 * MODEL_WIDTH : 2 * MODEL_WIDTH + HEAD_SIZE],
        gain_vec[2 * MODEL_WIDTH + HEAD_SIZE :],
    )


def score_block(query_copy, key_b, allowed):
    local_rows = query_copy.shape[0]
    grouped_rows = query_copy.reshape(
        local_rows, KEY_VALUE_HEADS, QUERY_HEADS // KEY_VALUE_HEADS, HEAD_SIZE
    )
    raw_scores = jnp.einsum(
        "tgjd,sgd->gjts", grouped_rows, key_b, preferred_element_type=jnp.float32
    ) * (1.0 / math.sqrt(HEAD_SIZE))
    return jnp.where(allowed[None, None], raw_scores, -1e30)


def layer_forward(state, dense, experts, route_rows, cosine, sine, allowed, peers):
    w_query, key_weight, value_weight, w_out, w_router, gain_raw = dense
    w_gate, w_up, w_down = experts
    local_rows = state.shape[0]
    experts_here = w_gate.shape[0]
    g_attn, g_ffn, g_query, g_key = split_gains(gain_raw.astype(jnp.float32))
    normalized_input = norm_rows(state, g_attn).astype(jnp.bfloat16)
    query_pre = jnp.dot(normalized_input, w_query, preferred_element_type=jnp.float32).reshape(
        local_rows, QUERY_HEADS, HEAD_SIZE
    )
    prerotation_key = jnp.dot(
        normalized_input, key_weight, preferred_element_type=jnp.float32
    ).reshape(local_rows, KEY_VALUE_HEADS, HEAD_SIZE)
    value_b = (
        jnp.dot(normalized_input, value_weight, preferred_element_type=jnp.float32)
        .astype(jnp.bfloat16)
        .reshape(local_rows, KEY_VALUE_HEADS, HEAD_SIZE)
    )
    query_f, key_f = head_piece(query_pre, prerotation_key, g_query, g_key, cosine, sine)
    query_copy = query_f.astype(jnp.bfloat16)
    key_b = key_f.astype(jnp.bfloat16)
    scores = score_block(query_copy, key_b, allowed)
    peaks = jnp.max(scores, axis=-1, keepdims=True)
    expos = jnp.exp(scores - peaks)
    totals = jnp.sum(expos, axis=-1, keepdims=True)
    log_total = peaks + jnp.log(totals)
    probs_b = (expos / totals).astype(jnp.bfloat16)
    attended = jnp.einsum("gjts,sgd->tgjd", probs_b, value_b, preferred_element_type=jnp.float32)
    attended = attended.reshape(local_rows, QUERY_HEADS * HEAD_SIZE).astype(jnp.bfloat16)
    middle = state + jnp.dot(attended, w_out, preferred_element_type=jnp.float32)
    mixer_in = norm_rows(middle, g_ffn).astype(jnp.bfloat16)
    logits = jnp.dot(mixer_in, w_router, preferred_element_type=jnp.float32)
    gates = softmax_last(jnp.take_along_axis(logits, route_rows, axis=1))
    slot_ids = slot_table(route_rows)
    outgoing = (
        jnp.zeros((EXPERTS * CAP, MODEL_WIDTH), jnp.bfloat16)
        .at[slot_ids]
        .set(jnp.repeat(mixer_in, TOP, axis=0))
    )
    incoming = lax.all_to_all(
        outgoing.reshape(peers, experts_here * CAP, MODEL_WIDTH),
        "expert",
        split_axis=0,
        concat_axis=0,
        tiled=True,
    )
    incoming = incoming.reshape(peers, experts_here, CAP, MODEL_WIDTH)
    gate_pre = jnp.einsum("secd,edf->secf", incoming, w_gate, preferred_element_type=jnp.float32)
    up_pre = jnp.einsum("secd,edf->secf", incoming, w_up, preferred_element_type=jnp.float32)
    hidden_b = (jax.nn.silu(gate_pre) * up_pre).astype(jnp.bfloat16)
    produced = jnp.einsum(
        "secf,efd->secd", hidden_b, w_down, preferred_element_type=jnp.float32
    ).astype(jnp.bfloat16)
    returned = lax.all_to_all(
        produced.reshape(peers, experts_here * CAP, MODEL_WIDTH),
        "expert",
        split_axis=0,
        concat_axis=0,
        tiled=True,
    )
    picked = returned.reshape(EXPERTS * CAP, MODEL_WIDTH)[slot_ids].reshape(
        local_rows, TOP, MODEL_WIDTH
    )
    new_state = middle + jnp.sum(gates[:, :, None] * picked.astype(jnp.float32), axis=1)
    memo = (
        state,
        normalized_input,
        query_pre,
        prerotation_key,
        query_copy,
        key_b,
        value_b,
        log_total,
        attended,
        middle,
        mixer_in,
        gates,
        slot_ids,
        picked,
        incoming,
        gate_pre,
        up_pre,
        hidden_b,
    )
    return (new_state, memo)


def layer_backward(grad_state, memo, dense, experts, route_rows, cosine, sine, allowed, peers):
    (
        state,
        normalized_input,
        query_pre,
        prerotation_key,
        query_copy,
        key_b,
        value_b,
        log_total,
        attended,
        middle,
        mixer_in,
        gates,
        slot_ids,
        picked,
        incoming,
        gate_pre,
        up_pre,
        hidden_b,
    ) = memo
    w_query, key_weight, value_weight, w_out, w_router, gain_raw = dense
    w_gate, w_up, w_down = experts
    local_rows = state.shape[0]
    experts_here = w_gate.shape[0]
    query_group_size = QUERY_HEADS // KEY_VALUE_HEADS
    scale = 1.0 / math.sqrt(HEAD_SIZE)
    g_attn, g_ffn, g_query, g_key = split_gains(gain_raw.astype(jnp.float32))
    grad_gates = jnp.sum(picked.astype(jnp.float32) * grad_state[:, None, :], axis=2)
    grad_chosen = gates * (grad_gates - jnp.sum(gates * grad_gates, axis=1, keepdims=True))
    choose = (route_rows[:, :, None] == jnp.arange(EXPERTS, dtype=jnp.int32)[None, None, :]).astype(
        jnp.float32
    )
    grad_logits = jnp.sum(choose * grad_chosen[:, :, None], axis=1).astype(jnp.bfloat16)
    grad_router = jnp.dot(mixer_in.T, grad_logits, preferred_element_type=jnp.float32)
    grad_mixer = jnp.dot(grad_logits, w_router.T, preferred_element_type=jnp.float32)
    grad_picked = (
        (gates[:, :, None] * grad_state[:, None, :])
        .astype(jnp.bfloat16)
        .reshape(local_rows * TOP, MODEL_WIDTH)
    )
    outgoing = jnp.zeros((EXPERTS * CAP, MODEL_WIDTH), jnp.bfloat16).at[slot_ids].set(grad_picked)
    grad_produced = lax.all_to_all(
        outgoing.reshape(peers, experts_here * CAP, MODEL_WIDTH),
        "expert",
        split_axis=0,
        concat_axis=0,
        tiled=True,
    )
    grad_produced = grad_produced.reshape(peers, experts_here, CAP, MODEL_WIDTH)
    grad_down = jnp.einsum(
        "secf,secd->efd", hidden_b, grad_produced, preferred_element_type=jnp.float32
    )
    grad_hidden = jnp.einsum(
        "secd,efd->secf", grad_produced, w_down, preferred_element_type=jnp.float32
    )
    sigmoid_gate = jax.nn.sigmoid(gate_pre)
    grad_gate_pre = (
        grad_hidden * up_pre * sigmoid_gate * (1.0 + gate_pre * (1.0 - sigmoid_gate))
    ).astype(jnp.bfloat16)
    grad_up_pre = (grad_hidden * gate_pre * sigmoid_gate).astype(jnp.bfloat16)
    grad_wgate = jnp.einsum(
        "secd,secf->edf", incoming, grad_gate_pre, preferred_element_type=jnp.float32
    )
    grad_wup = jnp.einsum(
        "secd,secf->edf", incoming, grad_up_pre, preferred_element_type=jnp.float32
    )
    grad_incoming = jnp.einsum(
        "secf,edf->secd", grad_gate_pre, w_gate, preferred_element_type=jnp.float32
    )
    grad_incoming = grad_incoming + jnp.einsum(
        "secf,edf->secd", grad_up_pre, w_up, preferred_element_type=jnp.float32
    )
    grad_incoming = grad_incoming.astype(jnp.bfloat16).reshape(
        peers, experts_here * CAP, MODEL_WIDTH
    )
    grad_returned = lax.all_to_all(
        grad_incoming, "expert", split_axis=0, concat_axis=0, tiled=True
    ).reshape(EXPERTS * CAP, MODEL_WIDTH)
    grad_mixer = grad_mixer + jnp.sum(
        grad_returned[slot_ids].reshape(local_rows, TOP, MODEL_WIDTH).astype(jnp.float32), axis=1
    )
    unused_mid, norm_back = jax.vjp(norm_rows, middle, g_ffn)
    grad_mid_part, grad_g_ffn = norm_back(grad_mixer)
    grad_middle = grad_state + grad_mid_part
    grad_middle_low = grad_middle.astype(jnp.bfloat16)
    grad_wout = jnp.dot(attended.T, grad_middle_low, preferred_element_type=jnp.float32)
    attended_gradient = jnp.dot(
        grad_middle_low, w_out.T, preferred_element_type=jnp.float32
    ).astype(jnp.bfloat16)
    attended_gradient = attended_gradient.reshape(
        local_rows, KEY_VALUE_HEADS, query_group_size, HEAD_SIZE
    )
    scores = score_block(query_copy, key_b, allowed)
    probs = jnp.exp(scores - log_total)
    probs_b = probs.astype(jnp.bfloat16)
    grad_probs = jnp.einsum(
        "tgjd,sgd->gjts", attended_gradient, value_b, preferred_element_type=jnp.float32
    )
    value_gradient = jnp.einsum(
        "gjts,tgjd->sgd", probs_b, attended_gradient, preferred_element_type=jnp.float32
    )
    value_gradient_copy = value_gradient.astype(jnp.bfloat16).reshape(
        local_rows, KEY_VALUE_HEADS * HEAD_SIZE
    )
    grad_scores = (
        probs * (grad_probs - jnp.sum(grad_probs * probs, axis=-1, keepdims=True))
    ).astype(jnp.bfloat16)
    grad_query = (
        jnp.einsum("gjts,sgd->tgjd", grad_scores, key_b, preferred_element_type=jnp.float32) * scale
    )
    query_grouped = query_copy.reshape(local_rows, KEY_VALUE_HEADS, query_group_size, HEAD_SIZE)
    grad_key = (
        jnp.einsum("gjts,tgjd->sgd", grad_scores, query_grouped, preferred_element_type=jnp.float32)
        * scale
    )
    unused_heads, head_back = jax.vjp(
        partial(head_piece, cosine=cosine, sine=sine), query_pre, prerotation_key, g_query, g_key
    )
    grad_qpre, prekey_gradient, grad_gq, grad_gk = head_back(
        (grad_query.reshape(local_rows, QUERY_HEADS, HEAD_SIZE), grad_key)
    )
    grad_qpre_b = grad_qpre.astype(jnp.bfloat16).reshape(local_rows, QUERY_HEADS * HEAD_SIZE)
    prekey_gradient_copy = prekey_gradient.astype(jnp.bfloat16).reshape(
        local_rows, KEY_VALUE_HEADS * HEAD_SIZE
    )
    grad_wquery = jnp.dot(normalized_input.T, grad_qpre_b, preferred_element_type=jnp.float32)
    grad_wkey = jnp.dot(
        normalized_input.T, prekey_gradient_copy, preferred_element_type=jnp.float32
    )
    grad_wvalue = jnp.dot(
        normalized_input.T, value_gradient_copy, preferred_element_type=jnp.float32
    )
    grad_normed = jnp.dot(grad_qpre_b, w_query.T, preferred_element_type=jnp.float32)
    grad_normed = grad_normed + jnp.dot(
        prekey_gradient_copy, key_weight.T, preferred_element_type=jnp.float32
    )
    grad_normed = grad_normed + jnp.dot(
        value_gradient_copy, value_weight.T, preferred_element_type=jnp.float32
    )
    unused_state, norm_front = jax.vjp(norm_rows, state, g_attn)
    grad_in_part, grad_g_attn = norm_front(grad_normed)
    grad_input = grad_middle + grad_in_part
    grad_gains = jnp.concatenate([grad_g_attn, grad_g_ffn, grad_gq, grad_gk])
    dense_grads = (grad_wquery, grad_wkey, grad_wvalue, grad_wout, grad_router, grad_gains)
    expert_grads = (grad_wgate, grad_wup, grad_down)
    return (grad_input, dense_grads, expert_grads)


def shards(
    tokens,
    cotangent,
    lengths,
    routes,
    gains,
    w_query,
    key_weight,
    value_weight,
    w_out,
    w_router,
    w_gate,
    w_up,
    w_down,
):
    local_rows = tokens.shape[0]
    peers = lax.axis_size("expert")
    cosine, sine, allowed = geometry(lengths, local_rows)
    state = tokens.astype(jnp.float32)
    memos = []
    for number in range(DECODER_LAYERS):
        dense = (
            lax.all_gather(w_query[number], ("fsdp", "expert"), axis=0, tiled=True),
            lax.all_gather(key_weight[number], ("fsdp", "expert"), axis=0, tiled=True),
            lax.all_gather(value_weight[number], ("fsdp", "expert"), axis=0, tiled=True),
            lax.all_gather(w_out[number], ("fsdp", "expert"), axis=0, tiled=True),
            lax.all_gather(w_router[number], ("fsdp", "expert"), axis=0, tiled=True),
            lax.all_gather(gains[number], ("fsdp", "expert"), axis=0, tiled=True),
        )
        experts = (
            lax.all_gather(w_gate[number], "fsdp", axis=1, tiled=True),
            lax.all_gather(w_up[number], "fsdp", axis=1, tiled=True),
            lax.all_gather(w_down[number], "fsdp", axis=2, tiled=True),
        )
        state, memo = layer_forward(
            state, dense, experts, routes[number], cosine, sine, allowed, peers
        )
        memos.append(memo)
    result = state.astype(jnp.bfloat16)
    grad_state = cotangent.astype(jnp.float32)
    dense_list = []
    expert_list = []
    for number in reversed(range(DECODER_LAYERS)):
        dense = (
            lax.all_gather(w_query[number], ("fsdp", "expert"), axis=0, tiled=True),
            lax.all_gather(key_weight[number], ("fsdp", "expert"), axis=0, tiled=True),
            lax.all_gather(value_weight[number], ("fsdp", "expert"), axis=0, tiled=True),
            lax.all_gather(w_out[number], ("fsdp", "expert"), axis=0, tiled=True),
            lax.all_gather(w_router[number], ("fsdp", "expert"), axis=0, tiled=True),
            lax.all_gather(gains[number], ("fsdp", "expert"), axis=0, tiled=True),
        )
        experts = (
            lax.all_gather(w_gate[number], "fsdp", axis=1, tiled=True),
            lax.all_gather(w_up[number], "fsdp", axis=1, tiled=True),
            lax.all_gather(w_down[number], "fsdp", axis=2, tiled=True),
        )
        grad_state, dense_grads, expert_grads = layer_backward(
            grad_state, memos[number], dense, experts, routes[number], cosine, sine, allowed, peers
        )
        dense_shards = (
            lax.psum_scatter(dense_grads[0], ("fsdp", "expert"), scatter_dimension=0, tiled=True),
            lax.psum_scatter(dense_grads[1], ("fsdp", "expert"), scatter_dimension=0, tiled=True),
            lax.psum_scatter(dense_grads[2], ("fsdp", "expert"), scatter_dimension=0, tiled=True),
            lax.psum_scatter(dense_grads[3], ("fsdp", "expert"), scatter_dimension=0, tiled=True),
            lax.psum_scatter(dense_grads[4], ("fsdp", "expert"), scatter_dimension=0, tiled=True),
            lax.psum_scatter(dense_grads[5], ("fsdp", "expert"), scatter_dimension=0, tiled=True),
        )
        expert_shards = (
            lax.psum_scatter(
                expert_grads[0].astype(jnp.bfloat16), "fsdp", scatter_dimension=1, tiled=True
            ).astype(jnp.float32),
            lax.psum_scatter(
                expert_grads[1].astype(jnp.bfloat16), "fsdp", scatter_dimension=1, tiled=True
            ).astype(jnp.float32),
            lax.psum_scatter(
                expert_grads[2].astype(jnp.bfloat16), "fsdp", scatter_dimension=2, tiled=True
            ).astype(jnp.float32),
        )
        dense_list.insert(0, dense_shards)
        expert_list.insert(0, expert_shards)
    d_gains = jnp.stack([entry[5] for entry in dense_list])
    d_query = jnp.stack([entry[0] for entry in dense_list])
    d_key = jnp.stack([entry[1] for entry in dense_list])
    d_value = jnp.stack([entry[2] for entry in dense_list])
    d_out = jnp.stack([entry[3] for entry in dense_list])
    d_router = jnp.stack([entry[4] for entry in dense_list])
    d_gate = jnp.stack([entry[0] for entry in expert_list])
    d_up = jnp.stack([entry[1] for entry in expert_list])
    d_down = jnp.stack([entry[2] for entry in expert_list])
    return (
        result,
        grad_state.astype(jnp.bfloat16),
        d_gains,
        d_query,
        d_key,
        d_value,
        d_out,
        d_router,
        d_gate,
        d_up,
        d_down,
    )


def general(mesh):
    return jax.shard_map(
        shards,
        mesh=mesh,
        in_specs=(
            P(("fsdp", "expert"), None),
            P(("fsdp", "expert"), None),
            P(("fsdp", "expert"), None),
            P(None, ("fsdp", "expert"), None),
            P(None, ("fsdp", "expert")),
            P(None, ("fsdp", "expert"), None),
            P(None, ("fsdp", "expert"), None),
            P(None, ("fsdp", "expert"), None),
            P(None, ("fsdp", "expert"), None),
            P(None, ("fsdp", "expert"), None),
            P(None, "expert", "fsdp", None),
            P(None, "expert", "fsdp", None),
            P(None, "expert", None, "fsdp"),
        ),
        out_specs=(
            P(("fsdp", "expert"), None),
            P(("fsdp", "expert"), None),
            P(None, ("fsdp", "expert")),
            P(None, ("fsdp", "expert"), None),
            P(None, ("fsdp", "expert"), None),
            P(None, ("fsdp", "expert"), None),
            P(None, ("fsdp", "expert"), None),
            P(None, ("fsdp", "expert"), None),
            P(None, "expert", "fsdp", None),
            P(None, "expert", "fsdp", None),
            P(None, "expert", None, "fsdp"),
        ),
        check_vma=False,
    )


FSDP, LINE, CORE = "fsdp", "line", "core"
CHIPS = (FSDP, LINE)
EVERY = (FSDP, LINE, CORE)
X, Y, ABOVE, BELOW = range(4)
GATE_COLUMNS = 128
PICK, SPREAD = "bst,btd->bsd", "bst,bsd->btd"


def swap(operand):
    return lax.ppermute(operand, CORE, [(0, 1), (1, 0)])


def by_core(core, mine, other, axis):
    return jnp.where(
        core == 0,
        jnp.concatenate([mine, other], axis=axis),
        jnp.concatenate([other, mine], axis=axis),
    )


def turned(operand):
    half_rows = operand.shape[0] // 2
    return jnp.concatenate([operand[half_rows:], operand[:half_rows]], axis=0)


def offload_gather(operand):
    return lax.all_gather(operand, CHIPS, axis=0, tiled=True)


PAIR = 4
ROW_UNITS = 8


ALL_CHIPS, PLANE, LINE_ONLY = range(3)


def routes_of_shards(grid, depth):
    depth = 1 if grid == PLANE else depth
    offsets = [s * k for k in range(1, depth) for s in (-1, 1)]

    def source(offset):
        return BELOW if offset < 0 else ABOVE

    def onward(offset):
        return ABOVE if offset < 0 else BELOW

    def further(offset):
        return offset - 1 if offset < 0 else offset + 1

    def line_hops(bits, first, last, offset):
        if depth == 1:
            return []
        if offset == 0:
            return [
                (ABOVE, first, last, (bits, -1, first, last, BELOW)),
                (BELOW, first, last, (bits, 1, first, last, ABOVE)),
            ]
        if abs(further(offset)) >= depth:
            return []
        return [(onward(offset), first, last, (bits, further(offset), first, last, source(offset)))]

    if grid == LINE_ONLY:
        return [(None, line_hops(0, 0, 8, 0))] + [
            ((0, offset, 0, 8, source(offset)), line_hops(0, 0, 8, offset)) for offset in offsets
        ]
    plan = []
    own = [(X, 0, 8, (1, 0, 0, 8, X)), (Y, 0, 8, (2, 0, 0, 8, Y))]
    plan.append((None, own + line_hops(0, 0, 8, 0)))
    plan.append(
        ((1, 0, 0, 8, X), [(Y, 3, 7, (3, 0, 3, 7, Y))] + line_hops(1, 6, 8, 0))
    )
    plan.append(
        (
            (2, 0, 0, 8, Y),
            [(X, 0, 3, (3, 0, 0, 3, X)), (X, 7, 8, (3, 0, 7, 8, X))]
            + line_hops(2, 6, 8, 0),
        )
    )

    def spread(offset):
        return (
            (0, offset, 0, 8, source(offset)),
            line_hops(0, 0, 8, offset)
            + [(X, 0, 6, (1, offset, 0, 6, X)), (Y, 0, 6, (2, offset, 0, 6, Y))],
        )

    def crossed(offset):
        return [
            ((1, offset, 0, 6, X), [(Y, 3, 6, (3, offset, 3, 6, Y))]),
            ((2, offset, 0, 6, Y), [(X, 0, 3, (3, offset, 0, 3, X))]),
        ]

    def lined(offset):
        return [
            ((bits, offset, 6, 8, source(offset)), line_hops(bits, 6, 8, offset))
            for bits in (1, 2, 3)
        ]

    def last(offset):
        return [((3, offset, 3, 6, Y), []), ((3, offset, 0, 3, X), [])]

    steps = [(-k, k) for k in range(1, depth)]
    plan += [spread(o) for pair in steps[:1] for o in pair]
    plan += [
        ((3, 0, 3, 7, Y), []),
        ((3, 0, 0, 3, X), []),
        ((3, 0, 7, 8, X), line_hops(3, 6, 8, 0)),
    ]
    for number, pair in enumerate(steps):
        for offset in pair:
            plan += crossed(offset)
        if number + 1 < len(steps):
            plan += [spread(o) for o in steps[number + 1]]
        for offset in pair:
            plan += lined(offset)
        for offset in pair:
            plan += last(offset)
    return plan


class Place:
    def __init__(self, grid, depth):
        self.grid = grid
        self.depth = depth
        self.pair = lax.axis_index(FSDP)
        self.line = lax.axis_index(LINE)
        self.core = lax.axis_index(CORE)
        x = lax.rem(self.pair, 2)
        y = lax.div(self.pair, 2)
        self.pairs = [
            self.pair,
            self.pair + 1 - 2 * x,
            self.pair + 2 - 4 * y,
            PAIR - 1 - self.pair,
        ]

    def shard(self, bits, offset):
        if self.grid == PLANE:
            return self.pairs[bits]
        if self.grid == LINE_ONLY:
            return self.line + offset
        return self.pairs[bits] * self.depth + self.line + offset

    def device(self, neighbour):
        if neighbour == X:
            return (self.pairs[1], self.line, self.core)
        if neighbour == Y:
            return (self.pairs[2], self.line, self.core)
        step = 1 if neighbour == ABOVE else -1
        return (self.pair, self.line + step, self.core)

    def holds(self, offset, neighbour=None):
        low, high = min(offset, 0), max(offset, 0)
        if neighbour == ABOVE:
            high = max(high, 1)
        if neighbour == BELOW:
            low = min(low, -1)
        tests = []
        if low < 0:
            tests.append(self.line >= -low)
        if high > 0:
            tests.append(self.line < self.depth - high)
        if not tests:
            return None
        return tests[0] if len(tests) == 1 else jnp.logical_and(tests[0], tests[1])

    def meet(self):
        barrier = pltpu.get_barrier_semaphore()
        neighbours = (() if self.grid == LINE_ONLY else (X, Y)) + (
            () if self.grid == PLANE else (ABOVE, BELOW)
        )
        for neighbour in neighbours:

            def greet(neighbour=neighbour):
                pl.semaphore_signal(
                    barrier,
                    inc=1,
                    device_id=self.device(neighbour),
                    device_id_type=pl.DeviceIdType.MESH,
                )

            when(self.holds(0, neighbour), greet)
        ends = 0
        if self.grid != PLANE:
            ends = (self.line == 0).astype(jnp.int32) + (self.line == self.depth - 1).astype(
                jnp.int32
            )
        pl.semaphore_wait(barrier, len(neighbours) - ends)


def when(test, action):
    if test is None:
        action()
    else:
        pl.when(test)(action)


def gather_steps(plan, here, x_ref, out_ref, own_sem, send_sems, recv_sems):
    number_of = {item: i for i, (item, _) in enumerate(plan)}
    unit = x_ref.shape[0] // ROW_UNITS
    own = pltpu.make_async_copy(x_ref, out_ref.at[here.shard(0, 0)], own_sem)
    sent = []
    steps = []

    def passing(bits, offset, neighbour, first, last, there, site, own_piece):
        rows = pl.ds(first * unit, (last - first) * unit)
        target = out_ref.at[here.shard(bits, offset), rows]
        return pltpu.make_async_remote_copy(
            src_ref=x_ref.at[rows] if own_piece else target,
            dst_ref=target,
            send_sem=send_sems.at[site],
            recv_sem=recv_sems.at[number_of[there]],
            device_id=here.device(neighbour),
            device_id_type=pl.DeviceIdType.MESH,
        )

    for item, hops in plan:
        bits, offset = (0, 0) if item is None else item[:2]

        def step(item=item, hops=hops, bits=bits, offset=offset, site=len(sent)):
            if item is None:
                own.start()
            else:
                piece = out_ref.at[
                    here.shard(bits, offset), pl.ds(item[2] * unit, (item[3] - item[2]) * unit)
                ]
                pltpu.make_async_remote_copy(
                    src_ref=piece,
                    dst_ref=piece,
                    send_sem=send_sems.at[0],
                    recv_sem=recv_sems.at[number_of[item]],
                    device_id=here.device(X),
                    device_id_type=pl.DeviceIdType.MESH,
                ).wait_recv()
            for hop, (neighbour, first, last, there) in enumerate(hops):
                when(
                    here.holds(0, neighbour) if neighbour in (ABOVE, BELOW) else None,
                    lambda n=neighbour, f=first, l=last, t=there, k=site + hop: passing(
                        bits, offset, n, f, l, t, k, item is None
                    ).start(),
                )

        steps.append(
            lambda step=step, item=item, offset=offset: when(
                None if item is None else here.holds(offset), step
            )
        )
        for neighbour, first, last, there in hops:
            sent.append((bits, offset, neighbour, first, last, there, len(sent), item is None))

    def finish():
        for one in sent:
            when(here.holds(one[1], one[2]), lambda one=one: passing(*one).wait_send())
        own.wait()

    return steps, finish


def gather_kernel(grid, depth, x_ref, out_ref, own_sem, send_sems, recv_sems):
    here = Place(grid, depth)
    here.meet()
    steps, finish = gather_steps(
        routes_of_shards(grid, depth), here, x_ref, out_ref, own_sem, send_sems, recv_sems
    )
    for step in steps:
        step()
    finish()


def count_plan(grid, depth):
    plan = routes_of_shards(grid, depth)
    return len(plan), sum(len(hops) for _, hops in plan)


def chips_in(grid, depth):
    return {ALL_CHIPS: PAIR * depth, PLANE: PAIR, LINE_ONLY: depth}[grid]


def gather_chips(operand, collective_id, grid=ALL_CHIPS):
    depth = lax.axis_size(LINE)
    items, hops = count_plan(grid, depth)
    chips = chips_in(grid, depth)
    rows, columns = operand.shape
    return pl.pallas_call(
        partial(gather_kernel, grid, depth),
        out_shape=jax.ShapeDtypeStruct((chips, rows, columns), operand.dtype),
        in_specs=[pl.BlockSpec(memory_space=pl.ANY)],
        out_specs=pl.BlockSpec(memory_space=pl.ANY),
        scratch_shapes=[
            pltpu.SemaphoreType.DMA,
            pltpu.SemaphoreType.DMA((hops,)),
            pltpu.SemaphoreType.DMA((items,)),
        ],
        compiler_params=pltpu.CompilerParams(collective_id=collective_id, has_side_effects=True),
        cost_estimate=pl.CostEstimate(
            flops=0, bytes_accessed=66 * chips * rows * columns, transcendentals=0
        ),
    )(operand).reshape(chips * rows, columns)


def scatter_kernel(grid, depth, x_ref, out_ref, sums, landed, own_sem, send_sems, recv_sems):
    plan = routes_of_shards(grid, depth)
    number_of = {item: i for i, (item, _) in enumerate(plan)}
    unit = x_ref.shape[1] // ROW_UNITS
    here = Place(grid, depth)
    own = pltpu.make_async_copy(x_ref, sums, own_sem)
    own.start()
    here.meet()
    own.wait()
    sites = {}
    start = 0
    for item, hops in plan:
        for neighbour, first, last, there in hops:
            sites[there] = (number_of[there] - 1, start)
            start += (last - first) * unit

    def total(shard, first, last, base):
        @pl.loop(0, (last - first) * unit // 16)
        def _(i):
            rows = pl.ds(first * unit + i * 16, 16)
            value = sums[shard, rows].astype(jnp.float32)
            value = value + landed[pl.ds(base + i * 16, 16)].astype(jnp.float32)
            sums[shard, rows] = value.astype(sums.dtype)

    def sending(item):
        bits, offset, first, last, neighbour = item
        sem, base = sites[item]
        size = (last - first) * unit
        return pltpu.make_async_remote_copy(
            src_ref=sums.at[here.shard(bits, offset), pl.ds(first * unit, size)],
            dst_ref=landed.at[pl.ds(base, size)],
            send_sem=send_sems.at[number_of[item]],
            recv_sem=recv_sems.at[sem],
            device_id=here.device(neighbour),
            device_id_type=pl.DeviceIdType.MESH,
        )

    for item, hops in reversed(plan):
        bits, offset = (0, 0) if item is None else item[:2]

        def step(item=item, hops=hops, bits=bits, offset=offset):
            for neighbour, first, last, there in hops:

                def take(first=first, last=last, there=there):
                    sem, base = sites[there]
                    size = (last - first) * unit
                    pltpu.make_async_remote_copy(
                        src_ref=landed.at[pl.ds(base, size)],
                        dst_ref=landed.at[pl.ds(base, size)],
                        send_sem=send_sems.at[0],
                        recv_sem=recv_sems.at[sem],
                        device_id=here.device(X),
                        device_id_type=pl.DeviceIdType.MESH,
                    ).wait_recv()
                    total(here.shard(bits, offset), first, last, base)

                when(
                    here.holds(0, neighbour) if neighbour in (ABOVE, BELOW) else None,
                    take,
                )
            if item is not None:
                sending(item).start()

        when(None if item is None else here.holds(offset), step)
    out_ref[...] = sums[here.shard(0, 0)]
    for item, hops in plan:
        if item is not None:
            when(here.holds(item[1]), lambda item=item: sending(item).wait_send())


def scatter_chips(operand, collective_id, grid=ALL_CHIPS):
    depth = lax.axis_size(LINE)
    chips = chips_in(grid, depth)
    items, hops = count_plan(grid, depth)
    rows, columns = operand.shape[0] // chips, operand.shape[1]
    landed = sum(
        (last - first) * rows // ROW_UNITS
        for _, row in routes_of_shards(grid, depth)
        for _, first, last, _ in row
    )
    return pl.pallas_call(
        partial(scatter_kernel, grid, depth),
        out_shape=jax.ShapeDtypeStruct((rows, columns), operand.dtype),
        in_specs=[pl.BlockSpec(memory_space=pl.ANY)],
        out_specs=pl.BlockSpec(memory_space=pltpu.VMEM),
        scratch_shapes=[
            pltpu.VMEM((chips, rows, columns), operand.dtype),
            pltpu.VMEM((landed, columns), operand.dtype),
            pltpu.SemaphoreType.DMA,
            pltpu.SemaphoreType.DMA((items,)),
            pltpu.SemaphoreType.DMA((hops,)),
        ],
        compiler_params=pltpu.CompilerParams(
            collective_id=collective_id, has_side_effects=True, vmem_limit_bytes=50 * 2**20
        ),
        cost_estimate=pl.CostEstimate(
            flops=0, bytes_accessed=66 * chips * rows * columns, transcendentals=0
        ),
    )(operand.reshape(chips, rows, columns))


def expert_work(x_ref, first, second, produced, out_ref, between):
    blocks, cap, tokens = first[0].shape
    ff = first[3].shape[0]
    group = PAIR
    count = group * cap

    @pl.loop(0, blocks // group)
    def _(g):
        at = pl.ds(pl.multiple_of(g * count, 16), count)
        for k, refs in enumerate((first, second)):
            pick_ref, gate_ref, up_gate_ref, down_ref, rows_ref, pre_ref, hidden_ref = refs

            for i in range(group):
                rows_ref[pl.ds(pl.multiple_of(g * count + i * cap, 16), cap)] = jnp.dot(
                    pick_ref[g * group + i],
                    x_ref[g * group + i],
                    preferred_element_type=jnp.float32,
                ).astype(jnp.bfloat16)
            pre = jnp.dot(rows_ref[at], up_gate_ref[...], preferred_element_type=jnp.float32)
            pre_ref[at] = pre.astype(pre_ref.dtype)
            gate_pre, up_pre = pre[:, :ff], pre[:, ff:]
            hidden = (gate_pre * (1.0 / (1.0 + jnp.exp(-gate_pre))) * up_pre).astype(jnp.bfloat16)
            hidden_ref[at] = hidden
            made = jnp.dot(hidden, down_ref[...], preferred_element_type=jnp.float32)
            produced[k] = (made * gate_ref[at]).astype(jnp.bfloat16)
        for i in range(group):
            total = None
            for k, refs in enumerate((first, second)):
                part = lax.dot_general(
                    refs[0][g * group + i],
                    produced[k, pl.ds(i * cap, cap)],
                    (((0,), (0,)), ((), ())),
                    preferred_element_type=jnp.float32,
                )
                total = part if total is None else total + part
            out_ref[g * group + i] = total.astype(jnp.bfloat16)
        for number, action in between:
            pl.when(g == number)(action)


def weights_kernel(layer, depth, working, gathering, *refs):
    refs = list(refs)

    def take(count):
        taken = refs[:count]
        del refs[:count]
        return taken

    w_gate, w_up, w_down, qkv_ref, w_out_ref = take(5)
    inputs = take(9) if working else []
    small_in = take(1) if gathering else []
    up_gate_refs = take(2)
    down_refs = take(2)
    dense_refs = take(2)
    outputs = take(7) if working else []
    small_out = take(1) if gathering else []
    own_sems, send_sems, recv_sems, side_send, side_recv, line_send, line_recv = take(7)
    here = Place(ALL_CHIPS, depth)
    share = w_gate.shape[2]
    ff = w_gate.shape[3]
    sibling = (here.pair, here.line, 1 - here.core)
    dense_sources = (qkv_ref, w_out_ref.at[layer])

    def device(bits):
        return (here.pairs[bits], here.line, here.core)

    def remote(source, target, send, recv, to):
        return pltpu.make_async_remote_copy(
            src_ref=source,
            dst_ref=target,
            send_sem=send,
            recv_sem=recv,
            device_id=to,
            device_id_type=pl.DeviceIdType.MESH,
        )

    barrier = pltpu.get_barrier_semaphore()
    greeted = [device(1), device(2), device(3), sibling]
    for to in greeted:
        pl.semaphore_signal(barrier, inc=1, device_id=to, device_id_type=pl.DeviceIdType.MESH)
    for neighbour in (ABOVE, BELOW):

        def greet(neighbour=neighbour):
            pl.semaphore_signal(
                barrier,
                inc=1,
                device_id=here.device(neighbour),
                device_id_type=pl.DeviceIdType.MESH,
            )

        when(here.holds(0, neighbour), greet)
    ends = (here.line == 0).astype(jnp.int32) + (here.line == depth - 1).astype(jnp.int32)
    pl.semaphore_wait(barrier, len(greeted) + 2 - ends)

    def shard(k, expert):
        return (w_gate, w_up, w_down)[k].at[layer, expert]

    def spot(which, k, origin):
        start = pl.ds(pl.multiple_of(origin * share, share), share)
        if k == 2:
            return down_refs[which].at[:, start]
        return up_gate_refs[which].at[start, pl.ds(k * ff, ff)]

    def across(bits, k):
        return remote(
            shard(k, here.pairs[bits]),
            spot(0, k, here.pair),
            send_sems.at[bits - 1, k],
            recv_sems.at[bits - 1, k],
            device(bits),
        )

    def beside(bits, k):
        source = shard(k, here.pair) if bits == 0 else spot(0, k, here.pairs[bits])
        return remote(
            source,
            spot(1, k, here.pairs[bits]),
            side_send.at[bits, k],
            side_recv.at[bits, k],
            sibling,
        )

    offsets = [0] + [s * k for k in range(1, depth) for s in (-1, 1)]

    def slab(k, offset):
        return dense_refs[k].at[here.core, here.line + offset]

    def along(k, offset, neighbour):
        number = offsets.index(offset)
        there = offset - 1 if neighbour == ABOVE else offset + 1
        return remote(
            dense_sources[k] if offset == 0 else slab(k, offset),
            slab(k, offset),
            line_send.at[k, number if offset else (0 if neighbour == ABOVE else len(offsets))],
            line_recv.at[k, offsets.index(there)],
            here.device(neighbour),
        )

    def dense_beside(k, offset):
        number = PAIR + offsets.index(offset)
        return remote(
            dense_sources[k] if offset == 0 else slab(k, offset),
            slab(k, offset),
            side_send.at[number, k],
            side_recv.at[number, k],
            sibling,
        )

    def dense_beside_landed(k, offset):
        number = PAIR + offsets.index(offset)
        target = dense_refs[k].at[1 - here.core, here.line + offset]
        return remote(target, target, side_send.at[number, k], side_recv.at[number, k], sibling)

    def onward(offset):
        neighbour = ABOVE if offset < 0 else BELOW
        return neighbour if abs(offset) + 1 < depth else None

    kept = [
        pltpu.make_async_copy(shard(k, here.pair), spot(0, k, here.pair), own_sems.at[k])
        for k in range(3)
    ] + [
        pltpu.make_async_copy(dense_sources[k], slab(k, 0), own_sems.at[3 + k]) for k in range(2)
    ]
    for k in range(2):
        for neighbour in (ABOVE, BELOW):
            when(here.holds(0, neighbour), lambda k=k, n=neighbour: along(k, 0, n).start())

    def send_across(k):
        for bits in (3, 1, 2):
            across(bits, k).start()

    if gathering:
        gather, gathered = gather_steps(
            routes_of_shards(ALL_CHIPS, depth), here, small_in[0], small_out[0], *refs
        )
        gather[0]()
    send_across(0)
    for copy in kept:
        copy.start()
    for k in range(3):
        beside(0, k).start()
    for k in range(2):
        dense_beside(k, 0).start()
    if gathering:
        for step in gather[1:]:
            step()
    for k in range(1, 3):
        send_across(k)
    def arrived(offset):
        for k in range(2):
            remote(
                slab(k, offset),
                slab(k, offset),
                line_send.at[k, 0],
                line_recv.at[k, offsets.index(offset)],
                sibling,
            ).wait_recv()
            neighbour = onward(offset)
            if neighbour is not None:
                when(
                    here.holds(0, neighbour),
                    lambda k=k, n=neighbour: along(k, offset, n).start(),
                )
            dense_beside(k, offset).start()

    def line_step(distance):
        for offset in offsets:
            if abs(offset) == distance:
                when(here.holds(offset), lambda offset=offset: arrived(offset))

    def crossed(k):
        for bits in (1, 2, 3):
            remote(
                spot(0, k, here.pairs[bits]),
                spot(0, k, here.pairs[bits]),
                send_sems.at[bits - 1, k],
                recv_sems.at[bits - 1, k],
                sibling,
            ).wait_recv()
            beside(bits, k).start()

    steps = [lambda distance=distance: line_step(distance) for distance in range(1, depth)]
    if working:
        x_ref, picks, gates, ups, downs = (
            inputs[0],
            inputs[1:3],
            inputs[3:5],
            inputs[5:7],
            inputs[7:9],
        )
        experts = [
            (picks[i], gates[i], ups[i], downs[i], outputs[i], outputs[2 + i], outputs[4 + i])
            for i in range(2)
        ]
        turns = x_ref.shape[0] // PAIR
        between = [(turns - len(steps) + i, step) for i, step in enumerate(steps)]
        expert_work(x_ref, *experts, refs[0], outputs[6], between)
    else:
        for step in steps:
            step()
    for k in range(3):
        crossed(k)
    for bits in range(PAIR):
        for k in range(3):
            beside(bits, k).wait_recv()
    for offset in offsets:

        def landed(offset=offset):
            for k in range(2):
                dense_beside_landed(k, offset).wait_recv()

        when(here.holds(offset), landed)
    for bits in (1, 2, 3):
        for k in range(3):
            across(bits, k).wait_send()
    for bits in range(PAIR):
        for k in range(3):
            beside(bits, k).wait_send()
    for offset in offsets:

        def left(offset=offset):
            for k in range(2):
                dense_beside(k, offset).wait_send()
                neighbours = (ABOVE, BELOW) if offset == 0 else (onward(offset),)
                for neighbour in neighbours:
                    if neighbour is not None:
                        when(
                            here.holds(0, neighbour),
                            lambda k=k, n=neighbour: along(k, offset, n).wait_send(),
                        )

        when(here.holds(offset), left)
    for copy in kept:
        copy.wait()
    if gathering:
        gathered()


def layer_weights(
    layer, w_gate, w_up, w_down, qkv_rows, w_out, collective_id, work=None, small=None
):
    depth = lax.axis_size(LINE)
    share, ff = w_gate.shape[2:]
    model = PAIR * share
    low = jnp.bfloat16
    shapes = [
        jax.ShapeDtypeStruct((model, 2 * ff), low),
        jax.ShapeDtypeStruct((model, 2 * ff), low),
        jax.ShapeDtypeStruct((ff, model), low),
        jax.ShapeDtypeStruct((ff, model), low),
        jax.ShapeDtypeStruct((2, depth) + qkv_rows.shape, low),
        jax.ShapeDtypeStruct((2, depth) + w_out.shape[1:], low),
    ]
    operands = [w_gate, w_up, w_down, qkv_rows, w_out]
    in_specs = [pl.BlockSpec(memory_space=pl.ANY)] * len(operands)
    out_specs = [pl.BlockSpec(memory_space=pl.ANY)] * len(shapes)
    offsets = 2 * depth - 1
    scratch = [
        pltpu.SemaphoreType.DMA((5,)),
        pltpu.SemaphoreType.DMA((3, 3)),
        pltpu.SemaphoreType.DMA((3, 3)),
        pltpu.SemaphoreType.DMA((PAIR + offsets, 3)),
        pltpu.SemaphoreType.DMA((PAIR + offsets, 3)),
        pltpu.SemaphoreType.DMA((2, offsets + 1)),
        pltpu.SemaphoreType.DMA((2, offsets)),
    ]
    if work is not None:
        gathered, picks, row_gates, weights = work
        blocks, cap, rows = picks[0].shape
        count = blocks * cap
        operands += [
            gathered.reshape(blocks, rows, model),
            *picks,
            *row_gates,
            weights[0][0],
            weights[1][0],
            weights[0][1],
            weights[1][1],
        ]
        in_specs += [pl.BlockSpec(memory_space=pltpu.VMEM)] * 9
        shapes += (
            [jax.ShapeDtypeStruct((count, model), low)] * 2
            + [jax.ShapeDtypeStruct((count, 2 * ff), low)] * 2
            + [jax.ShapeDtypeStruct((count, ff), low)] * 2
            + [jax.ShapeDtypeStruct((blocks, rows, model), low)]
        )
        out_specs += [pl.BlockSpec(memory_space=pltpu.VMEM)] * 7
        scratch.append(pltpu.VMEM((2, PAIR * cap, model), low))
    if small is not None:
        items, hops = count_plan(ALL_CHIPS, depth)
        operands.append(small)
        in_specs.append(pl.BlockSpec(memory_space=pl.ANY))
        shapes.append(jax.ShapeDtypeStruct((PAIR * depth,) + small.shape, small.dtype))
        out_specs.append(pl.BlockSpec(memory_space=pl.ANY))
        scratch += [
            pltpu.SemaphoreType.DMA,
            pltpu.SemaphoreType.DMA((hops,)),
            pltpu.SemaphoreType.DMA((items,)),
        ]
    made = pl.pallas_call(
        partial(weights_kernel, layer, depth, work is not None, small is not None),
        out_shape=shapes,
        in_specs=in_specs,
        out_specs=out_specs,
        scratch_shapes=scratch,
        compiler_params=pltpu.CompilerParams(
            collective_id=collective_id, has_side_effects=True, vmem_limit_bytes=58 * 2**20
        ),
        cost_estimate=pl.CostEstimate(flops=0, bytes_accessed=400 * 2**20, transcendentals=0),
    )(*operands)
    qkv = made[4].reshape(-1, qkv_rows.shape[1])
    out = made[5].reshape(-1, w_out.shape[2])
    return ((made[0], made[2]), (made[1], made[3])), qkv, out, made[6:]


def after(operand, *others):
    there = None
    for other in others:
        corner = other[(0,) * other.ndim].astype(jnp.float32)
        there = (corner == corner) if there is None else there & (corner == corner)
    return jnp.where(there, operand, jnp.zeros_like(operand))


def swap_pieces(piece_of, place, width):
    pieces = [(place, piece_of(place))]
    for step in range(1, width):
        sent = piece_of(place ^ step)
        got = lax.ppermute(sent, FSDP, [(i, i ^ step) for i in range(width)])
        pieces.append((place ^ step, got))
    return pieces


def block_scores(query_copy, key_b, allowed):
    return jnp.where(
        allowed[:, None],
        jnp.einsum("btjd,bsd->bjts", query_copy, key_b, preferred_element_type=jnp.float32)
        * (1.0 / math.sqrt(HEAD_SIZE)),
        -1e30,
    )


def by_owner(operand, width):
    rows = operand.shape[0]
    depth = lax.axis_size(LINE)
    return (
        operand.reshape(rows, width, depth, 2, -1).transpose(0, 3, 2, 1, 4).reshape(rows, -1)
    )


def by_place(operand, width):
    rows = operand.shape[0]
    depth = lax.axis_size(LINE)
    return (
        operand.reshape(rows, 2, depth, width, -1).transpose(0, 3, 2, 1, 4).reshape(rows, -1)
    )


def attention_forward(state, dense, angles):
    cosine, sine, allowed = angles
    w_qkv, w_out, normed, g_query, g_key = dense
    rows = state.shape[0]
    blocks = allowed.shape[0]
    heads = QUERY_HEADS // KEY_VALUE_HEADS
    cut = heads * HEAD_SIZE
    qkv = jnp.dot(normed, w_qkv, preferred_element_type=jnp.float32)
    query_pre = qkv[:, :cut].reshape(-1, heads, HEAD_SIZE)
    key_pre = qkv[:, cut : cut + HEAD_SIZE].reshape(-1, 1, HEAD_SIZE)
    value_b = qkv[:, cut + HEAD_SIZE :].astype(jnp.bfloat16).reshape(blocks, rows, HEAD_SIZE)
    query_f, key_f = head_piece(query_pre, key_pre, g_query, g_key, cosine, sine)
    query_b = query_f.astype(jnp.bfloat16).reshape(blocks, rows, heads, HEAD_SIZE)
    key_b = key_f.astype(jnp.bfloat16).reshape(blocks, rows, HEAD_SIZE)
    scores = block_scores(query_b, key_b, allowed)
    peaks = jnp.max(scores, axis=-1, keepdims=True)
    expos = jnp.exp(scores - peaks)
    totals = jnp.sum(expos, axis=-1, keepdims=True)
    log_total = peaks + jnp.log(totals)
    probs_b = (expos / totals).astype(jnp.bfloat16)
    attended = jnp.einsum("bjts,bsd->btjd", probs_b, value_b, preferred_element_type=jnp.float32)
    attended = attended.reshape(blocks * rows, cut).astype(jnp.bfloat16)
    partial_out = jnp.dot(attended, w_out, preferred_element_type=jnp.float32)
    middle = state + scatter_chips(partial_out.astype(jnp.bfloat16), 7, PLANE).astype(jnp.float32)
    return middle, (normed, query_pre, key_pre, query_b, key_b, value_b, log_total, attended)


def attention_backward(low, memo, dense, angles):
    cosine, sine, allowed = angles
    normed, query_pre, key_pre, query_b, key_b, value_b, log_total, attended = memo
    w_qkv, w_out, unused_normed, g_query, g_key = dense
    blocks, rows, heads, size = query_b.shape
    scale = 1.0 / math.sqrt(HEAD_SIZE)
    grad_attended = lax.dot_general(
        low, w_out, (((1,), (1,)), ((), ())), preferred_element_type=jnp.float32
    ).astype(jnp.bfloat16)
    grad_wout = lax.dot_general(
        attended, low, (((0,), (0,)), ((), ())), preferred_element_type=jnp.float32
    ).astype(jnp.bfloat16)
    grad_attended = grad_attended.reshape(query_b.shape)
    probs = jnp.exp(block_scores(query_b, key_b, allowed) - log_total)
    probs_b = probs.astype(jnp.bfloat16)
    grad_probs = jnp.einsum(
        "btjd,bsd->bjts", grad_attended, value_b, preferred_element_type=jnp.float32
    )
    grad_value = jnp.einsum(
        "bjts,btjd->bsd", probs_b, grad_attended, preferred_element_type=jnp.float32
    )
    grad_scores = (
        probs * (grad_probs - jnp.sum(grad_probs * probs, axis=-1, keepdims=True))
    ).astype(jnp.bfloat16)
    grad_query = (
        jnp.einsum("bjts,bsd->btjd", grad_scores, key_b, preferred_element_type=jnp.float32) * scale
    )
    grad_key = (
        jnp.einsum("bjts,btjd->bsd", grad_scores, query_b, preferred_element_type=jnp.float32)
        * scale
    )
    unused_heads, head_back = jax.vjp(
        partial(head_piece, cosine=cosine, sine=sine), query_pre, key_pre, g_query, g_key
    )
    grad_qpre, grad_kpre, grad_gq, grad_gk = head_back(
        (grad_query.reshape(query_pre.shape), grad_key.reshape(key_pre.shape))
    )
    grad_qkv = jnp.concatenate(
        [
            grad_qpre.astype(jnp.bfloat16).reshape(blocks * rows, heads * size),
            grad_kpre.astype(jnp.bfloat16).reshape(blocks * rows, size),
            grad_value.astype(jnp.bfloat16).reshape(blocks * rows, size),
        ],
        axis=1,
    )
    grad_wqkv = lax.dot_general(
        normed, grad_qkv, (((0,), (0,)), ((), ())), preferred_element_type=jnp.float32
    ).astype(jnp.bfloat16)
    return grad_qkv, grad_wqkv, grad_wout, grad_gq, grad_gk


def send_back(picks, pieces, waits=()):
    pick = jnp.concatenate(picks, axis=1)
    if waits:
        pick = after(pick, *waits)
    return (
        jnp.einsum(
            SPREAD,
            pick,
            jnp.concatenate(pieces, axis=1),
            preferred_element_type=jnp.float32,
        )
        .astype(jnp.bfloat16)
        .reshape(-1, pieces[0].shape[2])
    )


def expert_forward(gathered, picks, row_gates, weights):
    blocks = picks[0].shape[0]
    width = gathered.shape[1]
    grouped = gathered.reshape(blocks, -1, width)
    memo = []
    pieces = []
    for pick, row_gate, (w_up_gate, w_down) in zip(picks, row_gates, weights):
        ff = w_down.shape[0]
        rows = jnp.einsum(PICK, pick, grouped, preferred_element_type=jnp.float32)
        rows = rows.astype(jnp.bfloat16).reshape(-1, width)
        pre = jnp.dot(rows, w_up_gate, preferred_element_type=jnp.float32)
        gate_pre, up_pre = pre[:, :ff], pre[:, ff:]
        hidden = (jax.nn.silu(gate_pre) * up_pre).astype(jnp.bfloat16)
        produced = jnp.dot(hidden, w_down, preferred_element_type=jnp.float32)
        produced = (produced * row_gate).astype(jnp.bfloat16)
        pieces.append(produced.reshape(blocks, -1, width))
        memo.append((rows, pre, hidden))
    return send_back(picks, pieces), memo


def expert_backward(gathered, picks, row_gates, weights, memo, experts, waits):
    blocks = picks[0].shape[0]
    width = gathered.shape[1]
    grouped = gathered.reshape(blocks, -1, width)
    pieces = []
    grads = []
    for pick, row_gate, (w_up_gate, w_down), kept, expert in zip(
        picks, row_gates, weights, memo, experts
    ):
        rows, pre, hidden = kept
        ff = hidden.shape[1]
        gate_pre, up_pre = pre[:, :ff].astype(jnp.float32), pre[:, ff:].astype(jnp.float32)
        grad_rows = jnp.einsum(PICK, pick, grouped, preferred_element_type=jnp.float32)
        grad_rows = grad_rows.astype(jnp.bfloat16).reshape(-1, width)
        through = lax.dot_general(
            grad_rows, w_down, (((1,), (1,)), ((), ())), preferred_element_type=jnp.float32
        )
        hidden_f = hidden.astype(jnp.float32)
        gate_grad = jnp.sum(hidden_f * through, axis=1, keepdims=True)
        high = gate_grad.astype(jnp.bfloat16)
        low = (gate_grad - high.astype(jnp.float32)).astype(jnp.bfloat16)
        column = jnp.arange(GATE_COLUMNS, dtype=jnp.int32)[None, :]
        gate_part = jnp.where(
            column == expert, high, jnp.where(column == expert + EXPERTS, low, 0)
        )
        grad_hidden = through * row_gate
        sigmoid_gate = jax.nn.sigmoid(gate_pre)
        grad_gate_pre = (
            grad_hidden * up_pre * sigmoid_gate * (1.0 + gate_pre * (1.0 - sigmoid_gate))
        ).astype(jnp.bfloat16)
        grad_up_pre = (grad_hidden * gate_pre * sigmoid_gate).astype(jnp.bfloat16)
        grad_down = lax.dot_general(
            (hidden_f * row_gate).astype(jnp.bfloat16),
            grad_rows,
            (((0,), (0,)), ((), ())),
            preferred_element_type=jnp.float32,
        ).astype(jnp.bfloat16)
        grad_gate, grad_up = [
            lax.dot_general(
                rows, part, (((0,), (0,)), ((), ())), preferred_element_type=jnp.float32
            ).astype(jnp.bfloat16)
            for part in (grad_gate_pre, grad_up_pre)
        ]
        grad_in = lax.dot_general(
            jnp.concatenate([grad_gate_pre, grad_up_pre], axis=1),
            w_up_gate,
            (((1,), (1,)), ((), ())),
            preferred_element_type=jnp.float32,
        ).astype(jnp.bfloat16)
        piece = jnp.concatenate([grad_in, gate_part], axis=1)
        pieces.append(piece.reshape(blocks, -1, width + GATE_COLUMNS))
        grads.append((grad_gate, grad_up, grad_down))
    return send_back(picks, pieces, waits), grads


def chip_shards(
    tokens,
    cotangent,
    lengths,
    routes,
    gains,
    w_query,
    key_weight,
    value_weight,
    w_out,
    w_router,
    w_gate,
    w_up,
    w_down,
):
    rows = tokens.shape[0]
    width = lax.axis_size(FSDP)
    place = lax.axis_index(FSDP)
    line = lax.axis_index(LINE)
    core = lax.axis_index(CORE)
    devices = width * lax.axis_size(LINE) * 2
    chips = devices // 2
    chip = place * lax.axis_size(LINE) + line
    depth = lax.axis_size(LINE)
    group = QUERY_HEADS // KEY_VALUE_HEADS
    ff = w_gate.shape[3]
    short = w_query.shape[1]
    experts_here = w_gate.shape[1]
    gain_columns = -(-gains.size // short)
    side = jnp.concatenate(
        [w_router[number] for number in range(DECODER_LAYERS)]
        + [jnp.pad(gains.reshape(-1), (0, gain_columns * short - gains.size)).reshape(short, -1)],
        axis=1,
    )
    side = by_core(core, side, swap(side), 0)
    router_columns = DECODER_LAYERS * EXPERTS
    cut = side.shape[1]
    small = jnp.concatenate(
        [side]
        + [routes[number].astype(jnp.bfloat16) for number in range(DECODER_LAYERS)]
        + [jnp.broadcast_to(lengths.astype(jnp.bfloat16), (rows, lengths.shape[1]))],
        axis=1,
    )
    small = jnp.pad(small, ((0, 0), (0, -small.shape[1] % 128)))


    qkv_columns = (group + 2) * HEAD_SIZE

    def columns_of(number):
        return jnp.concatenate(
            [
                w_query[number]
                .reshape(short, width, depth, 2, HEAD_SIZE)
                .transpose(1, 0, 3, 2, 4)
                .reshape(width, short, group * HEAD_SIZE),
                key_weight[number].reshape(short, width, HEAD_SIZE).transpose(1, 0, 2),
                value_weight[number].reshape(short, width, HEAD_SIZE).transpose(1, 0, 2),
            ],
            axis=2,
        )

    columns = jnp.stack([columns_of(number) for number in range(DECODER_LAYERS)], axis=1)
    by_source = jnp.zeros_like(columns)
    for origin, piece in swap_pieces(
        lambda to: lax.dynamic_index_in_dim(columns, to, 0, keepdims=False), place, width
    ):
        by_source = lax.dynamic_update_index_in_dim(by_source, piece, origin, 0)

    def rows_by_source(number):
        return by_source[:, number].reshape(width * short, qkv_columns)

    def weights_of(number, work=None, beside=None):
        return layer_weights(
            number, w_gate, w_up, w_down, rows_by_source(number), w_out, 10 + number, work, beside
        )

    weights, qkv_whole, out_whole, made = weights_of(0, beside=small)
    small = made[0].reshape(chips * rows, -1)
    routers = [
        small[:, number * EXPERTS : (number + 1) * EXPERTS] for number in range(DECODER_LAYERS)
    ]
    all_gains = (
        small[:, router_columns:cut]
        .reshape(devices, -1)[:, : gains.size]
        .reshape(devices, DECODER_LAYERS, -1)
        .transpose(1, 0, 2)
        .reshape(DECODER_LAYERS, -1)
        .astype(jnp.float32)
    )
    all_routes = (
        small[:, cut : cut + DECODER_LAYERS * TOP]
        .reshape(chips, rows, DECODER_LAYERS, TOP)
        .transpose(0, 2, 1, 3)
    )
    cut = cut + DECODER_LAYERS * TOP
    all_lengths = (
        small.reshape(width, depth, rows, -1)[:, :, 0, cut : cut + lengths.shape[1]]
        .astype(jnp.int32)
    )
    all_lengths = lax.dynamic_index_in_dim(all_lengths, line, 1, keepdims=False)
    chosen = jnp.any(
        all_routes[..., None] == jnp.arange(EXPERTS, dtype=jnp.bfloat16), axis=3
    )
    chosen_f = chosen.astype(jnp.bfloat16)
    before = jnp.tril(jnp.ones((rows, rows), jnp.bfloat16), -1)
    ranks = jnp.einsum(
        "ts,clse->clte", before, chosen_f, preferred_element_type=jnp.float32
    )
    first = (line * 2 + core) * experts_here + place
    second = (line * 2 + (1 - core)) * experts_here + place
    slots = jnp.arange(CAP, dtype=jnp.float32)

    def pick_of(number, expert):
        named = lax.dynamic_index_in_dim(chosen[:, number], expert, 2, keepdims=False)
        rank = lax.dynamic_index_in_dim(ranks[:, number], expert, 2, keepdims=False)
        return (
            (rank[:, None, :] == slots[None, :, None]) & named[:, None, :]
        ).astype(jnp.bfloat16)

    picks = [(pick_of(number, first), pick_of(number, second)) for number in range(DECODER_LAYERS)]

    cosine, sine, allowed = jax.vmap(lambda own: geometry(own[None], rows))(all_lengths)
    angles = (
        cosine.reshape(width * rows, 1, -1),
        sine.reshape(width * rows, 1, -1),
        allowed,
    )
    g_attn, g_ffn, g_query, g_key = zip(*[split_gains(all_gains[i]) for i in range(DECODER_LAYERS)])

    share = MODEL_WIDTH // width

    def to_experts(part):
        return lax.all_to_all(part, FSDP, split_axis=0, concat_axis=0, tiled=True)

    state = tokens.astype(jnp.float32)
    kept = []
    for number in range(DECODER_LAYERS):
        normed = norm_rows(state, g_attn[number]).astype(jnp.bfloat16)
        normed = gather_chips(by_owner(normed, width), 6, PLANE)
        dense = (qkv_whole, out_whole, normed, g_query[number], g_key[number])
        middle, memo = attention_forward(state, dense, angles)
        mixer_in = norm_rows(middle, g_ffn[number]).astype(jnp.bfloat16)
        gathered = gather_chips(mixer_in, 2)
        if number == 0:
            cotangent_all = offload_gather(after(cotangent, gathered))
        logits = jnp.dot(gathered, routers[number], preferred_element_type=jnp.float32)
        named = chosen[:, number].reshape(chips * rows, EXPERTS)
        gates = softmax_last(jnp.where(named, logits, -1e30))
        row_gates = []
        for pick, expert in zip(picks[number], (first, second)):
            gate = lax.dynamic_index_in_dim(gates, expert, 1, keepdims=False)
            row_gates.append(
                jnp.sum(
                    pick.astype(jnp.float32) * gate.reshape(chips, 1, rows), axis=2
                ).reshape(-1, 1)
            )
        layer_experts = weights
        if number + 1 < DECODER_LAYERS:
            weights, qkv_whole, out_whole, made = weights_of(
                number + 1, (gathered, picks[number], row_gates, weights)
            )
            expert_memo = [(made[i], made[2 + i], made[4 + i]) for i in range(2)]
            produced = made[6].reshape(gathered.shape)
        else:
            produced, expert_memo = expert_forward(gathered, picks[number], row_gates, weights)
        new_state = middle + scatter_chips(produced, 3).astype(jnp.float32)
        own_gates = lax.dynamic_slice_in_dim(gates, chip * rows, rows, 0)
        kept.append(
            (state, middle, mixer_in, own_gates, row_gates, dense, layer_experts, memo, expert_memo)
        )
        state = new_state
    result = state.astype(jnp.bfloat16)

    def half_sum(operand):
        half = operand.shape[0] // 2
        mine = lax.dynamic_slice_in_dim(operand, core * half, half, 0)
        return mine, swap(lax.dynamic_slice_in_dim(operand, (1 - core) * half, half, 0))

    def line_sum(mine, other):
        return lax.psum_scatter(mine + other, LINE, scatter_dimension=0, tiled=True)

    def out_sum(mine, other):
        return line_sum(mine, other).astype(jnp.float32)

    def qkv_sum(mine, other):
        summed = line_sum(mine, other).reshape(width, short, qkv_columns)
        return swap_pieces(
            lambda to: lax.dynamic_index_in_dim(summed, to, 0, keepdims=False), place, width
        )

    grad_state = cotangent.astype(jnp.float32)
    grad_low = cotangent
    grad_gathered = cotangent_all
    small_grads = []
    d_out = []
    back_qkv = []
    d_experts = []
    earlier = []
    held = None
    for number in reversed(range(DECODER_LAYERS)):
        state, middle, mixer_in, own_gates, row_gates, dense, weights, memo, expert_memo = kept[
            number
        ]
        back, expert_grads = expert_backward(
            grad_gathered, picks[number], row_gates, weights, expert_memo, (first, second), earlier
        )
        d_expert = [mine + swap(other) for mine, other in zip(*expert_grads)]
        d_expert[2] = d_expert[2].reshape(ff, width, share).transpose(1, 0, 2)
        back_low = scatter_chips(back, 5)
        if held is not None:
            out_halves, qkv_halves = held
            d_out.insert(0, out_sum(after(out_halves[0], grad_gathered), out_halves[1]))
            back_qkv.insert(0, qkv_sum(after(qkv_halves[0], back_low), qkv_halves[1]))
        back = back_low.astype(jnp.float32)
        grad_gates = (
            back[:, MODEL_WIDTH : MODEL_WIDTH + EXPERTS]
            + back[:, MODEL_WIDTH + EXPERTS : MODEL_WIDTH + 2 * EXPERTS]
        )
        grad_logits = (
            own_gates
            * (grad_gates - jnp.sum(own_gates * grad_gates, axis=1, keepdims=True))
        ).astype(jnp.bfloat16)
        grad_router = lax.dot_general(
            mixer_in, grad_logits, (((0,), (0,)), ((), ())), preferred_element_type=jnp.float32
        )
        grad_mixer = back[:, :MODEL_WIDTH] + lax.dot_general(
            grad_logits,
            routers[number],
            (((1,), (1,)), ((), ())),
            preferred_element_type=jnp.float32,
        )
        unused_mid, norm_back = jax.vjp(norm_rows, middle, g_ffn[number])
        grad_mid_part, grad_g_ffn = norm_back(grad_mixer)
        grad_middle = grad_state + grad_mid_part
        low = gather_chips(
            after(grad_middle.astype(jnp.bfloat16), *d_expert), 6, PLANE
        )
        if number == 0:
            d_expert = [after(part, low) for part in d_expert]
        earlier = [to_experts(part.reshape(width, -1, part.shape[-1])) for part in d_expert]
        d_experts.insert(0, earlier)
        grad_qkv, grad_wqkv, grad_wout, grad_gq, grad_gk = attention_backward(
            low, memo, dense, angles
        )
        held = half_sum(grad_wout), half_sum(grad_wqkv)
        other = held[1][1]
        if number == 0:
            d_out.insert(0, out_sum(*held[0]))
            back_qkv.insert(0, qkv_sum(*held[1]))
        grad_normed = lax.dot_general(
            after(grad_qkv, other),
            dense[0],
            (((1,), (1,)), ((), ())),
            preferred_element_type=jnp.float32,
        ).astype(jnp.bfloat16)
        grad_normed = scatter_chips(grad_normed, 7, PLANE)
        grad_normed = by_place(grad_normed.astype(jnp.float32), width)
        unused_state, norm_front = jax.vjp(norm_rows, state, g_attn[number])
        grad_in_part, grad_g_attn = norm_front(grad_normed)
        grad_state = grad_middle + grad_in_part
        grad_low = grad_state.astype(jnp.bfloat16)
        if number > 0:
            grad_gathered = gather_chips(grad_low, 2)
        gain_grads = jnp.concatenate([grad_g_attn, grad_g_ffn, grad_gq, grad_gk])
        small_grads.insert(0, (grad_router, gain_grads.reshape(devices, -1)))
    d_out = jnp.stack(d_out)
    d_gate, d_up, d_down = [
        jnp.stack([entry[i].astype(jnp.float32) for entry in d_experts]) for i in range(3)
    ]
    own_gains = jnp.concatenate([gain_grad for _, gain_grad in small_grads], axis=1)
    own_gains = jnp.pad(own_gains, ((0, 0), (0, gain_columns * short - gains.size)))
    side = jnp.concatenate(
        [router_grad for router_grad, _ in small_grads] + [own_gains.reshape(MODEL_WIDTH, -1)],
        axis=1,
    ).astype(jnp.bfloat16)
    side = jnp.pad(side, ((0, 0), (0, -side.shape[1] % 128)))
    side = scatter_chips(side, 4).astype(jnp.float32)
    small = lax.dynamic_slice_in_dim(side, core * short, short, 0) + swap(
        lax.dynamic_slice_in_dim(side, (1 - core) * short, short, 0)
    )
    d_router = jnp.stack(
        [small[:, number * EXPERTS : (number + 1) * EXPERTS] for number in range(DECODER_LAYERS)]
    )
    d_gains = small[:, router_columns : router_columns + gain_columns].reshape(-1)[: gains.size]
    d_gains = d_gains.reshape(gains.shape)
    d_qkv = jnp.zeros((DECODER_LAYERS, width, short, qkv_columns), jnp.bfloat16)
    for number in reversed(range(DECODER_LAYERS)):
        for origin, piece in back_qkv[number]:
            if number > 0:
                piece = after(piece, side)
            d_qkv = lax.dynamic_update_slice(d_qkv, piece[None, None], (number, origin, 0, 0))
    d_qkv = d_qkv.astype(jnp.float32)
    cut = group * HEAD_SIZE
    d_query = (
        d_qkv[..., :cut]
        .reshape(DECODER_LAYERS, width, short, 2, depth, HEAD_SIZE)
        .transpose(0, 2, 1, 4, 3, 5)
        .reshape(w_query.shape)
    )
    d_key = d_qkv[..., cut : cut + HEAD_SIZE].transpose(0, 2, 1, 3).reshape(key_weight.shape)
    d_value = d_qkv[..., cut + HEAD_SIZE :].transpose(0, 2, 1, 3).reshape(value_weight.shape)
    return (
        result,
        grad_low,
        d_gains,
        d_query,
        d_key,
        d_value,
        d_out,
        d_router,
        d_gate,
        d_up,
        d_down,
    )


def by_chip(mesh):
    grid = Mesh(
        mesh.devices.reshape(mesh.shape[FSDP], mesh.shape["expert"] // 2, 2),
        EVERY,
    )
    experts = (LINE, CORE)
    return jax.shard_map(
        chip_shards,
        mesh=grid,
        in_specs=(
            P(EVERY, None),
            P(EVERY, None),
            P(EVERY, None),
            P(None, EVERY, None),
            P(None, EVERY),
            P(None, EVERY, None),
            P(None, EVERY, None),
            P(None, EVERY, None),
            P(None, EVERY, None),
            P(None, EVERY, None),
            P(None, experts, FSDP, None),
            P(None, experts, FSDP, None),
            P(None, experts, None, FSDP),
        ),
        out_specs=(
            P(EVERY, None),
            P(EVERY, None),
            P(None, EVERY),
            P(None, EVERY, None),
            P(None, EVERY, None),
            P(None, EVERY, None),
            P(None, EVERY, None),
            P(None, EVERY, None),
            P(None, experts, FSDP, None),
            P(None, experts, FSDP, None),
            P(None, experts, None, FSDP),
        ),
        check_vma=False,
    )


def solution(mesh):
    width = mesh.shape[FSDP]
    peers = mesh.shape["expert"]
    if width == KEY_VALUE_HEADS == PAIR and peers * width == EXPERTS == QUERY_HEADS:
        return by_chip(mesh)
    return general(mesh)
```
